32 devices in a mesh: dp: 8 (over y, x, core), seq: 4 (over z).
Axes of the slice: x: 2, y: 2, z: 4, core: 2. Of those that a mesh axis runs over, the one named last changes fastest.
Arguments:
- tokens: bfloat16 [16, 1024, 1280], P('dp', 'seq'), may hold values from -6 to 6
- protein_lengths: int32 [16, 16], P('dp'), may hold values from 0 to 1024, as said below
- norm1_gain: bfloat16 [2, 1280], P(None, 'dp'), may hold values from 0.099609375 to 1.8984375
- norm1_bias: bfloat16 [2, 1280], P(None, 'dp'), may hold values from -3 to 3
- w_in: bfloat16 [2, 1280, 640], P(None, 'dp', 'seq'), may hold values from -0.15625 to 0.15625
- in_bias: bfloat16 [2, 640], P(None, 'dp'), may hold values from -3 to 3
- norm2_gain: bfloat16 [2, 640], P(None, 'dp'), may hold values from 0.099609375 to 1.8984375
- norm2_bias: bfloat16 [2, 640], P(None, 'dp'), may hold values from -3 to 3
- w_conv: bfloat16 [2, 5, 640, 640], P(None, None, 'dp', 'seq'), may hold values from -0.109375 to 0.109375
- conv_bias: bfloat16 [2, 640], P(None, 'dp'), may hold values from -3 to 3
- norm3_gain: bfloat16 [2, 640], P(None, 'dp'), may hold values from 0.099609375 to 1.8984375
- norm3_bias: bfloat16 [2, 640], P(None, 'dp'), may hold values from -3 to 3
- w_out: bfloat16 [2, 640, 1280], P(None, 'dp', 'seq'), may hold values from -0.3125 to 0.3125
- out_bias: bfloat16 [2, 1280], P(None, 'dp'), may hold values from -2 to 2
- cotangent: bfloat16 [16, 1024, 1280], P('dp', 'seq'), may hold values from -6 to 6
Outputs:
- output: bfloat16 [16, 1024, 1280], P('dp', 'seq')
- input_grad: float32 [16, 1024, 1280], P('dp', 'seq')
- grad_norm1_gain: float32 [2, 1280], P(None, 'dp')
- grad_norm1_bias: float32 [2, 1280], P(None, 'dp')
- grad_w_in: float32 [2, 1280, 640], P(None, 'dp', 'seq')
- grad_in_bias: float32 [2, 640], P(None, 'dp')
- grad_norm2_gain: float32 [2, 640], P(None, 'dp')
- grad_norm2_bias: float32 [2, 640], P(None, 'dp')
- grad_w_conv: float32 [2, 5, 640, 640], P(None, None, 'dp', 'seq')
- grad_conv_bias: float32 [2, 640], P(None, 'dp')
- grad_norm3_gain: float32 [2, 640], P(None, 'dp')
- grad_norm3_bias: float32 [2, 640], P(None, 'dp')
- grad_w_out: float32 [2, 640, 1280], P(None, 'dp', 'seq')
- grad_out_bias: float32 [2, 1280], P(None, 'dp')
The draws below stay inside these ranges and needn't reach their ends.
Inputs may be any that keep to these rules, and one draw needn't show every extreme that they name: `protein_lengths`: in each row the nonzero lengths come first, each is 30 or more, and together they are at most 1024; in each aligned block of 2 rows, one row holds a protein that begins before position 256 and ends at the row's end.
All inputs are finite; a program needn't handle non-finite values.
Results may differ from the reference program's by a relative error of at most 0.014.
Values may be sent and summed in bfloat16 or wider, within the bound.
No kernel may reach another device: no remote copies, remote signals or barrier semaphores. Data moves between devices by JAX's collectives and lax.ppermute only.
A program may use at most 192 MiB of HBM per device.

```python
import math
import jax
import jax.numpy as jnp
from jax import lax

D = 1280
HID = 640
KER = 5
FIRST_DILATION = 64
SECOND_DILATION = 128
P_DEV = 256
ROWS_DEV = 2
DOCS = 16
MIN_DOC = 30
ROW_LEN = 1024
ROWS = 16


def draw_protein_lengths(key, part):
    key = jax.random.fold_in(key, 7)
    key_list = jax.random.split(key, 5)
    length_span = ROW_LEN - MIN_DOC + 1
    draw_one = jax.random.randint(key_list[0], (ROWS, DOCS), 0, length_span)
    draw_two = jax.random.randint(key_list[1], (ROWS, DOCS), 0, length_span)
    draw_three = jax.random.randint(key_list[2], (ROWS, DOCS), 0, length_span)
    raw_lengths = MIN_DOC + jnp.minimum(jnp.minimum(draw_one, draw_two), draw_three)
    running_ends = jnp.cumsum(raw_lengths, axis=1)
    packed = jnp.where(running_ends <= ROW_LEN, raw_lengths, 0)
    chosen = jax.random.randint(key_list[3], (ROWS // ROWS_DEV,), 0, ROWS_DEV)
    row_ids = jnp.arange(ROWS)
    long_rows = row_ids % ROWS_DEV == chosen[row_ids // ROWS_DEV]
    lead_raw = jax.random.randint(key_list[4], (ROWS,), 0, P_DEV)
    lead = jnp.where(lead_raw < MIN_DOC, 0, lead_raw).astype(jnp.int32)
    slot_ids = jnp.arange(DOCS)[None, :]
    with_lead = jnp.where(slot_ids == 0, lead[:, None], jnp.where(slot_ids == 1, ROW_LEN - lead[:, None], 0))
    alone = jnp.where(slot_ids == 0, ROW_LEN, 0)
    spanning = jnp.where((lead > 0)[:, None], with_lead, alone)
    return jnp.where(long_rows[:, None], spanning, packed).astype(jnp.int32)


def block_scale(stream_key, dims, cuts, least, largest):
    def one(axis_at, parts):
        steps = jax.random.uniform(jax.random.fold_in(jax.random.fold_in(stream_key, 6), axis_at), (parts,), jnp.float32, least / len(cuts), largest / len(cuts))
        return jnp.repeat(jnp.exp(steps), dims[axis_at] // parts).reshape((-1,) + (1,) * (len(dims) - axis_at - 1))

    level = one(*cuts[0])
    for cut in cuts[1:]:
        level = level * one(*cut)
    return level


def noise(rng, extent, scale, most, cuts=(), kind=jnp.bfloat16):
    gain = block_scale(rng, extent, cuts, -0.22, 0.18) if cuts else 1.0
    values = jax.random.normal(rng, extent, jnp.float32) * scale * gain
    return jnp.minimum(jnp.maximum(values, -most), most).astype(kind)


def setup_inputs(seed: int = 0) -> dict:
    keys = jax.random.split(jax.random.key(seed), 16)
    tokens = noise(keys[0], (ROWS, ROW_LEN, D), 1.0, 6.0, ((0, 8), (1, 4)))
    protein_lengths = draw_protein_lengths(jax.random.fold_in(keys[15], 71), 0)
    norm1_gain = jnp.clip(1.0 + 0.18 * jax.random.normal(keys[2], (2, D), jnp.float32), 0.099609375, 1.8984375).astype(jnp.bfloat16)
    norm1_bias = noise(keys[3], (2, D), 0.5, 3.0, ((1, 8),))
    w_in = noise(keys[4], (2, D, HID), D ** -0.5, 0.15625, ((1, 8), (2, 4)))
    in_bias = noise(keys[5], (2, HID), 0.5, 3.0, ((1, 8),))
    norm2_gain = jnp.clip(1.0 + 0.18 * jax.random.normal(keys[6], (2, HID), jnp.float32), 0.099609375, 1.8984375).astype(jnp.bfloat16)
    norm2_bias = noise(keys[7], (2, HID), 0.5, 3.0, ((1, 8),))
    w_conv = noise(keys[8], (2, KER, HID, HID), (KER * HID) ** -0.5, 0.109375, ((2, 8), (3, 4)))
    conv_bias = noise(keys[9], (2, HID), 0.5, 3.0, ((1, 8),))
    norm3_gain = jnp.clip(1.0 + 0.18 * jax.random.normal(keys[10], (2, HID), jnp.float32), 0.099609375, 1.8984375).astype(jnp.bfloat16)
    norm3_bias = noise(keys[11], (2, HID), 0.5, 3.0, ((1, 8),))
    w_out = noise(keys[12], (2, HID, D), (HID // 2) ** -0.5, 0.3125, ((1, 8), (2, 4)))
    out_bias = noise(keys[13], (2, D), 0.3, 2.0, ((1, 8),))
    cotangent = noise(keys[14], (ROWS, ROW_LEN, D), 1.0, 6.0, ((0, 8), (1, 4)))
    return dict(tokens=tokens, protein_lengths=protein_lengths, norm1_gain=norm1_gain, norm1_bias=norm1_bias, w_in=w_in, in_bias=in_bias, norm2_gain=norm2_gain, norm2_bias=norm2_bias, w_conv=w_conv, conv_bias=conv_bias, norm3_gain=norm3_gain, norm3_bias=norm3_bias, w_out=w_out, out_bias=out_bias, cotangent=cotangent)


epsilon = 1e-05

@jax.custom_vjp
def low(v):
    return lax.optimization_barrier(v.astype(jnp.bfloat16)).astype(jnp.float32)

@jax.custom_vjp
def low_back(v):
    return v

def low_keep(v):
    return (low(v), None)

def low_pass(kept, grad):
    return (grad,)

def back_keep(v):
    return (v, None)

def back_low(kept, grad):
    return (low(grad),)
low.defvjp(low_keep, low_pass)
low_back.defvjp(back_keep, back_low)

def norm_gelu(values, gain_vector, bias_vector):
    row_mean = lax.optimization_barrier(jnp.mean(values, -1, keepdims=True))
    centred = values - row_mean
    spread = lax.optimization_barrier(jnp.mean(centred * centred, -1, keepdims=True))
    return jax.nn.gelu(centred * lax.rsqrt(spread + epsilon) * gain_vector + bias_vector, approximate=True)

def kernel_tap_flags(lengths, token_positions, dilation_step):
    doc_ends = jnp.cumsum(lengths, axis=1).astype(jnp.int32)
    row_total = doc_ends[:, -1:]
    where_pos = token_positions[None, :, None]
    finished = doc_ends[:, None, :] <= where_pos
    doc_start = lax.optimization_barrier(jnp.sum(jnp.where(finished, lengths[:, None, :], 0), axis=2)).astype(jnp.int32)
    doc_stop = lax.optimization_barrier(jnp.min(jnp.where(finished, row_total[:, :, None] + 1, doc_ends[:, None, :]), axis=2)).astype(jnp.int32)
    is_live = token_positions[None, :] < row_total
    flag_list = []
    for tap_index in range(KER):
        target = token_positions[None, :] + (tap_index - KER // 2) * dilation_step
        flag_list.append(is_live & (target >= doc_start) & (target < doc_stop))
    return flag_list

def dilated_conv(activations, flag_list, kernel, bias_vector, dilation_step):
    halo_width = KER // 2 * dilation_step
    padded = jnp.pad(activations, ((0, 0), (halo_width, halo_width), (0, 0)))
    length = activations.shape[1]
    pieces = [jnp.where(flag_list[tap_index][:, :, None], padded[:, tap_index * dilation_step:tap_index * dilation_step + length], 0.0) for tap_index in range(KER)]
    stacked = jnp.stack(pieces, axis=2)
    return jnp.einsum('glkh,khj->glj', stacked, kernel, precision=lax.Precision.HIGHEST) + bias_vector

def project(activations, weight):
    return jnp.einsum('glh,hj->glj', activations, weight, precision=lax.Precision.HIGHEST)

def residual_block(stream, flag_list, params, dilation_step):
    gain_one, bias_one, w_first, bias_first, gain_two, bias_two, w_middle, bias_middle, gain_three, bias_three, w_last, bias_last = params
    act_one = low(norm_gelu(stream, gain_one, bias_one))
    projected = low_back(project(act_one, w_first) + bias_first)
    act_two = low(norm_gelu(projected, gain_two, bias_two))
    conv_out = low_back(dilated_conv(act_two, flag_list, w_middle, bias_middle, dilation_step))
    act_three = low(norm_gelu(conv_out, gain_three, bias_three))
    branch = low_back(project(act_three, w_last) + bias_last)
    return stream + branch

def reference(tokens, protein_lengths, norm1_gain, norm1_bias, w_in, in_bias, norm2_gain, norm2_bias, w_conv, conv_bias, norm3_gain, norm3_bias, w_out, out_bias, cotangent):
    params = tuple((weight.astype(jnp.float32) for weight in (norm1_gain, norm1_bias, w_in, in_bias, norm2_gain, norm2_bias, w_conv, conv_bias, norm3_gain, norm3_bias, w_out, out_bias)))
    group_rows = math.gcd(ROWS, 4)
    group_count = ROWS // group_rows
    inputs = tokens.astype(jnp.float32).reshape(group_count, group_rows, ROW_LEN, D)
    lengths = protein_lengths.reshape(group_count, group_rows, DOCS)
    upstream = cotangent.astype(jnp.float32).reshape(group_count, group_rows, ROW_LEN, D)
    token_positions = jnp.arange(ROW_LEN, dtype=jnp.int32)

    def one_group(running, pieces):
        stream, packed_group_lengths, group_upstream = pieces
        tap_flag_groups = (kernel_tap_flags(packed_group_lengths, token_positions, FIRST_DILATION), kernel_tap_flags(packed_group_lengths, token_positions, SECOND_DILATION))

        def forward(values, weights):
            for block_number, dilation_step in enumerate((FIRST_DILATION, SECOND_DILATION)):
                values = residual_block(values, tap_flag_groups[block_number], tuple((weight[block_number] for weight in weights)), dilation_step)
            return values
        result, pullback = jax.vjp(forward, stream, params)
        grad_stream, grad_weights = pullback(group_upstream)
        running = tuple((old_sum + grad_piece for old_sum, grad_piece in zip(running, grad_weights)))
        return (running, (result.astype(jnp.bfloat16), grad_stream))
    zero_grads = tuple((jnp.zeros_like(weight) for weight in params))
    summed, (outputs, grads_in) = lax.scan(one_group, zero_grads, (inputs, lengths, upstream))
    return (outputs.reshape(ROWS, ROW_LEN, D), grads_in.reshape(ROWS, ROW_LEN, D), summed[0], summed[1], summed[2], summed[3], summed[4], summed[5], summed[6], summed[7], summed[8], summed[9], summed[10], summed[11])
```

```python
import jax
import jax.numpy as jnp
from jax import lax
from jax.sharding import PartitionSpec as P

KER = 5
FIRST_DILATION = 64
SECOND_DILATION = 128


epsilon = 1e-05


def extended(block, sides, width):
    for axis, dim in sides:
        count = lax.axis_size(axis)
        forward = [(i, i + 1) for i in range(count - 1)]
        backward = [(target, source) for source, target in forward]
        low = lax.ppermute(
            lax.slice_in_dim(block, block.shape[dim] - width, None, axis=dim), axis, forward
        )
        high = lax.ppermute(lax.slice_in_dim(block, 0, width, axis=dim), axis, backward)
        block = jnp.concatenate([low, block, high], axis=dim)
    return block


def norm_gelu(values, gain_vector, bias_vector):
    row_mean = jnp.mean(values, -1, keepdims=True)
    centred = values - row_mean
    spread = jnp.mean(centred * centred, -1, keepdims=True)
    return jax.nn.gelu(
        centred * lax.rsqrt(spread + epsilon) * gain_vector + bias_vector, approximate=True
    )


def kernel_tap_flags(lengths, token_positions, dilation_step):
    doc_ends = jnp.cumsum(lengths, axis=1)
    row_total = doc_ends[:, -1:]
    where_pos = token_positions[None, :, None]
    finished = doc_ends[:, None, :] <= where_pos
    doc_start = jnp.sum(jnp.where(finished, lengths[:, None, :], 0), axis=2)
    doc_stop = jnp.min(jnp.where(finished, row_total[:, :, None] + 1, doc_ends[:, None, :]), axis=2)
    is_live = token_positions[None, :] < row_total
    flag_list = []
    for tap_index in range(KER):
        target = token_positions[None, :] + (tap_index - KER // 2) * dilation_step
        flag_list.append(is_live & (target >= doc_start) & (target < doc_stop))
    return flag_list


def contract_rows(left_rows, right_rows):
    return lax.dot_general(
        left_rows, right_rows, (((0,), (0,)), ((), ())), preferred_element_type=jnp.float32
    )


def times_transpose(left_rows, weight):
    return lax.dot_general(
        left_rows, weight, (((1,), (1,)), ((), ())), preferred_element_type=jnp.float32
    )


def forward_taps(activations, flag_list, dilation_step):
    padded = extended(activations, (("seq", 1),), KER // 2 * dilation_step)
    seq_len = activations.shape[1]
    zero_value = jnp.zeros((), activations.dtype)
    pieces = [
        jnp.where(
            flag_list[tap_index][:, :, None],
            padded[:, tap_index * dilation_step : tap_index * dilation_step + seq_len],
            zero_value,
        )
        for tap_index in range(KER)
    ]
    return jnp.stack(pieces, axis=2).reshape(
        activations.shape[0] * seq_len, KER * activations.shape[2]
    )


def backward_taps(gradient, flag_list, dilation_step):
    padded = extended(gradient, (("seq", 1),), KER // 2 * dilation_step)
    seq_len = gradient.shape[1]
    zero_value = jnp.zeros((), gradient.dtype)
    pieces = []
    for tap_index in range(KER):
        mirror = KER - 1 - tap_index
        pieces.append(
            jnp.where(
                flag_list[mirror][:, :, None],
                padded[:, mirror * dilation_step : mirror * dilation_step + seq_len],
                zero_value,
            )
        )
    return jnp.stack(pieces, axis=2).reshape(gradient.shape[0] * seq_len, KER * gradient.shape[2])


def shifted(block, step):
    count = lax.axis_size("seq")
    return lax.ppermute(block, "seq", [(i, (i + step) % count) for i in range(count)])


def weight_pack(block_number, device_shards):
    w_in, w_conv, w_out = (device_shards[i][block_number] for i in (2, 6, 10))
    width = w_in.shape[1]
    folds = w_out.shape[1] // width
    pieces = [w_in, w_conv.reshape(-1, width)]
    pieces += [w_out[:, i * width : (i + 1) * width] for i in range(folds)]
    return jnp.concatenate(pieces, axis=0)


def vector_pack(block_number, device_shards, width):
    order = (0, 1, 11, 3, 4, 5, 7, 8, 9)
    flat = jnp.concatenate([device_shards[i][block_number] for i in order])
    rows = -(-flat.shape[0] // (16 * width)) * 16
    return jnp.pad(flat, (0, rows * width - flat.shape[0])).reshape(rows, width)


def seq_gathered(packed):
    count = lax.axis_size("seq")
    me = lax.axis_index("seq")
    held = [packed] + [shifted(packed, step) for step in range(1, count)]
    ring = jnp.stack(held[::-1] + held[::-1])
    return lax.dynamic_slice_in_dim(ring, (count - 1 - me) % count, count, axis=0)


def folded_columns(out_parts):
    count, folds, depth, width = out_parts.shape
    per_fold = count // folds
    return (
        out_parts.reshape(folds, per_fold, folds, depth, width)
        .transpose(0, 3, 1, 2, 4)
        .reshape(folds * depth, per_fold * folds * width)
    )


def unfolded_columns(out_rows, folds, count):
    per_fold = count // folds
    depth = out_rows.shape[0] // folds
    width = out_rows.shape[1] // count
    return (
        out_rows.reshape(folds, depth, per_fold, folds, width)
        .transpose(0, 2, 3, 1, 4)
        .reshape(count, folds * depth, width)
    )


def gathered_params(block_number, device_shards):
    w_in, w_conv, w_out = (device_shards[i][block_number] for i in (2, 6, 10))
    first_rows = w_in.shape[0]
    taps, middle_rows, width = w_conv.shape
    folds = w_out.shape[1] // width
    count = lax.axis_size("seq")
    hidden = width * count
    by_seq = seq_gathered(weight_pack(block_number, device_shards))
    straight = first_rows + taps * middle_rows
    upper = by_seq[:, :straight].transpose(1, 0, 2).reshape(straight, hidden)
    lower = folded_columns(by_seq[:, straight:].reshape(count, folds, middle_rows, width))
    vectors = vector_pack(block_number, device_shards, hidden)
    whole = lax.all_gather(jnp.concatenate([upper, lower, vectors]), "dp")
    parts = whole.shape[0]
    w_first = whole[:, :first_rows].reshape(parts * first_rows, hidden)
    w_middle = (
        whole[:, first_rows:straight]
        .reshape(parts, taps, middle_rows, hidden)
        .transpose(1, 0, 2, 3)
        .reshape(taps, parts * middle_rows, hidden)
    )
    w_last = jnp.concatenate(
        [
            whole[:, straight + i * middle_rows : straight + (i + 1) * middle_rows].reshape(
                parts * middle_rows, hidden
            )
            for i in range(folds)
        ],
        axis=1,
    )
    flat = whole[:, straight + folds * middle_rows :].reshape(parts, -1).astype(jnp.float32)
    wide_end = 3 * first_rows
    wide = flat[:, :wide_end].reshape(parts, 3, first_rows).transpose(1, 0, 2).reshape(3, -1)
    narrow = (
        flat[:, wide_end : wide_end + 6 * middle_rows]
        .reshape(parts, 6, middle_rows)
        .transpose(1, 0, 2)
        .reshape(6, -1)
    )
    return (w_first, w_middle, w_last, wide, narrow)


def block_forward_pass(inputs, weights, flag_list, dilation_step):
    w_first, w_middle, w_last, wide_vectors, narrow_vectors = weights
    row_count, seq_len, model_width = inputs.shape
    hidden = w_middle.shape[1]
    act_one = norm_gelu(
        inputs.reshape(row_count * seq_len, model_width), wide_vectors[0], wide_vectors[1]
    ).astype(jnp.bfloat16)
    projected = jnp.dot(act_one, w_first, preferred_element_type=jnp.float32) + narrow_vectors[0]
    act_two = norm_gelu(projected, narrow_vectors[1], narrow_vectors[2]).astype(jnp.bfloat16)
    tap_rows = forward_taps(act_two.reshape(row_count, seq_len, hidden), flag_list, dilation_step)
    conv_out = (
        jnp.dot(
            tap_rows, w_middle.reshape(KER * hidden, hidden), preferred_element_type=jnp.float32
        )
        + narrow_vectors[3]
    )
    act_three = norm_gelu(conv_out, narrow_vectors[4], narrow_vectors[5]).astype(jnp.bfloat16)
    branch = jnp.dot(act_three, w_last, preferred_element_type=jnp.float32) + wide_vectors[2]
    output = inputs + branch.reshape(row_count, seq_len, model_width)
    return (output, (act_one, projected, tap_rows, conv_out, act_three))


def backward_block(inputs, upstream, weights, kept_values, flag_list, dilation_step):
    w_first, w_middle, w_last, wide_vectors, narrow_vectors = weights
    act_one, projected, tap_rows, conv_out, act_three = kept_values
    row_count, seq_len, model_width = inputs.shape
    hidden = w_middle.shape[1]
    token_count = row_count * seq_len
    grad_branch = upstream.reshape(token_count, model_width).astype(jnp.bfloat16)
    grad_last = contract_rows(act_three, grad_branch)
    grad_out_bias = jnp.sum(grad_branch.astype(jnp.float32), axis=0)
    grad_three = times_transpose(grad_branch, w_last)
    unused_slot, pull_three = jax.vjp(norm_gelu, conv_out, narrow_vectors[4], narrow_vectors[5])
    grad_conv, grad_gain_three, grad_bias_three = pull_three(grad_three)
    grad_conv = grad_conv.astype(jnp.bfloat16)
    grad_conv_bias = jnp.sum(grad_conv.astype(jnp.float32), axis=0)
    grad_middle = contract_rows(tap_rows, grad_conv).reshape(KER, hidden, hidden)
    flipped = jnp.transpose(w_middle, (0, 2, 1)).reshape(KER * hidden, hidden)
    grad_two = jnp.dot(
        backward_taps(grad_conv.reshape(row_count, seq_len, hidden), flag_list, dilation_step),
        flipped,
        preferred_element_type=jnp.float32,
    )
    unused_slot, pull_two = jax.vjp(norm_gelu, projected, narrow_vectors[1], narrow_vectors[2])
    grad_projected, grad_gain_two, grad_bias_two = pull_two(grad_two)
    grad_projected = grad_projected.astype(jnp.bfloat16)
    grad_in_bias = jnp.sum(grad_projected.astype(jnp.float32), axis=0)
    grad_first = contract_rows(act_one, grad_projected)
    grad_one = times_transpose(grad_projected, w_first)
    unused_slot, pull_one = jax.vjp(
        norm_gelu, inputs.reshape(token_count, model_width), wide_vectors[0], wide_vectors[1]
    )
    grad_inputs, grad_gain_one, grad_bias_one = pull_one(grad_one)
    result = upstream + grad_inputs.reshape(row_count, seq_len, model_width)
    wide_grads = jnp.stack([grad_gain_one, grad_bias_one, grad_out_bias])
    narrow_grads = jnp.stack(
        [
            grad_in_bias,
            grad_gain_two,
            grad_bias_two,
            grad_conv_bias,
            grad_gain_three,
            grad_bias_three,
        ]
    )
    return (result, (grad_first, grad_middle, grad_last, wide_grads, narrow_grads))


def reduce_grads(block_grads):
    grad_first, grad_middle, grad_last, wide_grads, narrow_grads = block_grads
    parts = lax.axis_size("dp")
    count = lax.axis_size("seq")
    me = lax.axis_index("seq")
    taps, hidden, _ = grad_middle.shape
    first_rows = grad_first.shape[0] // parts
    middle_rows = hidden // parts
    width = hidden // count
    folds = grad_last.shape[1] // hidden
    short = jnp.bfloat16
    vectors = jnp.concatenate(
        [
            wide_grads.reshape(3, parts, first_rows).transpose(1, 0, 2).reshape(parts, -1),
            narrow_grads.reshape(6, parts, middle_rows).transpose(1, 0, 2).reshape(parts, -1),
        ],
        axis=1,
    ).astype(short)
    length = vectors.shape[1]
    rows = -(-length // (16 * hidden)) * 16
    vectors = jnp.pad(vectors, ((0, 0), (0, rows * hidden - length))).reshape(parts, rows, hidden)
    pieces = [
        grad_first.astype(short).reshape(parts, first_rows, hidden),
        grad_middle.astype(short)
        .reshape(taps, parts, middle_rows, hidden)
        .transpose(1, 0, 2, 3)
        .reshape(parts, taps * middle_rows, hidden),
    ]
    pieces += [
        grad_last[:, i * hidden : (i + 1) * hidden].astype(short).reshape(parts, middle_rows, hidden)
        for i in range(folds)
    ]
    mine = lax.psum_scatter(
        jnp.concatenate(pieces + [vectors], axis=1), "dp", scatter_dimension=0, tiled=False
    )
    straight = first_rows + taps * middle_rows
    total = straight + folds * middle_rows
    upper = mine[:straight].reshape(straight, count, width).transpose(1, 0, 2)
    lower = unfolded_columns(mine[straight:total], folds, count)
    vector_rows = -(-length // width)
    flat = mine[total:].reshape(-1)[:length]
    flat = jnp.pad(flat, (0, vector_rows * width - length)).reshape(1, vector_rows, width)
    ring = jnp.concatenate([upper, lower, jnp.broadcast_to(flat, (count,) + flat.shape[1:])], axis=1)
    ring = jnp.concatenate([ring, ring])
    ring = lax.dynamic_slice_in_dim(ring, me, count, axis=0)
    held = [ring[0]] + [shifted(ring[step], step) for step in range(1, count)]
    held = [block.astype(jnp.float32) for block in held]
    while len(held) > 1:
        half = len(held) // 2
        held = [held[i] + held[i + half] for i in range(half)]
    summed = held[0]
    last = summed[straight:total].reshape(folds, middle_rows, width).transpose(1, 0, 2)
    flat = summed[total:].reshape(-1)
    return (
        summed[:first_rows],
        summed[first_rows:straight].reshape(taps, middle_rows, width),
        last.reshape(middle_rows, folds * width),
        flat[: 3 * first_rows].reshape(3, first_rows),
        flat[3 * first_rows : length].reshape(6, middle_rows),
    )


def local(
    tokens,
    protein_lengths,
    norm1_gain,
    norm1_bias,
    w_in,
    in_bias,
    norm2_gain,
    norm2_bias,
    w_conv,
    conv_bias,
    norm3_gain,
    norm3_bias,
    w_out,
    out_bias,
    cotangent,
):
    device_shards = (
        norm1_gain,
        norm1_bias,
        w_in,
        in_bias,
        norm2_gain,
        norm2_bias,
        w_conv,
        conv_bias,
        norm3_gain,
        norm3_bias,
        w_out,
        out_bias,
    )
    seq_len = tokens.shape[1]
    token_positions = lax.axis_index("seq") * seq_len + jnp.arange(seq_len, dtype=jnp.int32)
    early_tap_flags = kernel_tap_flags(protein_lengths, token_positions, FIRST_DILATION)
    later_tap_flags = kernel_tap_flags(protein_lengths, token_positions, SECOND_DILATION)
    hidden_before_blocks = tokens.astype(jnp.float32)
    early_weights = gathered_params(0, device_shards)
    late_weights = gathered_params(1, device_shards)
    hidden_after_first, early_kept = block_forward_pass(
        hidden_before_blocks, early_weights, early_tap_flags, FIRST_DILATION
    )
    hidden_after_second, late_kept = block_forward_pass(
        hidden_after_first, late_weights, later_tap_flags, SECOND_DILATION
    )
    gradient_after_first, grads_late = backward_block(
        hidden_after_first,
        cotangent.astype(jnp.float32),
        late_weights,
        late_kept,
        later_tap_flags,
        SECOND_DILATION,
    )
    reduced_late = reduce_grads(grads_late)
    grad_stream_zero, grads_early = backward_block(
        hidden_before_blocks,
        gradient_after_first,
        early_weights,
        early_kept,
        early_tap_flags,
        FIRST_DILATION,
    )
    reduced_early = reduce_grads(grads_early)
    first_early, middle_early, last_early, wide_early, narrow_early = reduced_early
    first_late, middle_late, last_late, wide_late, narrow_late = reduced_late
    return (
        hidden_after_second.astype(jnp.bfloat16),
        grad_stream_zero,
        jnp.stack([wide_early[0], wide_late[0]]),
        jnp.stack([wide_early[1], wide_late[1]]),
        jnp.stack([first_early, first_late]),
        jnp.stack([narrow_early[0], narrow_late[0]]),
        jnp.stack([narrow_early[1], narrow_late[1]]),
        jnp.stack([narrow_early[2], narrow_late[2]]),
        jnp.stack([middle_early, middle_late]),
        jnp.stack([narrow_early[3], narrow_late[3]]),
        jnp.stack([narrow_early[4], narrow_late[4]]),
        jnp.stack([narrow_early[5], narrow_late[5]]),
        jnp.stack([last_early, last_late]),
        jnp.stack([wide_early[2], wide_late[2]]),
    )


def solution(mesh):
    placed = (
        P("dp", "seq", None),
        P("dp", None),
        P(None, "dp"),
        P(None, "dp"),
        P(None, "dp", "seq"),
        P(None, "dp"),
        P(None, "dp"),
        P(None, "dp"),
        P(None, None, "dp", "seq"),
        P(None, "dp"),
        P(None, "dp"),
        P(None, "dp"),
        P(None, "dp", "seq"),
        P(None, "dp"),
        P("dp", "seq", None),
    )
    return jax.shard_map(
        local,
        mesh=mesh,
        in_specs=placed,
        out_specs=(
            P("dp", "seq", None),
            P("dp", "seq", None),
            P(None, "dp"),
            P(None, "dp"),
            P(None, "dp", "seq"),
            P(None, "dp"),
            P(None, "dp"),
            P(None, "dp"),
            P(None, None, "dp", "seq"),
            P(None, "dp"),
            P(None, "dp"),
            P(None, "dp"),
            P(None, "dp", "seq"),
            P(None, "dp"),
        ),
        check_vma=False,
    )
```

```python
import functools
import math

import jax
import jax.numpy as jnp
from jax import lax
from jax.experimental import pallas as pl
from jax.experimental.pallas import tpu as pltpu
from jax.sharding import PartitionSpec as P

KER = 5
FIRST_DILATION = 64
SECOND_DILATION = 128


epsilon = 1e-05
CUBIC = 0.044715
SLOPE = math.sqrt(2.0 / math.pi)
VECTOR_ROWS = 16


def seq_neighbours(block, width):
    count = lax.axis_size("seq")
    forward = [(i, i + 1) for i in range(count - 1)]
    backward = [(target, source) for source, target in forward]
    low = lax.ppermute(block[:, block.shape[1] - width :], "seq", forward)
    high = lax.ppermute(block[:, :width], "seq", backward)
    return low, high


def normalized(values):
    centred = values - jnp.mean(values, -1, keepdims=True)
    scale = lax.rsqrt(jnp.mean(centred * centred, -1, keepdims=True) + epsilon)
    return centred * scale, scale


def gelu(h):
    return 0.5 * h * (1.0 + jnp.tanh(SLOPE * (h + CUBIC * (h * h * h))))


def norm_gelu(values, gain_vector, bias_vector):
    return gelu(normalized(values)[0] * gain_vector + bias_vector)


def norm_gelu_back(incoming, values, gain_vector, bias_vector):
    n, scale = normalized(values)
    h = n * gain_vector + bias_vector
    square = h * h
    t = jnp.tanh(SLOPE * (h + CUBIC * (square * h)))
    slope = 0.5 * (1.0 + t) + (0.5 * SLOPE) * h * (1.0 - t * t) * (1.0 + (3.0 * CUBIC) * square)
    dh = incoming * slope
    dn = dh * gain_vector
    back = dn - jnp.mean(dn, -1, keepdims=True) - n * jnp.mean(dn * n, -1, keepdims=True)
    return back * scale, column_sum(dh * n), column_sum(dh)


def column_sum(values):
    return jnp.sum(values, axis=0, keepdims=True)


def matmul(left, right):
    return jnp.dot(left, right, preferred_element_type=jnp.float32)


def matmul_back(left, right):
    return lax.dot_general(
        left, right, (((1,), (1,)), ((), ())), preferred_element_type=jnp.float32
    )


def matmul_rows(left, right):
    return lax.dot_general(
        left, right, (((0,), (0,)), ((), ())), preferred_element_type=jnp.float32
    )


def merged(ref):
    parts, rows, columns = ref.shape
    return ref[...].reshape(parts * rows, columns)


def kernel_tap_flags(lengths, token_positions, dilation_step):
    doc_ends = jnp.cumsum(lengths, axis=1)
    row_total = doc_ends[:, -1:]
    where_pos = token_positions[None, :, None]
    finished = doc_ends[:, None, :] <= where_pos
    doc_start = jnp.sum(jnp.where(finished, lengths[:, None, :], 0), axis=2)
    doc_stop = jnp.min(jnp.where(finished, row_total[:, :, None] + 1, doc_ends[:, None, :]), axis=2)
    is_live = token_positions[None, :] < row_total
    flag_list = []
    for tap_index in range(KER):
        target = token_positions[None, :] + (tap_index - KER // 2) * dilation_step
        flag_list.append(is_live & (target >= doc_start) & (target < doc_stop))
    flag_list += [flag_list[-1]] * (8 - KER)
    return jnp.stack(flag_list, axis=2).astype(jnp.bfloat16)


def project_kernel(x_ref, w_ref, wide_ref, narrow_ref, act_one_ref, u_ref, act_two_ref):
    act_one = norm_gelu(
        x_ref[...].astype(jnp.float32), wide_ref[0:1, :], wide_ref[1:2, :]
    ).astype(jnp.bfloat16)
    act_one_ref[...] = act_one
    u = matmul(act_one, merged(w_ref)) + narrow_ref[0:1, :]
    u_ref[...] = u
    act_two_ref[...] = norm_gelu(u, narrow_ref[1:2, :], narrow_ref[2:3, :]).astype(jnp.bfloat16)


def tap_slices(low_ref, own_ref, high_ref, flag_ref, dilation_step):
    length = own_ref.shape[1]
    width = low_ref.shape[1]
    padded = jnp.concatenate([low_ref[0], own_ref[0], high_ref[0]], axis=0)
    for k in range(KER):
        start = width + (k - KER // 2) * dilation_step
        yield k, padded[start : start + length] * flag_ref[0][:, k : k + 1]


def convolve_kernel(
    dilation_step,
    low_ref,
    own_ref,
    high_ref,
    flag_ref,
    x_ref,
    k0_ref,
    k1_ref,
    k2_ref,
    k3_ref,
    k4_ref,
    left_ref,
    right_ref,
    wide_ref,
    narrow_ref,
    tap_ref,
    v_ref,
    act_three_ref,
    next_ref,
):
    taps = (k0_ref, k1_ref, k2_ref, k3_ref, k4_ref)
    hidden = own_ref.shape[2]
    total = narrow_ref[3:4, :]
    for k, piece in tap_slices(low_ref, own_ref, high_ref, flag_ref, dilation_step):
        tap_ref[:, k * hidden : (k + 1) * hidden] = piece
        total = total + matmul(piece, merged(taps[k]))
    v_ref[...] = total
    act_three = norm_gelu(total, narrow_ref[4:5, :], narrow_ref[5:6, :]).astype(jnp.bfloat16)
    act_three_ref[...] = act_three
    for i, half_ref in enumerate((left_ref, right_ref)):
        columns = slice(i * hidden, (i + 1) * hidden)
        branch = matmul(act_three, merged(half_ref)) + wide_ref[2:3, columns]
        next_ref[:, columns] = (x_ref[:, columns].astype(jnp.float32) + branch).astype(
            next_ref.dtype
        )


def out_back_kernel(
    g_ref, v_ref, left_ref, right_ref, narrow_ref, short_ref, gv_ref, narrow_sum_ref, wide_sum_ref
):
    hidden = v_ref.shape[1]

    @pl.when(pl.program_id(0) == 0)
    def _():
        narrow_sum_ref[...] = jnp.zeros_like(narrow_sum_ref)
        wide_sum_ref[...] = jnp.zeros_like(wide_sum_ref)

    short = g_ref[...].astype(jnp.bfloat16)
    short_ref[...] = short
    wide_sum_ref[0:1, :] += column_sum(short.astype(jnp.float32))
    incoming = matmul_back(short[:, :hidden], merged(left_ref))
    incoming = incoming + matmul_back(short[:, hidden:], merged(right_ref))
    gv, gain_sum, bias_sum = norm_gelu_back(
        incoming, v_ref[...], narrow_ref[4:5, :], narrow_ref[5:6, :]
    )
    gv = gv.astype(jnp.bfloat16)
    gv_ref[...] = gv
    narrow_sum_ref[0:1, :] += column_sum(gv.astype(jnp.float32))
    narrow_sum_ref[1:2, :] += gain_sum
    narrow_sum_ref[2:3, :] += bias_sum


def weight_grad_kernel(tap_ref, gv_ref, act_three_ref, short_ref, pack_ref):
    step = pl.program_id(0)

    def store(value):
        pack_ref[...] = value.astype(jnp.bfloat16).reshape(pack_ref.shape)

    @pl.when(step < KER)
    def _():
        store(matmul_rows(tap_ref[...], gv_ref[...]))

    @pl.when(step >= KER)
    def _():
        store(matmul_rows(act_three_ref[...], short_ref[...]))


def conv_back_kernel(
    dilation_step,
    low_ref,
    own_ref,
    high_ref,
    flag_ref,
    u_ref,
    x_ref,
    g_ref,
    k0_ref,
    k1_ref,
    k2_ref,
    k3_ref,
    k4_ref,
    w_ref,
    wide_ref,
    narrow_ref,
    gu_ref,
    next_ref,
    narrow_sum_ref,
    wide_sum_ref,
):
    @pl.when(pl.program_id(0) == 0)
    def _():
        narrow_sum_ref[...] = jnp.zeros_like(narrow_sum_ref)
        wide_sum_ref[...] = jnp.zeros_like(wide_sum_ref)

    taps = (k0_ref, k1_ref, k2_ref, k3_ref, k4_ref)
    total = None
    for k, piece in tap_slices(low_ref, own_ref, high_ref, flag_ref, dilation_step):
        term = matmul_back(piece, merged(taps[KER - 1 - k]))
        total = term if total is None else total + term
    gu, gain_sum, bias_sum = norm_gelu_back(
        total, u_ref[...], narrow_ref[1:2, :], narrow_ref[2:3, :]
    )
    gu = gu.astype(jnp.bfloat16)
    gu_ref[...] = gu
    narrow_sum_ref[0:1, :] += column_sum(gu.astype(jnp.float32))
    narrow_sum_ref[1:2, :] += gain_sum
    narrow_sum_ref[2:3, :] += bias_sum
    gx, gain_sum, bias_sum = norm_gelu_back(
        matmul_back(gu, merged(w_ref)),
        x_ref[...].astype(jnp.float32),
        wide_ref[0:1, :],
        wide_ref[1:2, :],
    )
    next_ref[...] = g_ref[...].astype(jnp.float32) + gx
    wide_sum_ref[0:1, :] += gain_sum
    wide_sum_ref[1:2, :] += bias_sum


def in_grad_kernel(pack_in_ref, act_one_ref, gu_ref, pack_ref):
    value = matmul_rows(act_one_ref[...], gu_ref[...])
    pack_ref[...] = value.astype(jnp.bfloat16).reshape(pack_ref.shape)


def tiled(rows, columns):
    return pl.BlockSpec((rows, columns), lambda i: (i, 0))


def fixed(*shape):
    return pl.BlockSpec(shape, lambda i: (0,) * len(shape))


def row_block(shape):
    return pl.BlockSpec((1,) + shape[1:], lambda i: (i, 0, 0))


def pack_block(parts, rows, columns, index):
    return pl.BlockSpec((parts, rows, columns), lambda i: (0, index, 0))


def cost(flops, width):
    return pl.CostEstimate(flops=flops, bytes_accessed=width, transcendentals=0)


def call(kernel, grid, in_specs, out_specs, out_shape, flops, moved, name, aliases=None):
    return pl.pallas_call(
        kernel,
        grid=(grid,),
        in_specs=in_specs,
        out_specs=out_specs,
        out_shape=out_shape,
        input_output_aliases=aliases or {},
        cost_estimate=cost(flops, moved),
        compiler_params=pltpu.CompilerParams(vmem_limit_bytes=48 * 1024 * 1024),
        name=name,
    )


def shape_of(shape, dtype):
    return jax.ShapeDtypeStruct(shape, dtype)


class Sizes:
    def __init__(self, pack, model, hidden):
        self.parts = pack.shape[0]
        self.model, self.hidden = model, hidden
        self.first_rows = model // self.parts
        self.middle_rows = hidden // self.parts
        self.folds = model // hidden
        self.conv_at = self.first_rows // self.middle_rows
        self.out_at = self.conv_at + KER

    def first(self):
        return pack_block(self.parts, self.first_rows, self.hidden, 0)

    def taps(self):
        return [
            pack_block(self.parts, self.middle_rows, self.hidden, self.conv_at + k)
            for k in range(KER)
        ]

    def last(self):
        return [
            pack_block(self.parts, self.middle_rows, self.hidden, self.out_at + i)
            for i in range(self.folds)
        ]


def project(inputs, weights):
    pack, wide, narrow = weights
    tokens, model = inputs.shape
    hidden = narrow.shape[1]
    sizes = Sizes(pack, model, hidden)
    tile = min(128, tokens)
    return call(
        project_kernel,
        tokens // tile,
        [tiled(tile, model), sizes.first(), fixed(3, model), fixed(6, hidden)],
        [tiled(tile, model), tiled(tile, hidden), tiled(tile, hidden)],
        [
            shape_of((tokens, model), jnp.bfloat16),
            shape_of((tokens, hidden), jnp.float32),
            shape_of((tokens, hidden), jnp.bfloat16),
        ],
        4 * tokens * model * hidden,
        12 * tokens * model,
        "project",
    )(inputs, pack, wide, narrow)


def convolve(act_two, flags, inputs, weights, dilation_step, next_dtype):
    pack, wide, narrow = weights
    rows, length, hidden = act_two.shape
    tokens, model = inputs.shape
    sizes = Sizes(pack, model, hidden)
    low, high = seq_neighbours(act_two, KER // 2 * dilation_step)
    return call(
        functools.partial(convolve_kernel, dilation_step),
        rows,
        [
            row_block(low.shape),
            row_block(act_two.shape),
            row_block(high.shape),
            row_block(flags.shape),
            tiled(length, model),
            *sizes.taps(),
            *sizes.last(),
            fixed(3, model),
            fixed(6, hidden),
        ],
        [
            tiled(length, KER * hidden),
            tiled(length, hidden),
            tiled(length, hidden),
            tiled(length, model),
        ],
        [
            shape_of((tokens, KER * hidden), jnp.bfloat16),
            shape_of((tokens, hidden), jnp.float32),
            shape_of((tokens, hidden), jnp.bfloat16),
            shape_of((tokens, model), next_dtype),
        ],
        2 * tokens * hidden * (KER * hidden + model),
        16 * tokens * model,
        "convolve",
    )(low, act_two, high, flags, inputs, *([pack] * (KER + 2)), wide, narrow)


def out_back(upstream, conv_out, weights):
    pack, wide, narrow = weights
    tokens, model = upstream.shape
    hidden = narrow.shape[1]
    sizes = Sizes(pack, model, hidden)
    tile = min(128, tokens)
    return call(
        out_back_kernel,
        tokens // tile,
        [tiled(tile, model), tiled(tile, hidden), *sizes.last(), fixed(6, hidden)],
        [tiled(tile, model), tiled(tile, hidden), fixed(8, hidden), fixed(8, model)],
        [
            shape_of((tokens, model), jnp.bfloat16),
            shape_of((tokens, hidden), jnp.bfloat16),
            shape_of((8, hidden), jnp.float32),
            shape_of((8, model), jnp.float32),
        ],
        4 * tokens * model * hidden,
        10 * tokens * model,
        "out_back",
    )(upstream, conv_out, pack, pack, narrow)


def weight_grads(tap_rows, gv, act_three, short, pack):
    tokens, hidden = gv.shape
    model = short.shape[1]
    sizes = Sizes(pack, model, hidden)
    whole = pl.BlockSpec((tokens, hidden), lambda s: (0, 0))
    return call(
        weight_grad_kernel,
        KER + sizes.folds,
        [
            pl.BlockSpec((tokens, hidden), lambda s: (0, jnp.minimum(s, KER - 1))),
            whole,
            whole,
            pl.BlockSpec((tokens, hidden), lambda s: (0, jnp.maximum(s - KER, 0))),
        ],
        pl.BlockSpec(
            (sizes.parts, sizes.middle_rows, hidden), lambda s: (0, sizes.conv_at + s, 0)
        ),
        shape_of(pack.shape, jnp.bfloat16),
        2 * tokens * hidden * (KER * hidden + model),
        8 * tokens * model,
        "weight_grads",
    )(tap_rows, gv, act_three, short)


def conv_back(gv, flags, u, inputs, upstream, weights, dilation_step):
    pack, wide, narrow = weights
    rows, length, hidden = gv.shape
    tokens, model = inputs.shape
    sizes = Sizes(pack, model, hidden)
    low, high = seq_neighbours(gv, KER // 2 * dilation_step)
    return call(
        functools.partial(conv_back_kernel, dilation_step),
        rows,
        [
            row_block(low.shape),
            row_block(gv.shape),
            row_block(high.shape),
            row_block(flags.shape),
            tiled(length, hidden),
            tiled(length, model),
            tiled(length, model),
            *sizes.taps(),
            sizes.first(),
            fixed(3, model),
            fixed(6, hidden),
        ],
        [tiled(length, hidden), tiled(length, model), fixed(8, hidden), fixed(8, model)],
        [
            shape_of((tokens, hidden), jnp.bfloat16),
            shape_of((tokens, model), jnp.float32),
            shape_of((8, hidden), jnp.float32),
            shape_of((8, model), jnp.float32),
        ],
        2 * tokens * hidden * (KER * hidden + model),
        16 * tokens * model,
        "conv_back",
    )(low, gv, high, flags, u, inputs, upstream, *([pack] * (KER + 1)), wide, narrow)


def in_grads(grad_pack, act_one, gu):
    tokens, model = act_one.shape
    hidden = gu.shape[1]
    sizes = Sizes(grad_pack, model, hidden)
    return call(
        in_grad_kernel,
        1,
        [pl.BlockSpec(memory_space=pl.ANY), fixed(tokens, model), fixed(tokens, hidden)],
        sizes.first(),
        shape_of(grad_pack.shape, jnp.bfloat16),
        2 * tokens * hidden * model,
        4 * tokens * model,
        "in_grads",
        {0: 0},
    )(grad_pack, act_one, gu)


def shifted(block, step):
    count = lax.axis_size("seq")
    return lax.ppermute(block, "seq", [(i, (i + step) % count) for i in range(count)])


def weight_pack(block_number, device_shards):
    w_in, w_conv, w_out = (device_shards[i][block_number] for i in (2, 6, 10))
    width = w_in.shape[1]
    folds = w_out.shape[1] // width
    pieces = [w_in, w_conv.reshape(-1, width)]
    pieces += [w_out[:, i * width : (i + 1) * width] for i in range(folds)]
    return jnp.concatenate(pieces, axis=0)


def vector_pack(block_number, device_shards, width):
    order = (0, 1, 11, 3, 4, 5, 7, 8, 9)
    rows = [device_shards[i][block_number] for i in order]
    rows = [jnp.pad(row, (0, width - row.shape[0])) for row in rows]
    return jnp.pad(jnp.stack(rows), ((0, VECTOR_ROWS - len(rows)), (0, 0)))


def seq_gathered(packed):
    count = lax.axis_size("seq")
    me = lax.axis_index("seq")
    held = [packed] + [shifted(packed, step) for step in range(1, count)]
    ring = jnp.stack(held[::-1] + held[::-1])
    return lax.dynamic_slice_in_dim(ring, (count - 1 - me) % count, count, axis=0)


def folded_columns(out_parts):
    count, folds, depth, width = out_parts.shape
    per_fold = count // folds
    return (
        out_parts.reshape(folds, per_fold, folds, depth, width)
        .transpose(0, 3, 1, 2, 4)
        .reshape(folds * depth, per_fold * folds * width)
    )


def unfolded_columns(out_rows, folds, count):
    per_fold = count // folds
    depth = out_rows.shape[0] // folds
    width = out_rows.shape[1] // count
    return (
        out_rows.reshape(folds, depth, per_fold, folds, width)
        .transpose(0, 2, 3, 1, 4)
        .reshape(count, folds * depth, width)
    )


def pack_is_aligned(middle_rows):
    return middle_rows % 16 == 0


def gathered_params(block_number, device_shards):
    w_in, w_conv, w_out = (device_shards[i][block_number] for i in (2, 6, 10))
    first_rows = w_in.shape[0]
    taps, middle_rows, width = w_conv.shape
    folds = w_out.shape[1] // width
    count = lax.axis_size("seq")
    hidden = width * count
    by_seq = seq_gathered(weight_pack(block_number, device_shards))
    straight = first_rows + taps * middle_rows
    total = straight + folds * middle_rows
    upper = by_seq[:, :straight].transpose(1, 0, 2).reshape(straight, hidden)
    lower = folded_columns(by_seq[:, straight:].reshape(count, folds, middle_rows, width))
    vectors = vector_pack(block_number, device_shards, hidden)
    whole = lax.all_gather(jnp.concatenate([upper, lower, vectors]), "dp")
    tail = whole[:, total:].astype(jnp.float32)
    wide = tail[:, :3, :first_rows].transpose(1, 0, 2).reshape(3, -1)
    narrow = tail[:, 3:9, :middle_rows].transpose(1, 0, 2).reshape(6, -1)
    if not pack_is_aligned(middle_rows):
        bounds = [0, first_rows]
        bounds += [first_rows + (k + 1) * middle_rows for k in range(taps + folds)]
        whole = jnp.concatenate(
            [whole[:, a:b].reshape(1, -1, hidden) for a, b in zip(bounds, bounds[1:])], axis=1
        )
    return (whole, wide, narrow)


def reduce_grads(grad_pack, wide_grads, narrow_grads):
    parts = lax.axis_size("dp")
    count = lax.axis_size("seq")
    me = lax.axis_index("seq")
    hidden = narrow_grads.shape[1]
    model = wide_grads.shape[1]
    first_rows = model // parts
    middle_rows = hidden // parts
    width = hidden // count
    folds = model // hidden
    straight = first_rows + KER * middle_rows
    total = straight + folds * middle_rows
    if not pack_is_aligned(middle_rows):
        bounds = [0, model] + [model + (k + 1) * hidden for k in range(KER + folds)]
        grad_pack = jnp.concatenate(
            [grad_pack[0, a:b].reshape(parts, -1, hidden) for a, b in zip(bounds, bounds[1:])]
            + [jnp.zeros((parts, VECTOR_ROWS, hidden), jnp.bfloat16)],
            axis=1,
        )
    vectors = jnp.concatenate(
        [
            jnp.pad(
                block.reshape(-1, parts, rows).transpose(1, 0, 2),
                ((0, 0), (0, 0), (0, hidden - rows)),
            )
            for block, rows in ((wide_grads, first_rows), (narrow_grads, middle_rows))
        ]
        + [jnp.zeros((parts, VECTOR_ROWS - 9, hidden), jnp.float32)],
        axis=1,
    ).astype(jnp.bfloat16)
    grad_pack = lax.dynamic_update_slice(grad_pack, vectors, (0, total, 0))
    mine = lax.psum_scatter(grad_pack, "dp", scatter_dimension=0, tiled=False)
    upper = mine[:straight].reshape(straight, count, width).transpose(1, 0, 2)
    lower = unfolded_columns(mine[straight:total], folds, count)
    fold = -(-first_rows // width)
    tail = mine[total:, : fold * width].reshape(1, VECTOR_ROWS * fold, width)
    tail = jnp.broadcast_to(tail, (count,) + tail.shape[1:])
    ring = jnp.concatenate([upper, lower, tail], axis=1)
    ring = jnp.concatenate([ring, ring])
    ring = lax.dynamic_slice_in_dim(ring, me, count, axis=0)
    held = [ring[0]] + [shifted(ring[step], step) for step in range(1, count)]
    held = [block.astype(jnp.float32) for block in held]
    while len(held) > 1:
        half = len(held) // 2
        held = [held[i] + held[i + half] for i in range(half)]
    summed = held[0]
    last = summed[straight:total].reshape(folds, middle_rows, width).transpose(1, 0, 2)
    tail = summed[total:].reshape(VECTOR_ROWS, fold * width)
    return (
        summed[:first_rows],
        summed[first_rows:straight].reshape(KER, middle_rows, width),
        last.reshape(middle_rows, folds * width),
        tail[:3, :first_rows],
        tail[3:9, :middle_rows],
    )


def block_forward(inputs, weights, flags, dilation_step, next_dtype):
    rows, length, _ = flags.shape
    act_one, u, act_two = project(inputs, weights)
    tap_rows, conv_out, act_three, output = convolve(
        act_two.reshape(rows, length, -1), flags, inputs, weights, dilation_step, next_dtype
    )
    return output, (act_one, u, tap_rows, conv_out, act_three)


def block_backward(inputs, upstream, weights, kept, flags, dilation_step):
    act_one, u, tap_rows, conv_out, act_three = kept
    rows, length, _ = flags.shape
    short, gv, narrow_a, wide_a = out_back(upstream, conv_out, weights)
    pack = weights[0]
    grad_shape = shape_of(
        (pack.shape[0], sum(pack_rows(pack, inputs.shape[1], gv.shape[1])), gv.shape[1]),
        jnp.bfloat16,
    )
    grad_pack = weight_grads(tap_rows, gv, act_three, short, grad_shape)
    gu, result, narrow_b, wide_b = conv_back(
        gv.reshape(rows, length, -1), flags, u, inputs, upstream, weights, dilation_step
    )
    grad_pack = in_grads(grad_pack, act_one, gu)
    wide = jnp.concatenate([wide_b[0:2], wide_a[0:1]])
    narrow = jnp.concatenate([narrow_b[0:3], narrow_a[0:3]])
    return result, (grad_pack, wide, narrow)


def pack_rows(pack, model, hidden):
    parts = pack.shape[0]
    extra = VECTOR_ROWS if pack_is_aligned(hidden // lax.axis_size("dp")) else 0
    return model // parts, (KER * hidden + model) // parts, extra


def local(
    tokens,
    protein_lengths,
    norm1_gain,
    norm1_bias,
    w_in,
    in_bias,
    norm2_gain,
    norm2_bias,
    w_conv,
    conv_bias,
    norm3_gain,
    norm3_bias,
    w_out,
    out_bias,
    cotangent,
):
    device_shards = (
        norm1_gain,
        norm1_bias,
        w_in,
        in_bias,
        norm2_gain,
        norm2_bias,
        w_conv,
        conv_bias,
        norm3_gain,
        norm3_bias,
        w_out,
        out_bias,
    )
    rows, seq_len, model = tokens.shape
    token_positions = lax.axis_index("seq") * seq_len + jnp.arange(seq_len, dtype=jnp.int32)
    early_flags = kernel_tap_flags(protein_lengths, token_positions, FIRST_DILATION)
    later_flags = kernel_tap_flags(protein_lengths, token_positions, SECOND_DILATION)
    early_weights = gathered_params(0, device_shards)
    late_weights = gathered_params(1, device_shards)
    flat_tokens = tokens.reshape(rows * seq_len, model)
    middle, early_kept = block_forward(
        flat_tokens, early_weights, early_flags, FIRST_DILATION, jnp.float32
    )
    middle, late_weights = lax.optimization_barrier((middle, late_weights))
    output, late_kept = block_forward(
        middle, late_weights, later_flags, SECOND_DILATION, jnp.bfloat16
    )
    middle_grad, grads_late = block_backward(
        middle,
        cotangent.reshape(rows * seq_len, model),
        late_weights,
        late_kept,
        later_flags,
        SECOND_DILATION,
    )
    reduced_late = reduce_grads(*grads_late)
    input_grad, grads_early = block_backward(
        flat_tokens, middle_grad, early_weights, early_kept, early_flags, FIRST_DILATION
    )
    reduced_early = reduce_grads(*grads_early)
    first_early, middle_early, last_early, wide_early, narrow_early = reduced_early
    first_late, middle_late, last_late, wide_late, narrow_late = reduced_late
    return (
        output.reshape(tokens.shape),
        input_grad.reshape(tokens.shape),
        jnp.stack([wide_early[0], wide_late[0]]),
        jnp.stack([wide_early[1], wide_late[1]]),
        jnp.stack([first_early, first_late]),
        jnp.stack([narrow_early[0], narrow_late[0]]),
        jnp.stack([narrow_early[1], narrow_late[1]]),
        jnp.stack([narrow_early[2], narrow_late[2]]),
        jnp.stack([middle_early, middle_late]),
        jnp.stack([narrow_early[3], narrow_late[3]]),
        jnp.stack([narrow_early[4], narrow_late[4]]),
        jnp.stack([narrow_early[5], narrow_late[5]]),
        jnp.stack([last_early, last_late]),
        jnp.stack([wide_early[2], wide_late[2]]),
    )


def solution(mesh):
    placed = (
        P("dp", "seq", None),
        P("dp", None),
        P(None, "dp"),
        P(None, "dp"),
        P(None, "dp", "seq"),
        P(None, "dp"),
        P(None, "dp"),
        P(None, "dp"),
        P(None, None, "dp", "seq"),
        P(None, "dp"),
        P(None, "dp"),
        P(None, "dp"),
        P(None, "dp", "seq"),
        P(None, "dp"),
        P("dp", "seq", None),
    )
    return jax.shard_map(
        local,
        mesh=mesh,
        in_specs=placed,
        out_specs=(
            P("dp", "seq", None),
            P("dp", "seq", None),
            P(None, "dp"),
            P(None, "dp"),
            P(None, "dp", "seq"),
            P(None, "dp"),
            P(None, "dp"),
            P(None, "dp"),
            P(None, None, "dp", "seq"),
            P(None, "dp"),
            P(None, "dp"),
            P(None, "dp"),
            P(None, "dp", "seq"),
            P(None, "dp"),
        ),
        check_vma=False,
    )
```

```python
import functools
import math

import jax
import jax.numpy as jnp
from jax import lax
from jax.experimental import pallas as pl
from jax.experimental.pallas import tpu as pltpu
from jax.sharding import PartitionSpec as P

KER = 5
FIRST_DILATION = 64
SECOND_DILATION = 128


epsilon = 1e-05
CUBIC = 0.044715
SLOPE = math.sqrt(2.0 / math.pi)
VECTOR_ROWS = 16


def seq_neighbours(block, width):
    count = lax.axis_size("seq")
    forward = [(i, i + 1) for i in range(count - 1)]
    backward = [(target, source) for source, target in forward]
    low = lax.ppermute(block[:, block.shape[1] - width :], "seq", forward)
    high = lax.ppermute(block[:, :width], "seq", backward)
    return low, high


def normalized(values):
    centred = values - jnp.mean(values, -1, keepdims=True)
    scale = lax.rsqrt(jnp.mean(centred * centred, -1, keepdims=True) + epsilon)
    return centred * scale, scale


def gelu(h):
    return 0.5 * h * (1.0 + jnp.tanh(SLOPE * (h + CUBIC * (h * h * h))))


def norm_gelu(values, gain_vector, bias_vector):
    return gelu(normalized(values)[0] * gain_vector + bias_vector)


def norm_gelu_back(incoming, values, gain_vector, bias_vector):
    n, scale = normalized(values)
    h = n * gain_vector + bias_vector
    square = h * h
    t = jnp.tanh(SLOPE * (h + CUBIC * (square * h)))
    slope = 0.5 * (1.0 + t) + (0.5 * SLOPE) * h * (1.0 - t * t) * (1.0 + (3.0 * CUBIC) * square)
    dh = incoming * slope
    dn = dh * gain_vector
    back = dn - jnp.mean(dn, -1, keepdims=True) - n * jnp.mean(dn * n, -1, keepdims=True)
    return back * scale, column_sum(dh * n), column_sum(dh)


def column_sum(values):
    return jnp.sum(values, axis=0, keepdims=True)


def matmul(left, right):
    return jnp.dot(left, right, preferred_element_type=jnp.float32)


def matmul_back(left, right):
    return lax.dot_general(
        left, right, (((1,), (1,)), ((), ())), preferred_element_type=jnp.float32
    )


def matmul_rows(left, right):
    return lax.dot_general(
        left, right, (((0,), (0,)), ((), ())), preferred_element_type=jnp.float32
    )


def merged(ref):
    parts, rows, columns = ref.shape
    return ref[...].reshape(parts * rows, columns)


def kernel_tap_flags(lengths, token_positions, dilation_step):
    doc_ends = jnp.cumsum(lengths, axis=1)
    row_total = doc_ends[:, -1:]
    where_pos = token_positions[None, :, None]
    finished = doc_ends[:, None, :] <= where_pos
    doc_start = jnp.sum(jnp.where(finished, lengths[:, None, :], 0), axis=2)
    doc_stop = jnp.min(jnp.where(finished, row_total[:, :, None] + 1, doc_ends[:, None, :]), axis=2)
    is_live = token_positions[None, :] < row_total
    flag_list = []
    for tap_index in range(KER):
        target = token_positions[None, :] + (tap_index - KER // 2) * dilation_step
        flag_list.append(is_live & (target >= doc_start) & (target < doc_stop))
    flag_list += [flag_list[-1]] * (8 - KER)
    return jnp.stack(flag_list, axis=2).astype(jnp.bfloat16)


def project_kernel(x_ref, w_ref, wide_ref, narrow_ref, act_one_ref, u_ref, act_two_ref):
    act_one = norm_gelu(
        x_ref[...].astype(jnp.float32), wide_ref[0:1, :], wide_ref[1:2, :]
    ).astype(jnp.bfloat16)
    act_one_ref[...] = act_one
    u = matmul(act_one, merged(w_ref)) + narrow_ref[0:1, :]
    u_ref[...] = u
    act_two_ref[...] = norm_gelu(u, narrow_ref[1:2, :], narrow_ref[2:3, :]).astype(jnp.bfloat16)


def tap_slices(low_ref, own_ref, high_ref, flag_ref, dilation_step):
    length = own_ref.shape[1]
    width = low_ref.shape[1]
    padded = jnp.concatenate([low_ref[0], own_ref[0], high_ref[0]], axis=0)
    for k in range(KER):
        start = width + (k - KER // 2) * dilation_step
        yield k, padded[start : start + length] * flag_ref[0][:, k : k + 1]


def convolve_kernel(
    dilation_step,
    low_ref,
    own_ref,
    high_ref,
    flag_ref,
    x_ref,
    k0_ref,
    k1_ref,
    k2_ref,
    k3_ref,
    k4_ref,
    left_ref,
    right_ref,
    wide_ref,
    narrow_ref,
    tap_ref,
    v_ref,
    act_three_ref,
    next_ref,
):
    taps = (k0_ref, k1_ref, k2_ref, k3_ref, k4_ref)
    hidden = own_ref.shape[2]
    total = narrow_ref[3:4, :]
    for k, piece in tap_slices(low_ref, own_ref, high_ref, flag_ref, dilation_step):
        tap_ref[:, k * hidden : (k + 1) * hidden] = piece
        total = total + matmul(piece, merged(taps[k]))
    v_ref[...] = total
    act_three = norm_gelu(total, narrow_ref[4:5, :], narrow_ref[5:6, :]).astype(jnp.bfloat16)
    act_three_ref[...] = act_three
    for i, half_ref in enumerate((left_ref, right_ref)):
        columns = slice(i * hidden, (i + 1) * hidden)
        branch = matmul(act_three, merged(half_ref)) + wide_ref[2:3, columns]
        next_ref[:, columns] = (x_ref[:, columns].astype(jnp.float32) + branch).astype(
            next_ref.dtype
        )


def out_back_kernel(
    g_ref, v_ref, left_ref, right_ref, narrow_ref, short_ref, gv_ref, narrow_sum_ref, wide_sum_ref
):
    hidden = v_ref.shape[1]

    @pl.when(pl.program_id(0) == 0)
    def _():
        narrow_sum_ref[...] = jnp.zeros_like(narrow_sum_ref)
        wide_sum_ref[...] = jnp.zeros_like(wide_sum_ref)

    short = g_ref[...].astype(jnp.bfloat16)
    short_ref[...] = short
    wide_sum_ref[0:1, :] += column_sum(short.astype(jnp.float32))
    incoming = matmul_back(short[:, :hidden], merged(left_ref))
    incoming = incoming + matmul_back(short[:, hidden:], merged(right_ref))
    gv, gain_sum, bias_sum = norm_gelu_back(
        incoming, v_ref[...], narrow_ref[4:5, :], narrow_ref[5:6, :]
    )
    gv = gv.astype(jnp.bfloat16)
    gv_ref[...] = gv
    narrow_sum_ref[0:1, :] += column_sum(gv.astype(jnp.float32))
    narrow_sum_ref[1:2, :] += gain_sum
    narrow_sum_ref[2:3, :] += bias_sum


def weight_grad_kernel(tap_ref, gv_ref, act_three_ref, short_ref, pack_ref):
    step = pl.program_id(0)

    def store(value):
        pack_ref[...] = value.astype(jnp.bfloat16).reshape(pack_ref.shape)

    @pl.when(step < KER)
    def _():
        store(matmul_rows(tap_ref[...], gv_ref[...]))

    @pl.when(step >= KER)
    def _():
        store(matmul_rows(act_three_ref[...], short_ref[...]))


def conv_back_kernel(
    dilation_step,
    low_ref,
    own_ref,
    high_ref,
    flag_ref,
    u_ref,
    x_ref,
    g_ref,
    k0_ref,
    k1_ref,
    k2_ref,
    k3_ref,
    k4_ref,
    w_ref,
    wide_ref,
    narrow_ref,
    gu_ref,
    next_ref,
    narrow_sum_ref,
    wide_sum_ref,
):
    @pl.when(pl.program_id(0) == 0)
    def _():
        narrow_sum_ref[...] = jnp.zeros_like(narrow_sum_ref)
        wide_sum_ref[...] = jnp.zeros_like(wide_sum_ref)

    taps = (k0_ref, k1_ref, k2_ref, k3_ref, k4_ref)
    total = None
    for k, piece in tap_slices(low_ref, own_ref, high_ref, flag_ref, dilation_step):
        term = matmul_back(piece, merged(taps[KER - 1 - k]))
        total = term if total is None else total + term
    gu, gain_sum, bias_sum = norm_gelu_back(
        total, u_ref[...], narrow_ref[1:2, :], narrow_ref[2:3, :]
    )
    gu = gu.astype(jnp.bfloat16)
    gu_ref[...] = gu
    narrow_sum_ref[0:1, :] += column_sum(gu.astype(jnp.float32))
    narrow_sum_ref[1:2, :] += gain_sum
    narrow_sum_ref[2:3, :] += bias_sum
    gx, gain_sum, bias_sum = norm_gelu_back(
        matmul_back(gu, merged(w_ref)),
        x_ref[...].astype(jnp.float32),
        wide_ref[0:1, :],
        wide_ref[1:2, :],
    )
    next_ref[...] = g_ref[...].astype(jnp.float32) + gx
    wide_sum_ref[0:1, :] += gain_sum
    wide_sum_ref[1:2, :] += bias_sum


def in_grad_kernel(pack_in_ref, act_one_ref, gu_ref, pack_ref):
    value = matmul_rows(act_one_ref[...], gu_ref[...])
    pack_ref[...] = value.astype(jnp.bfloat16).reshape(pack_ref.shape)


def tiled(rows, columns):
    return pl.BlockSpec((rows, columns), lambda i: (i, 0))


def fixed(*shape):
    return pl.BlockSpec(shape, lambda i: (0,) * len(shape))


def row_block(shape):
    return pl.BlockSpec((1,) + shape[1:], lambda i: (i, 0, 0))


def pack_block(parts, rows, columns, index):
    return pl.BlockSpec((parts, rows, columns), lambda i: (0, index, 0))


def cost(flops, width):
    return pl.CostEstimate(flops=flops, bytes_accessed=width, transcendentals=0)


def call(kernel, grid, in_specs, out_specs, out_shape, flops, moved, name, aliases=None):
    return pl.pallas_call(
        kernel,
        grid=(grid,),
        in_specs=in_specs,
        out_specs=out_specs,
        out_shape=out_shape,
        input_output_aliases=aliases or {},
        cost_estimate=cost(flops, moved),
        compiler_params=pltpu.CompilerParams(vmem_limit_bytes=48 * 1024 * 1024),
        name=name,
    )


def shape_of(shape, dtype):
    return jax.ShapeDtypeStruct(shape, dtype)


class Sizes:
    def __init__(self, pack, model, hidden):
        self.parts = pack.shape[0]
        self.model, self.hidden = model, hidden
        self.first_rows = model // self.parts
        self.middle_rows = hidden // self.parts
        self.folds = model // hidden
        self.conv_at = self.first_rows // self.middle_rows
        self.out_at = self.conv_at + KER

    def first(self):
        return pack_block(self.parts, self.first_rows, self.hidden, 0)

    def taps(self):
        return [
            pack_block(self.parts, self.middle_rows, self.hidden, self.conv_at + k)
            for k in range(KER)
        ]

    def last(self):
        return [
            pack_block(self.parts, self.middle_rows, self.hidden, self.out_at + i)
            for i in range(self.folds)
        ]


def project(inputs, weights):
    pack, wide, narrow = weights
    tokens, model = inputs.shape
    hidden = narrow.shape[1]
    sizes = Sizes(pack, model, hidden)
    tile = min(128, tokens)
    return call(
        project_kernel,
        tokens // tile,
        [tiled(tile, model), sizes.first(), fixed(3, model), fixed(6, hidden)],
        [tiled(tile, model), tiled(tile, hidden), tiled(tile, hidden)],
        [
            shape_of((tokens, model), jnp.bfloat16),
            shape_of((tokens, hidden), jnp.float32),
            shape_of((tokens, hidden), jnp.bfloat16),
        ],
        4 * tokens * model * hidden,
        12 * tokens * model,
        "project",
    )(inputs, pack, wide, narrow)


def convolve(act_two, flags, inputs, weights, dilation_step, next_dtype):
    pack, wide, narrow = weights
    rows, length, hidden = act_two.shape
    tokens, model = inputs.shape
    sizes = Sizes(pack, model, hidden)
    low, high = seq_neighbours(act_two, KER // 2 * dilation_step)
    return call(
        functools.partial(convolve_kernel, dilation_step),
        rows,
        [
            row_block(low.shape),
            row_block(act_two.shape),
            row_block(high.shape),
            row_block(flags.shape),
            tiled(length, model),
            *sizes.taps(),
            *sizes.last(),
            fixed(3, model),
            fixed(6, hidden),
        ],
        [
            tiled(length, KER * hidden),
            tiled(length, hidden),
            tiled(length, hidden),
            tiled(length, model),
        ],
        [
            shape_of((tokens, KER * hidden), jnp.bfloat16),
            shape_of((tokens, hidden), jnp.float32),
            shape_of((tokens, hidden), jnp.bfloat16),
            shape_of((tokens, model), next_dtype),
        ],
        2 * tokens * hidden * (KER * hidden + model),
        16 * tokens * model,
        "convolve",
    )(low, act_two, high, flags, inputs, *([pack] * (KER + 2)), wide, narrow)


def out_back(upstream, conv_out, weights):
    pack, wide, narrow = weights
    tokens, model = upstream.shape
    hidden = narrow.shape[1]
    sizes = Sizes(pack, model, hidden)
    tile = min(128, tokens)
    return call(
        out_back_kernel,
        tokens // tile,
        [tiled(tile, model), tiled(tile, hidden), *sizes.last(), fixed(6, hidden)],
        [tiled(tile, model), tiled(tile, hidden), fixed(8, hidden), fixed(8, model)],
        [
            shape_of((tokens, model), jnp.bfloat16),
            shape_of((tokens, hidden), jnp.bfloat16),
            shape_of((8, hidden), jnp.float32),
            shape_of((8, model), jnp.float32),
        ],
        4 * tokens * model * hidden,
        10 * tokens * model,
        "out_back",
    )(upstream, conv_out, pack, pack, narrow)


def weight_grads(tap_rows, gv, act_three, short, pack):
    tokens, hidden = gv.shape
    model = short.shape[1]
    sizes = Sizes(pack, model, hidden)
    whole = pl.BlockSpec((tokens, hidden), lambda s: (0, 0))
    return call(
        weight_grad_kernel,
        KER + sizes.folds,
        [
            pl.BlockSpec((tokens, hidden), lambda s: (0, jnp.minimum(s, KER - 1))),
            whole,
            whole,
            pl.BlockSpec((tokens, hidden), lambda s: (0, jnp.maximum(s - KER, 0))),
        ],
        pl.BlockSpec(
            (sizes.parts, sizes.middle_rows, hidden), lambda s: (0, sizes.conv_at + s, 0)
        ),
        shape_of(pack.shape, jnp.bfloat16),
        2 * tokens * hidden * (KER * hidden + model),
        8 * tokens * model,
        "weight_grads",
    )(tap_rows, gv, act_three, short)


def conv_back(gv, flags, u, inputs, upstream, weights, dilation_step):
    pack, wide, narrow = weights
    rows, length, hidden = gv.shape
    tokens, model = inputs.shape
    sizes = Sizes(pack, model, hidden)
    low, high = seq_neighbours(gv, KER // 2 * dilation_step)
    return call(
        functools.partial(conv_back_kernel, dilation_step),
        rows,
        [
            row_block(low.shape),
            row_block(gv.shape),
            row_block(high.shape),
            row_block(flags.shape),
            tiled(length, hidden),
            tiled(length, model),
            tiled(length, model),
            *sizes.taps(),
            sizes.first(),
            fixed(3, model),
            fixed(6, hidden),
        ],
        [tiled(length, hidden), tiled(length, model), fixed(8, hidden), fixed(8, model)],
        [
            shape_of((tokens, hidden), jnp.bfloat16),
            shape_of((tokens, model), jnp.float32),
            shape_of((8, hidden), jnp.float32),
            shape_of((8, model), jnp.float32),
        ],
        2 * tokens * hidden * (KER * hidden + model),
        16 * tokens * model,
        "conv_back",
    )(low, gv, high, flags, u, inputs, upstream, *([pack] * (KER + 1)), wide, narrow)


def in_grads(grad_pack, act_one, gu):
    tokens, model = act_one.shape
    hidden = gu.shape[1]
    sizes = Sizes(grad_pack, model, hidden)
    return call(
        in_grad_kernel,
        1,
        [pl.BlockSpec(memory_space=pl.ANY), fixed(tokens, model), fixed(tokens, hidden)],
        sizes.first(),
        shape_of(grad_pack.shape, jnp.bfloat16),
        2 * tokens * hidden * model,
        4 * tokens * model,
        "in_grads",
        {0: 0},
    )(grad_pack, act_one, gu)


def shifted(block, step):
    count = lax.axis_size("seq")
    return lax.ppermute(block, "seq", [(i, (i + step) % count) for i in range(count)])


def weight_pack(block_number, device_shards):
    w_in, w_conv, w_out = (device_shards[i][block_number] for i in (2, 6, 10))
    width = w_in.shape[1]
    folds = w_out.shape[1] // width
    pieces = [w_in, w_conv.reshape(-1, width)]
    pieces += [w_out[:, i * width : (i + 1) * width] for i in range(folds)]
    return jnp.concatenate(pieces, axis=0)


def vector_pack(block_number, device_shards, width):
    order = (0, 1, 11, 3, 4, 5, 7, 8, 9)
    rows = [device_shards[i][block_number] for i in order]
    rows = [jnp.pad(row, (0, width - row.shape[0])) for row in rows]
    return jnp.pad(jnp.stack(rows), ((0, VECTOR_ROWS - len(rows)), (0, 0)))


def seq_gathered(packed):
    count = lax.axis_size("seq")
    me = lax.axis_index("seq")
    held = [packed] + [shifted(packed, step) for step in range(1, count)]
    ring = jnp.stack(held[::-1] + held[::-1])
    return lax.dynamic_slice_in_dim(ring, (count - 1 - me) % count, count, axis=0)


def folded_columns(out_parts):
    count, folds, depth, width = out_parts.shape
    per_fold = count // folds
    return (
        out_parts.reshape(folds, per_fold, folds, depth, width)
        .transpose(0, 3, 1, 2, 4)
        .reshape(folds * depth, per_fold * folds * width)
    )


def unfolded_columns(out_rows, folds, count):
    per_fold = count // folds
    depth = out_rows.shape[0] // folds
    width = out_rows.shape[1] // count
    return (
        out_rows.reshape(folds, depth, per_fold, folds, width)
        .transpose(0, 2, 3, 1, 4)
        .reshape(count, folds * depth, width)
    )


def pack_is_aligned(middle_rows):
    return middle_rows % 16 == 0


def gathered_params(block_number, device_shards, after=None):
    w_in, w_conv, w_out = (device_shards[i][block_number] for i in (2, 6, 10))
    first_rows = w_in.shape[0]
    taps, middle_rows, width = w_conv.shape
    folds = w_out.shape[1] // width
    count = lax.axis_size("seq")
    hidden = width * count
    by_seq = seq_gathered(weight_pack(block_number, device_shards))
    straight = first_rows + taps * middle_rows
    total = straight + folds * middle_rows
    upper = by_seq[:, :straight].transpose(1, 0, 2).reshape(straight, hidden)
    lower = folded_columns(by_seq[:, straight:].reshape(count, folds, middle_rows, width))
    vectors = vector_pack(block_number, device_shards, hidden)
    packed = jnp.concatenate([upper, lower, vectors])
    if after is not None:
        packed, after = lax.optimization_barrier((packed, after))
    whole = lax.all_gather(packed, "dp")
    tail = whole[:, total:].astype(jnp.float32)
    wide = tail[:, :3, :first_rows].transpose(1, 0, 2).reshape(3, -1)
    narrow = tail[:, 3:9, :middle_rows].transpose(1, 0, 2).reshape(6, -1)
    if not pack_is_aligned(middle_rows):
        bounds = [0, first_rows]
        bounds += [first_rows + (k + 1) * middle_rows for k in range(taps + folds)]
        whole = jnp.concatenate(
            [whole[:, a:b].reshape(1, -1, hidden) for a, b in zip(bounds, bounds[1:])], axis=1
        )
    return (whole, wide, narrow)


def reduce_dp(grad_pack, wide_grads, narrow_grads):
    parts = lax.axis_size("dp")
    hidden = narrow_grads.shape[1]
    model = wide_grads.shape[1]
    first_rows = model // parts
    middle_rows = hidden // parts
    folds = model // hidden
    total = first_rows + (KER + folds) * middle_rows
    if not pack_is_aligned(middle_rows):
        bounds = [0, model] + [model + (k + 1) * hidden for k in range(KER + folds)]
        grad_pack = jnp.concatenate(
            [grad_pack[0, a:b].reshape(parts, -1, hidden) for a, b in zip(bounds, bounds[1:])]
            + [jnp.zeros((parts, VECTOR_ROWS, hidden), jnp.bfloat16)],
            axis=1,
        )
    vectors = jnp.concatenate(
        [
            jnp.pad(
                block.reshape(-1, parts, rows).transpose(1, 0, 2),
                ((0, 0), (0, 0), (0, hidden - rows)),
            )
            for block, rows in ((wide_grads, first_rows), (narrow_grads, middle_rows))
        ]
        + [jnp.zeros((parts, VECTOR_ROWS - 9, hidden), jnp.float32)],
        axis=1,
    ).astype(jnp.bfloat16)
    grad_pack = lax.dynamic_update_slice(grad_pack, vectors, (0, total, 0))
    return lax.psum_scatter(grad_pack, "dp", scatter_dimension=0, tiled=False)


def reduce_seq(mine, model, hidden):
    parts = lax.axis_size("dp")
    count = lax.axis_size("seq")
    me = lax.axis_index("seq")
    first_rows = model // parts
    middle_rows = hidden // parts
    width = hidden // count
    folds = model // hidden
    straight = first_rows + KER * middle_rows
    total = straight + folds * middle_rows
    upper = mine[:straight].reshape(straight, count, width).transpose(1, 0, 2)
    lower = unfolded_columns(mine[straight:total], folds, count)
    fold = -(-first_rows // width)
    tail = mine[total:, : fold * width].reshape(1, VECTOR_ROWS * fold, width)
    tail = jnp.broadcast_to(tail, (count,) + tail.shape[1:])
    ring = jnp.concatenate([upper, lower, tail], axis=1)
    ring = jnp.concatenate([ring, ring])
    ring = lax.dynamic_slice_in_dim(ring, me, count, axis=0)
    held = [ring[0]] + [shifted(ring[step], step) for step in range(1, count)]
    held = [block.astype(jnp.float32) for block in held]
    while len(held) > 1:
        half = len(held) // 2
        held = [held[i] + held[i + half] for i in range(half)]
    summed = held[0]
    last = summed[straight:total].reshape(folds, middle_rows, width).transpose(1, 0, 2)
    tail = summed[total:].reshape(VECTOR_ROWS, fold * width)
    return (
        summed[:first_rows],
        summed[first_rows:straight].reshape(KER, middle_rows, width),
        last.reshape(middle_rows, folds * width),
        tail[:3, :first_rows],
        tail[3:9, :middle_rows],
    )


def block_forward(inputs, weights, flags, dilation_step, next_dtype):
    rows, length, _ = flags.shape
    act_one, u, act_two = project(inputs, weights)
    tap_rows, conv_out, act_three, output = convolve(
        act_two.reshape(rows, length, -1), flags, inputs, weights, dilation_step, next_dtype
    )
    return output, (act_one, u, tap_rows, conv_out, act_three)


def block_backward(inputs, upstream, weights, kept, flags, dilation_step, before=None):
    act_one, u, tap_rows, conv_out, act_three = kept
    rows, length, _ = flags.shape
    short, gv, narrow_a, wide_a = out_back(upstream, conv_out, weights)
    pack = weights[0]
    grad_shape = shape_of(
        (pack.shape[0], sum(pack_rows(pack, inputs.shape[1], gv.shape[1])), gv.shape[1]),
        jnp.bfloat16,
    )
    grad_pack = weight_grads(tap_rows, gv, act_three, short, grad_shape)
    gu, result, narrow_b, wide_b = conv_back(
        gv.reshape(rows, length, -1), flags, u, inputs, upstream, weights, dilation_step
    )
    if before is not None:
        gu, before = lax.optimization_barrier((gu, before))
    grad_pack = in_grads(grad_pack, act_one, gu)
    wide = jnp.concatenate([wide_b[0:2], wide_a[0:1]])
    narrow = jnp.concatenate([narrow_b[0:3], narrow_a[0:3]])
    return result, reduce_dp(grad_pack, wide, narrow), before


def pack_rows(pack, model, hidden):
    parts = pack.shape[0]
    extra = VECTOR_ROWS if pack_is_aligned(hidden // lax.axis_size("dp")) else 0
    return model // parts, (KER * hidden + model) // parts, extra


def local(
    tokens,
    protein_lengths,
    norm1_gain,
    norm1_bias,
    w_in,
    in_bias,
    norm2_gain,
    norm2_bias,
    w_conv,
    conv_bias,
    norm3_gain,
    norm3_bias,
    w_out,
    out_bias,
    cotangent,
):
    device_shards = (
        norm1_gain,
        norm1_bias,
        w_in,
        in_bias,
        norm2_gain,
        norm2_bias,
        w_conv,
        conv_bias,
        norm3_gain,
        norm3_bias,
        w_out,
        out_bias,
    )
    rows, seq_len, model = tokens.shape
    token_positions = lax.axis_index("seq") * seq_len + jnp.arange(seq_len, dtype=jnp.int32)
    early_flags = kernel_tap_flags(protein_lengths, token_positions, FIRST_DILATION)
    later_flags = kernel_tap_flags(protein_lengths, token_positions, SECOND_DILATION)
    early_weights = gathered_params(0, device_shards)
    late_weights = gathered_params(1, device_shards, early_weights[0])
    flat_tokens = tokens.reshape(rows * seq_len, model)
    middle, early_kept = block_forward(
        flat_tokens, early_weights, early_flags, FIRST_DILATION, jnp.float32
    )
    middle, late_weights = lax.optimization_barrier((middle, late_weights))
    output, late_kept = block_forward(
        middle, late_weights, later_flags, SECOND_DILATION, jnp.bfloat16
    )
    middle_grad, mine_late, _ = block_backward(
        middle,
        cotangent.reshape(rows * seq_len, model),
        late_weights,
        late_kept,
        later_flags,
        SECOND_DILATION,
    )
    input_grad, mine_early, mine_late = block_backward(
        flat_tokens,
        middle_grad,
        early_weights,
        early_kept,
        early_flags,
        FIRST_DILATION,
        mine_late,
    )
    hidden = early_weights[2].shape[1]
    reduced_late = reduce_seq(mine_late, model, hidden)
    reduced_early = reduce_seq(mine_early, model, hidden)
    first_early, middle_early, last_early, wide_early, narrow_early = reduced_early
    first_late, middle_late, last_late, wide_late, narrow_late = reduced_late
    return (
        output.reshape(tokens.shape),
        input_grad.reshape(tokens.shape),
        jnp.stack([wide_early[0], wide_late[0]]),
        jnp.stack([wide_early[1], wide_late[1]]),
        jnp.stack([first_early, first_late]),
        jnp.stack([narrow_early[0], narrow_late[0]]),
        jnp.stack([narrow_early[1], narrow_late[1]]),
        jnp.stack([narrow_early[2], narrow_late[2]]),
        jnp.stack([middle_early, middle_late]),
        jnp.stack([narrow_early[3], narrow_late[3]]),
        jnp.stack([narrow_early[4], narrow_late[4]]),
        jnp.stack([narrow_early[5], narrow_late[5]]),
        jnp.stack([last_early, last_late]),
        jnp.stack([wide_early[2], wide_late[2]]),
    )


def solution(mesh):
    placed = (
        P("dp", "seq", None),
        P("dp", None),
        P(None, "dp"),
        P(None, "dp"),
        P(None, "dp", "seq"),
        P(None, "dp"),
        P(None, "dp"),
        P(None, "dp"),
        P(None, None, "dp", "seq"),
        P(None, "dp"),
        P(None, "dp"),
        P(None, "dp"),
        P(None, "dp", "seq"),
        P(None, "dp"),
        P("dp", "seq", None),
    )
    return jax.shard_map(
        local,
        mesh=mesh,
        in_specs=placed,
        out_specs=(
            P("dp", "seq", None),
            P("dp", "seq", None),
            P(None, "dp"),
            P(None, "dp"),
            P(None, "dp", "seq"),
            P(None, "dp"),
            P(None, "dp"),
            P(None, "dp"),
            P(None, None, "dp", "seq"),
            P(None, "dp"),
            P(None, "dp"),
            P(None, "dp"),
            P(None, "dp", "seq"),
            P(None, "dp"),
        ),
        check_vma=False,
    )
```

```python
import functools
import math

import jax
import jax.numpy as jnp
from jax import lax
from jax.experimental import pallas as pl
from jax.experimental.pallas import tpu as pltpu
from jax.sharding import PartitionSpec as P

KER = 5
FIRST_DILATION = 64
SECOND_DILATION = 128


epsilon = 1e-05
CUBIC = 0.044715
SLOPE = math.sqrt(2.0 / math.pi)
VECTOR_ROWS = 16


def seq_neighbours(block, width):
    count = lax.axis_size("seq")
    forward = [(i, i + 1) for i in range(count - 1)]
    backward = [(target, source) for source, target in forward]
    low = lax.ppermute(block[:, block.shape[1] - width :], "seq", forward)
    high = lax.ppermute(block[:, :width], "seq", backward)
    return low, high


def normalized(values):
    centred = values - jnp.mean(values, -1, keepdims=True)
    scale = lax.rsqrt(jnp.mean(centred * centred, -1, keepdims=True) + epsilon)
    return centred * scale, scale


def gelu(h):
    return 0.5 * h * (1.0 + jnp.tanh(SLOPE * (h + CUBIC * (h * h * h))))


def norm_gelu(values, gain_vector, bias_vector):
    return gelu(normalized(values)[0] * gain_vector + bias_vector)


def norm_gelu_back(incoming, values, gain_vector, bias_vector):
    n, scale = normalized(values)
    h = n * gain_vector + bias_vector
    square = h * h
    t = jnp.tanh(SLOPE * (h + CUBIC * (square * h)))
    slope = 0.5 * (1.0 + t) + (0.5 * SLOPE) * h * (1.0 - t * t) * (1.0 + (3.0 * CUBIC) * square)
    dh = incoming * slope
    dn = dh * gain_vector
    back = dn - jnp.mean(dn, -1, keepdims=True) - n * jnp.mean(dn * n, -1, keepdims=True)
    return back * scale, column_sum(dh * n), column_sum(dh)


def column_sum(values):
    return jnp.sum(values, axis=0, keepdims=True)


def matmul(left, right):
    return jnp.dot(left, right, preferred_element_type=jnp.float32)


def matmul_back(left, right):
    return lax.dot_general(
        left, right, (((1,), (1,)), ((), ())), preferred_element_type=jnp.float32
    )


def matmul_rows(left, right):
    return lax.dot_general(
        left, right, (((0,), (0,)), ((), ())), preferred_element_type=jnp.float32
    )


def merged(ref):
    parts, rows, columns = ref.shape
    return ref[...].reshape(parts * rows, columns)


def kernel_tap_flags(lengths, token_positions, dilation_step):
    doc_ends = jnp.cumsum(lengths, axis=1)
    row_total = doc_ends[:, -1:]
    where_pos = token_positions[None, :, None]
    finished = doc_ends[:, None, :] <= where_pos
    doc_start = jnp.sum(jnp.where(finished, lengths[:, None, :], 0), axis=2)
    doc_stop = jnp.min(jnp.where(finished, row_total[:, :, None] + 1, doc_ends[:, None, :]), axis=2)
    is_live = token_positions[None, :] < row_total
    flag_list = []
    for tap_index in range(KER):
        target = token_positions[None, :] + (tap_index - KER // 2) * dilation_step
        flag_list.append(is_live & (target >= doc_start) & (target < doc_stop))
    flag_list += [flag_list[-1]] * (8 - KER)
    return jnp.stack(flag_list, axis=2).astype(jnp.bfloat16)


def project_kernel(x_ref, w_ref, wide_ref, narrow_ref, act_one_ref, u_ref, act_two_ref):
    act_one = norm_gelu(
        x_ref[...].astype(jnp.float32), wide_ref[0:1, :], wide_ref[1:2, :]
    ).astype(jnp.bfloat16)
    act_one_ref[...] = act_one
    u = matmul(act_one, merged(w_ref)) + narrow_ref[0:1, :]
    u_ref[...] = u
    act_two_ref[...] = norm_gelu(u, narrow_ref[1:2, :], narrow_ref[2:3, :]).astype(jnp.bfloat16)


def tap_slices(low_ref, own_ref, high_ref, flag_ref, dilation_step):
    length = own_ref.shape[1]
    width = low_ref.shape[1]
    padded = jnp.concatenate([low_ref[0], own_ref[0], high_ref[0]], axis=0)
    for k in range(KER):
        start = width + (k - KER // 2) * dilation_step
        yield k, padded[start : start + length] * flag_ref[0][:, k : k + 1]


def convolve_kernel(
    dilation_step,
    low_ref,
    own_ref,
    high_ref,
    flag_ref,
    x_ref,
    k0_ref,
    k1_ref,
    k2_ref,
    k3_ref,
    k4_ref,
    left_ref,
    right_ref,
    wide_ref,
    narrow_ref,
    tap_ref,
    v_ref,
    act_three_ref,
    next_ref,
):
    taps = (k0_ref, k1_ref, k2_ref, k3_ref, k4_ref)
    hidden = own_ref.shape[2]
    total = narrow_ref[3:4, :]
    for k, piece in tap_slices(low_ref, own_ref, high_ref, flag_ref, dilation_step):
        tap_ref[:, k * hidden : (k + 1) * hidden] = piece
        total = total + matmul(piece, merged(taps[k]))
    v_ref[...] = total
    act_three = norm_gelu(total, narrow_ref[4:5, :], narrow_ref[5:6, :]).astype(jnp.bfloat16)
    act_three_ref[...] = act_three
    for i, half_ref in enumerate((left_ref, right_ref)):
        columns = slice(i * hidden, (i + 1) * hidden)
        branch = matmul(act_three, merged(half_ref)) + wide_ref[2:3, columns]
        next_ref[:, columns] = (x_ref[:, columns].astype(jnp.float32) + branch).astype(
            next_ref.dtype
        )


def out_back_kernel(
    g_ref, v_ref, left_ref, right_ref, narrow_ref, short_ref, gv_ref, narrow_sum_ref, wide_sum_ref
):
    hidden = v_ref.shape[1]

    @pl.when(pl.program_id(0) == 0)
    def _():
        narrow_sum_ref[...] = jnp.zeros_like(narrow_sum_ref)
        wide_sum_ref[...] = jnp.zeros_like(wide_sum_ref)

    short = g_ref[...].astype(jnp.bfloat16)
    short_ref[...] = short
    wide_sum_ref[0:1, :] += column_sum(short.astype(jnp.float32))
    incoming = matmul_back(short[:, :hidden], merged(left_ref))
    incoming = incoming + matmul_back(short[:, hidden:], merged(right_ref))
    gv, gain_sum, bias_sum = norm_gelu_back(
        incoming, v_ref[...], narrow_ref[4:5, :], narrow_ref[5:6, :]
    )
    gv = gv.astype(jnp.bfloat16)
    gv_ref[...] = gv
    narrow_sum_ref[0:1, :] += column_sum(gv.astype(jnp.float32))
    narrow_sum_ref[1:2, :] += gain_sum
    narrow_sum_ref[2:3, :] += bias_sum


def weight_grad_kernel(tap_ref, gv_ref, act_three_ref, short_ref, pack_ref):
    step = pl.program_id(0)

    def store(value):
        pack_ref[...] = value.astype(jnp.bfloat16).reshape(pack_ref.shape)

    @pl.when(step < KER)
    def _():
        store(matmul_rows(tap_ref[...], gv_ref[...]))

    @pl.when(step >= KER)
    def _():
        store(matmul_rows(act_three_ref[...], short_ref[...]))


def conv_back_kernel(
    dilation_step,
    low_ref,
    own_ref,
    high_ref,
    flag_ref,
    u_ref,
    x_ref,
    g_ref,
    k0_ref,
    k1_ref,
    k2_ref,
    k3_ref,
    k4_ref,
    w_ref,
    wide_ref,
    narrow_ref,
    gu_ref,
    next_ref,
    narrow_sum_ref,
    wide_sum_ref,
):
    @pl.when(pl.program_id(0) == 0)
    def _():
        narrow_sum_ref[...] = jnp.zeros_like(narrow_sum_ref)
        wide_sum_ref[...] = jnp.zeros_like(wide_sum_ref)

    taps = (k0_ref, k1_ref, k2_ref, k3_ref, k4_ref)
    total = None
    for k, piece in tap_slices(low_ref, own_ref, high_ref, flag_ref, dilation_step):
        term = matmul_back(piece, merged(taps[KER - 1 - k]))
        total = term if total is None else total + term
    gu, gain_sum, bias_sum = norm_gelu_back(
        total, u_ref[...], narrow_ref[1:2, :], narrow_ref[2:3, :]
    )
    gu = gu.astype(jnp.bfloat16)
    gu_ref[...] = gu
    narrow_sum_ref[0:1, :] += column_sum(gu.astype(jnp.float32))
    narrow_sum_ref[1:2, :] += gain_sum
    narrow_sum_ref[2:3, :] += bias_sum
    gx, gain_sum, bias_sum = norm_gelu_back(
        matmul_back(gu, merged(w_ref)),
        x_ref[...].astype(jnp.float32),
        wide_ref[0:1, :],
        wide_ref[1:2, :],
    )
    next_ref[...] = g_ref[...].astype(jnp.float32) + gx
    wide_sum_ref[0:1, :] += gain_sum
    wide_sum_ref[1:2, :] += bias_sum


def in_grad_kernel(pack_in_ref, act_one_ref, gu_ref, pack_ref):
    value = matmul_rows(act_one_ref[...], gu_ref[...])
    pack_ref[...] = value.astype(jnp.bfloat16).reshape(pack_ref.shape)


def spread(rows, place_ref, hold_ref, own_ref, other_ref):
    chip, core = place_ref[0] // 2, place_ref[0] % 2
    for i in range(own_ref.shape[0]):
        at = 2 * (chip ^ i)
        own_ref[i] = hold_ref[at + core, rows]
        other_ref[i] = hold_ref[at + 1 - core, rows]


def share_grad_kernel(
    place_ref, tap_ref, gv_ref, act_three_ref, short_ref, own_ref, other_ref, hold_ref
):
    step = pl.program_id(0)

    def store(value):
        hold_ref[...] = value.astype(jnp.bfloat16).reshape(hold_ref.shape)

    @pl.when(step < KER)
    def _():
        store(matmul_rows(tap_ref[...], gv_ref[...]))

    @pl.when(step >= KER)
    def _():
        store(matmul_rows(act_three_ref[...], short_ref[...]))

    spread(slice(None), place_ref, hold_ref, own_ref, other_ref)


def share_in_kernel(place_ref, act_one_ref, gu_ref, *refs):
    *sum_refs, own_ref, other_ref, hold_ref = refs
    parts = hold_ref.shape[0]
    hidden = gu_ref.shape[1]
    depth = act_one_ref.shape[1] // parts
    value = matmul_rows(act_one_ref[...], gu_ref[...]).astype(jnp.bfloat16)
    hold_ref[:, :depth, :] = value.reshape(parts, depth, hidden)
    for block in range(len(sum_refs) // 4):
        narrow_a, wide_a, narrow_b, wide_b = (ref[...] for ref in sum_refs[4 * block : 4 * block + 4])
        wide = jnp.concatenate([wide_b[0:2], wide_a[0:1]], axis=0)
        narrow = jnp.concatenate([narrow_b[0:3], narrow_a[0:3]], axis=0)
        narrow_depth = hidden // parts
        for part in range(parts):
            rows = [
                wide[:, part * depth : (part + 1) * depth],
                jnp.concatenate(
                    [
                        narrow[:, part * narrow_depth : (part + 1) * narrow_depth],
                        jnp.zeros((6, depth - narrow_depth), jnp.float32),
                    ],
                    axis=1,
                ),
                jnp.zeros((VECTOR_ROWS - 9, depth), jnp.float32),
            ]
            rows = jnp.concatenate(rows, axis=0)
            rows = jnp.concatenate(
                [rows, jnp.zeros((VECTOR_ROWS, hidden - depth), jnp.float32)], axis=1
            )
            start = depth + block * VECTOR_ROWS
            hold_ref[part, start : start + VECTOR_ROWS, :] = rows.astype(jnp.bfloat16)
    spread(slice(None), place_ref, hold_ref, own_ref, other_ref)


def plus(left, right):
    return left.astype(jnp.float32) + right.astype(jnp.float32)


def first_sum_kernel(cut, count, *refs):
    step = pl.program_id(0)
    keep_a, send_a, keep_b, send_b = refs[2 * count :]
    pieces = [
        plus(own[0], got[0]).astype(jnp.bfloat16) for own, got in zip(refs[:count], refs[count:])
    ]
    total = pieces[0] if count == 1 else jnp.concatenate(pieces, axis=0)
    upper, lower = total[:cut], total[cut:]

    @pl.when(step % 2 == 0)
    def _():
        keep_a[0] = upper

    @pl.when(step % 2 == 1)
    def _():
        send_a[0] = upper

    @pl.when(step < 2)
    def _():
        keep_b[0] = lower

    @pl.when(step >= 2)
    def _():
        send_b[0] = lower


def second_sum_kernel(keep_a, got_a, keep_b, got_b, kept_a, send_a, kept_b, send_b):
    for keep, got, kept, send in (
        (keep_a, got_a, kept_a, send_a),
        (keep_b, got_b, kept_b, send_b),
    ):
        kept[...] = plus(keep[0], got[0]).astype(jnp.bfloat16)
        send[...] = plus(keep[1], got[1]).astype(jnp.bfloat16)


def seq_split_kernel(folded_rows, vector_rows, place_ref, *refs):
    *in_refs, out_ref = refs
    if len(in_refs) == 1:
        total = in_refs[0][...]
    else:
        halves = [plus(in_refs[i][...], in_refs[i + 1][...]) for i in range(0, len(in_refs), 2)]
        total = jnp.concatenate(halves, axis=0)
    total = total.astype(jnp.float32)
    count, rows, width = out_ref.shape
    at, end = folded_rows
    fold = (end - at) // 2
    for s in range(count):
        columns = total[:, s * width : (s + 1) * width]
        if end > at:
            unit = at + (s // 2) * fold
            left = (s % 2) * 2 * width
            pair = total[unit : unit + fold, left : left + 2 * width]
            pieces = [columns[:at], pair[:, :width], pair[:, width:], columns[end:]]
            columns = jnp.concatenate([p for p in pieces if p.shape[0]], axis=0)
        if vector_rows:
            columns = jnp.concatenate(
                [columns[: rows - vector_rows], total[rows - vector_rows :, :width]], axis=0
            )
        out_ref[(s - place_ref[1] + count) % count] = columns.astype(jnp.bfloat16)


def last_sum_kernel(layout, *refs):
    sums = {}
    at = 0
    for name, count in layout:
        own, one, two, three = (ref[...].astype(jnp.float32) for ref in refs[at : at + 4])
        at += 4
        sums[name] = (own + two) + (one + three)
    first_ref, taps_ref, last_ref = refs[at : at + 3]
    vector_refs = refs[at + 3 :]
    depth = taps_ref.shape[2]
    straight = KER * depth
    first_rows = first_ref.shape[1]
    for block, piece in ((0, sums["early"]), (1, sums["late"])):
        for k in range(KER):
            taps_ref[block, k] = piece[k * depth : (k + 1) * depth]
        last_ref[block] = jnp.concatenate(
            [piece[straight : straight + depth], piece[straight + depth : straight + 2 * depth]],
            axis=1,
        )
    rest = sums["early"][straight + 2 * depth :]
    first_ref[0] = rest[first_rows : 2 * first_rows]
    first_ref[1] = rest[:first_rows]
    for block in range(2):
        start = 2 * first_rows + block * VECTOR_ROWS
        for i, ref in enumerate(vector_refs):
            row = rest[start + i : start + i + 1]
            ref[block : block + 1, :] = row[:, : ref.shape[1]]


def tiled(rows, columns):
    return pl.BlockSpec((rows, columns), lambda i: (i, 0))


def fixed(*shape):
    return pl.BlockSpec(shape, lambda i: (0,) * len(shape))


def row_block(shape):
    return pl.BlockSpec((1,) + shape[1:], lambda i: (i, 0, 0))


def pack_block(parts, rows, columns, index):
    return pl.BlockSpec((parts, rows, columns), lambda i: (0, index, 0))


def cost(flops, width):
    return pl.CostEstimate(flops=flops, bytes_accessed=width, transcendentals=0)


def call(kernel, grid, in_specs, out_specs, out_shape, flops, moved, name, aliases=None, scratch=()):
    return pl.pallas_call(
        kernel,
        grid=(grid,),
        in_specs=in_specs,
        out_specs=out_specs,
        out_shape=out_shape,
        scratch_shapes=list(scratch),
        input_output_aliases=aliases or {},
        cost_estimate=cost(flops, moved),
        compiler_params=pltpu.CompilerParams(vmem_limit_bytes=48 * 1024 * 1024),
        name=name,
    )


def shape_of(shape, dtype):
    return jax.ShapeDtypeStruct(shape, dtype)


class Sizes:
    def __init__(self, pack, model, hidden):
        self.parts = pack.shape[0]
        self.model, self.hidden = model, hidden
        self.first_rows = model // self.parts
        self.middle_rows = hidden // self.parts
        self.folds = model // hidden
        self.conv_at = self.first_rows // self.middle_rows
        self.out_at = self.conv_at + KER

    def first(self):
        return pack_block(self.parts, self.first_rows, self.hidden, 0)

    def taps(self):
        return [
            pack_block(self.parts, self.middle_rows, self.hidden, self.conv_at + k)
            for k in range(KER)
        ]

    def last(self):
        return [
            pack_block(self.parts, self.middle_rows, self.hidden, self.out_at + i)
            for i in range(self.folds)
        ]


def project(inputs, weights):
    pack, wide, narrow = weights
    tokens, model = inputs.shape
    hidden = narrow.shape[1]
    sizes = Sizes(pack, model, hidden)
    tile = min(128, tokens)
    return call(
        project_kernel,
        tokens // tile,
        [tiled(tile, model), sizes.first(), fixed(3, model), fixed(6, hidden)],
        [tiled(tile, model), tiled(tile, hidden), tiled(tile, hidden)],
        [
            shape_of((tokens, model), jnp.bfloat16),
            shape_of((tokens, hidden), jnp.float32),
            shape_of((tokens, hidden), jnp.bfloat16),
        ],
        4 * tokens * model * hidden,
        12 * tokens * model,
        "project",
    )(inputs, pack, wide, narrow)


def convolve(act_two, flags, inputs, weights, dilation_step, next_dtype):
    pack, wide, narrow = weights
    rows, length, hidden = act_two.shape
    tokens, model = inputs.shape
    sizes = Sizes(pack, model, hidden)
    low, high = seq_neighbours(act_two, KER // 2 * dilation_step)
    return call(
        functools.partial(convolve_kernel, dilation_step),
        rows,
        [
            row_block(low.shape),
            row_block(act_two.shape),
            row_block(high.shape),
            row_block(flags.shape),
            tiled(length, model),
            *sizes.taps(),
            *sizes.last(),
            fixed(3, model),
            fixed(6, hidden),
        ],
        [
            tiled(length, KER * hidden),
            tiled(length, hidden),
            tiled(length, hidden),
            tiled(length, model),
        ],
        [
            shape_of((tokens, KER * hidden), jnp.bfloat16),
            shape_of((tokens, hidden), jnp.float32),
            shape_of((tokens, hidden), jnp.bfloat16),
            shape_of((tokens, model), next_dtype),
        ],
        2 * tokens * hidden * (KER * hidden + model),
        16 * tokens * model,
        "convolve",
    )(low, act_two, high, flags, inputs, *([pack] * (KER + 2)), wide, narrow)


def out_back(upstream, conv_out, weights):
    pack, wide, narrow = weights
    tokens, model = upstream.shape
    hidden = narrow.shape[1]
    sizes = Sizes(pack, model, hidden)
    tile = min(128, tokens)
    return call(
        out_back_kernel,
        tokens // tile,
        [tiled(tile, model), tiled(tile, hidden), *sizes.last(), fixed(6, hidden)],
        [tiled(tile, model), tiled(tile, hidden), fixed(8, hidden), fixed(8, model)],
        [
            shape_of((tokens, model), jnp.bfloat16),
            shape_of((tokens, hidden), jnp.bfloat16),
            shape_of((8, hidden), jnp.float32),
            shape_of((8, model), jnp.float32),
        ],
        4 * tokens * model * hidden,
        10 * tokens * model,
        "out_back",
    )(upstream, conv_out, pack, pack, narrow)


def weight_grads(tap_rows, gv, act_three, short, pack, conv_at=None):
    tokens, hidden = gv.shape
    model = short.shape[1]
    sizes = Sizes(pack, model, hidden)
    conv_at = sizes.conv_at if conv_at is None else conv_at
    whole = pl.BlockSpec((tokens, hidden), lambda s: (0, 0))
    return call(
        weight_grad_kernel,
        KER + sizes.folds,
        [
            pl.BlockSpec((tokens, hidden), lambda s: (0, jnp.minimum(s, KER - 1))),
            whole,
            whole,
            pl.BlockSpec((tokens, hidden), lambda s: (0, jnp.maximum(s - KER, 0))),
        ],
        pl.BlockSpec(
            (sizes.parts, sizes.middle_rows, hidden), lambda s: (0, conv_at + s, 0)
        ),
        shape_of(pack.shape, jnp.bfloat16),
        2 * tokens * hidden * (KER * hidden + model),
        8 * tokens * model,
        "weight_grads",
    )(tap_rows, gv, act_three, short)


def conv_back(gv, flags, u, inputs, upstream, weights, dilation_step):
    low, high = seq_neighbours(gv, KER // 2 * dilation_step)
    return conv_back_with(low, gv, high, flags, u, inputs, upstream, weights, dilation_step)


def conv_back_with(low, gv, high, flags, u, inputs, upstream, weights, dilation_step):
    pack, wide, narrow = weights
    rows, length, hidden = gv.shape
    tokens, model = inputs.shape
    sizes = Sizes(pack, model, hidden)
    return call(
        functools.partial(conv_back_kernel, dilation_step),
        rows,
        [
            row_block(low.shape),
            row_block(gv.shape),
            row_block(high.shape),
            row_block(flags.shape),
            tiled(length, hidden),
            tiled(length, model),
            tiled(length, model),
            *sizes.taps(),
            sizes.first(),
            fixed(3, model),
            fixed(6, hidden),
        ],
        [tiled(length, hidden), tiled(length, model), fixed(8, hidden), fixed(8, model)],
        [
            shape_of((tokens, hidden), jnp.bfloat16),
            shape_of((tokens, model), jnp.float32),
            shape_of((8, hidden), jnp.float32),
            shape_of((8, model), jnp.float32),
        ],
        2 * tokens * hidden * (KER * hidden + model),
        16 * tokens * model,
        "conv_back",
    )(low, gv, high, flags, u, inputs, upstream, *([pack] * (KER + 1)), wide, narrow)


def in_grads(grad_pack, act_one, gu):
    tokens, model = act_one.shape
    hidden = gu.shape[1]
    sizes = Sizes(grad_pack, model, hidden)
    return call(
        in_grad_kernel,
        1,
        [pl.BlockSpec(memory_space=pl.ANY), fixed(tokens, model), fixed(tokens, hidden)],
        sizes.first(),
        shape_of(grad_pack.shape, jnp.bfloat16),
        2 * tokens * hidden * model,
        4 * tokens * model,
        "in_grads",
        {0: 0},
    )(grad_pack, act_one, gu)


def scalars():
    return pl.BlockSpec(memory_space=pltpu.SMEM)


def place():
    return jnp.stack([lax.axis_index("dp"), lax.axis_index("seq")]).astype(jnp.int32)


def share_grads(where, tap_rows, gv, act_three, short):
    tokens, hidden = gv.shape
    model = short.shape[1]
    parts = lax.axis_size("dp")
    folds = model // hidden
    depth = hidden // parts
    whole = pl.BlockSpec((tokens, hidden), lambda s: (0, 0))
    share = pl.BlockSpec((parts // 2, depth, hidden), lambda s: (0, s, 0))
    shape = shape_of((parts // 2, (KER + folds) * depth, hidden), jnp.bfloat16)
    return call(
        share_grad_kernel,
        KER + folds,
        [
            scalars(),
            pl.BlockSpec((tokens, hidden), lambda s: (0, jnp.minimum(s, KER - 1))),
            whole,
            whole,
            pl.BlockSpec((tokens, hidden), lambda s: (0, jnp.maximum(s - KER, 0))),
        ],
        [share, share],
        [shape, shape],
        2 * tokens * hidden * (KER * hidden + model),
        8 * tokens * model,
        "share_grads",
        scratch=[pltpu.VMEM((parts, depth, hidden), jnp.bfloat16)],
    )(where, tap_rows, gv, act_three, short)


def share_in_grads(where, act_one, gu, sums):
    tokens, model = act_one.shape
    hidden = gu.shape[1]
    parts = lax.axis_size("dp")
    rows = model // parts + len(sums) // 4 * VECTOR_ROWS
    shape = shape_of((parts // 2, rows, hidden), jnp.bfloat16)
    return call(
        share_in_kernel,
        1,
        [scalars()] + [fixed(*array.shape) for array in (act_one, gu, *sums)],
        [fixed(*shape.shape)] * 2,
        [shape, shape],
        2 * tokens * hidden * model,
        4 * tokens * model,
        "share_in_grads",
        scratch=[pltpu.VMEM((parts, rows, hidden), jnp.bfloat16)],
    )(where, act_one, gu, *sums)


def chip_slot(shape, index):
    return pl.BlockSpec((1,) + shape[1:], lambda i: (index(i), 0, 0))


def first_sum(owns, gots):
    hidden = owns[0].shape[2]
    rows = sum(own.shape[1] for own in owns)
    cut = rows // 32 * 16
    a, b = (2, cut, hidden), (2, rows - cut, hidden)
    outs = [
        (a, lambda i: i // 2),
        (a, lambda i: i // 2),
        (b, lambda i: jnp.minimum(i, 1)),
        (b, lambda i: jnp.maximum(i - 2, 0)),
    ]
    return call(
        functools.partial(first_sum_kernel, cut, len(owns)),
        4,
        [chip_slot(array.shape, lambda i: i) for array in (*owns, *gots)],
        [chip_slot(shape, index) for shape, index in outs],
        [shape_of(shape, jnp.bfloat16) for shape, _ in outs],
        4 * rows * hidden,
        24 * rows * hidden,
        "first_sum",
    )(*owns, *gots)


def second_sum(keep_a, got_a, keep_b, got_b):
    ins = (keep_a, got_a, keep_b, got_b)
    outs = [shape_of(array.shape[1:], jnp.bfloat16) for array in ins]
    return call(
        second_sum_kernel,
        1,
        [fixed(*array.shape) for array in ins],
        [fixed(*out.shape) for out in outs],
        outs,
        2 * keep_a.size,
        12 * keep_a.size,
        "second_sum",
    )(*ins)


def seq_split(where, folded_rows, vector_rows, *ins):
    count = lax.axis_size("seq")
    rows = sum(array.shape[0] for array in ins[:: 2 if len(ins) > 1 else 1])
    width = ins[0].shape[1] // count
    shape = (count, rows, width)
    return call(
        functools.partial(seq_split_kernel, folded_rows, vector_rows),
        1,
        [scalars()] + [fixed(*array.shape) for array in ins],
        fixed(*shape),
        shape_of(shape, jnp.bfloat16),
        rows * width * count,
        6 * rows * width * count,
        "seq_split",
    )(where, *ins)


def seq_exchange(split):
    return [split[0]] + [shifted(split[step], step) for step in range(1, split.shape[0])]


def last_sum(pieces, out_shapes):
    flat = [array for _, piece in pieces for array in piece]
    outs = [shape_of(shape, jnp.float32) for shape in out_shapes]
    return call(
        functools.partial(last_sum_kernel, [(name, len(piece)) for name, piece in pieces]),
        1,
        [fixed(*array.shape) for array in flat],
        [fixed(*shape) for shape in out_shapes],
        outs,
        4 * flat[0].size,
        8 * flat[0].size,
        "last_sum",
    )(*flat)


def dp_swapped(block, bit):
    count = lax.axis_size("dp")
    return lax.ppermute(block, "dp", [(i, i ^ (1 << bit)) for i in range(count)])


class Chain:
    def __init__(self, token):
        self.token = token

    def hold(self, *values):
        return lax.optimization_barrier((*values, self.token))[:-1]

    def step(self, function, *values):
        out = function(*self.hold(*values))
        self.token = out[0] if isinstance(out, (list, tuple)) else out
        return out


def shifted(block, step):
    count = lax.axis_size("seq")
    return lax.ppermute(block, "seq", [(i, (i + step) % count) for i in range(count)])


def weight_pack(block_number, device_shards):
    w_in, w_conv, w_out = (device_shards[i][block_number] for i in (2, 6, 10))
    width = w_in.shape[1]
    folds = w_out.shape[1] // width
    pieces = [w_in, w_conv.reshape(-1, width)]
    pieces += [w_out[:, i * width : (i + 1) * width] for i in range(folds)]
    return jnp.concatenate(pieces, axis=0)


def vector_pack(block_number, device_shards, width):
    order = (0, 1, 11, 3, 4, 5, 7, 8, 9)
    rows = [device_shards[i][block_number] for i in order]
    rows = [jnp.pad(row, (0, width - row.shape[0])) for row in rows]
    return jnp.pad(jnp.stack(rows), ((0, VECTOR_ROWS - len(rows)), (0, 0)))


def seq_gathered(packed):
    count = lax.axis_size("seq")
    me = lax.axis_index("seq")
    held = [packed] + [shifted(packed, step) for step in range(1, count)]
    ring = jnp.stack(held[::-1] + held[::-1])
    return lax.dynamic_slice_in_dim(ring, (count - 1 - me) % count, count, axis=0)


def folded_columns(out_parts):
    count, folds, depth, width = out_parts.shape
    per_fold = count // folds
    return (
        out_parts.reshape(folds, per_fold, folds, depth, width)
        .transpose(0, 3, 1, 2, 4)
        .reshape(folds * depth, per_fold * folds * width)
    )


def unfolded_columns(out_rows, folds, count):
    per_fold = count // folds
    depth = out_rows.shape[0] // folds
    width = out_rows.shape[1] // count
    return (
        out_rows.reshape(folds, depth, per_fold, folds, width)
        .transpose(0, 2, 3, 1, 4)
        .reshape(count, folds * depth, width)
    )


def pack_is_aligned(middle_rows):
    return middle_rows % 16 == 0


def gathered_params(block_number, device_shards, after=None):
    w_in, w_conv, w_out = (device_shards[i][block_number] for i in (2, 6, 10))
    first_rows = w_in.shape[0]
    taps, middle_rows, width = w_conv.shape
    folds = w_out.shape[1] // width
    count = lax.axis_size("seq")
    hidden = width * count
    by_seq = seq_gathered(weight_pack(block_number, device_shards))
    straight = first_rows + taps * middle_rows
    total = straight + folds * middle_rows
    upper = by_seq[:, :straight].transpose(1, 0, 2).reshape(straight, hidden)
    lower = folded_columns(by_seq[:, straight:].reshape(count, folds, middle_rows, width))
    vectors = vector_pack(block_number, device_shards, hidden)
    packed = jnp.concatenate([upper, lower, vectors])
    if after is not None:
        packed, after = lax.optimization_barrier((packed, after))
    whole = lax.all_gather(packed, "dp")
    tail = whole[:, total:].astype(jnp.float32)
    wide = tail[:, :3, :first_rows].transpose(1, 0, 2).reshape(3, -1)
    narrow = tail[:, 3:9, :middle_rows].transpose(1, 0, 2).reshape(6, -1)
    if not pack_is_aligned(middle_rows):
        bounds = [0, first_rows]
        bounds += [first_rows + (k + 1) * middle_rows for k in range(taps + folds)]
        whole = jnp.concatenate(
            [whole[:, a:b].reshape(1, -1, hidden) for a, b in zip(bounds, bounds[1:])], axis=1
        )
    return (whole, wide, narrow)


def reduce_dp(grad_pack, wide_grads, narrow_grads):
    parts = lax.axis_size("dp")
    hidden = narrow_grads.shape[1]
    model = wide_grads.shape[1]
    first_rows = model // parts
    middle_rows = hidden // parts
    folds = model // hidden
    total = first_rows + (KER + folds) * middle_rows
    if not pack_is_aligned(middle_rows):
        bounds = [0, model] + [model + (k + 1) * hidden for k in range(KER + folds)]
        grad_pack = jnp.concatenate(
            [grad_pack[0, a:b].reshape(parts, -1, hidden) for a, b in zip(bounds, bounds[1:])]
            + [jnp.zeros((parts, VECTOR_ROWS, hidden), jnp.bfloat16)],
            axis=1,
        )
    vectors = jnp.concatenate(
        [
            jnp.pad(
                block.reshape(-1, parts, rows).transpose(1, 0, 2),
                ((0, 0), (0, 0), (0, hidden - rows)),
            )
            for block, rows in ((wide_grads, first_rows), (narrow_grads, middle_rows))
        ]
        + [jnp.zeros((parts, VECTOR_ROWS - 9, hidden), jnp.float32)],
        axis=1,
    ).astype(jnp.bfloat16)
    grad_pack = lax.dynamic_update_slice(grad_pack, vectors, (0, total, 0))
    return lax.psum_scatter(grad_pack, "dp", scatter_dimension=0, tiled=False)


def reduce_seq(mine, model, hidden):
    parts = lax.axis_size("dp")
    count = lax.axis_size("seq")
    me = lax.axis_index("seq")
    first_rows = model // parts
    middle_rows = hidden // parts
    width = hidden // count
    folds = model // hidden
    straight = first_rows + KER * middle_rows
    total = straight + folds * middle_rows
    upper = mine[:straight].reshape(straight, count, width).transpose(1, 0, 2)
    lower = unfolded_columns(mine[straight:total], folds, count)
    fold = -(-first_rows // width)
    tail = mine[total:, : fold * width].reshape(1, VECTOR_ROWS * fold, width)
    tail = jnp.broadcast_to(tail, (count,) + tail.shape[1:])
    ring = jnp.concatenate([upper, lower, tail], axis=1)
    ring = jnp.concatenate([ring, ring])
    ring = lax.dynamic_slice_in_dim(ring, me, count, axis=0)
    held = [ring[0]] + [shifted(ring[step], step) for step in range(1, count)]
    held = [block.astype(jnp.float32) for block in held]
    while len(held) > 1:
        half = len(held) // 2
        held = [held[i] + held[i + half] for i in range(half)]
    summed = held[0]
    last = summed[straight:total].reshape(folds, middle_rows, width).transpose(1, 0, 2)
    tail = summed[total:].reshape(VECTOR_ROWS, fold * width)
    return (
        summed[:first_rows],
        summed[first_rows:straight].reshape(KER, middle_rows, width),
        last.reshape(middle_rows, folds * width),
        tail[:3, :first_rows],
        tail[3:9, :middle_rows],
    )


def block_forward(inputs, weights, flags, dilation_step, next_dtype):
    rows, length, _ = flags.shape
    act_one, u, act_two = project(inputs, weights)
    tap_rows, conv_out, act_three, output = convolve(
        act_two.reshape(rows, length, -1), flags, inputs, weights, dilation_step, next_dtype
    )
    return output, (act_one, u, tap_rows, conv_out, act_three)


def block_backward(inputs, upstream, weights, kept, flags, dilation_step, before=None):
    act_one, u, tap_rows, conv_out, act_three = kept
    rows, length, _ = flags.shape
    short, gv, narrow_a, wide_a = out_back(upstream, conv_out, weights)
    pack = weights[0]
    grad_shape = shape_of(
        (pack.shape[0], sum(pack_rows(pack, inputs.shape[1], gv.shape[1])), gv.shape[1]),
        jnp.bfloat16,
    )
    grad_pack = weight_grads(tap_rows, gv, act_three, short, grad_shape)
    gu, result, narrow_b, wide_b = conv_back(
        gv.reshape(rows, length, -1), flags, u, inputs, upstream, weights, dilation_step
    )
    if before is not None:
        gu, before = lax.optimization_barrier((gu, before))
    grad_pack = in_grads(grad_pack, act_one, gu)
    wide = jnp.concatenate([wide_b[0:2], wide_a[0:1]])
    narrow = jnp.concatenate([narrow_b[0:3], narrow_a[0:3]])
    return result, reduce_dp(grad_pack, wide, narrow), before


def exchanged_backward(inputs, weights, kept, flags, dilations, cotangent, out_shapes):
    where = place()
    parts = lax.axis_size("dp")
    hidden = weights[1][2].shape[1]
    model = inputs[0].shape[1]
    depth = hidden // parts
    folded = (KER * depth, (KER + model // hidden) * depth)
    rows, length, _ = flags[0].shape

    act_one, u, tap_rows, conv_out, act_three = kept[1]
    short, gv, *out_sums_late = out_back(cotangent, conv_out, weights[1])
    blocks = gv.reshape(rows, length, -1)
    halos = seq_neighbours(blocks, KER // 2 * dilations[1])
    pack_shape = shape_of((parts, folded[1], hidden), jnp.bfloat16)
    pack = weight_grads(tap_rows, gv, act_three, short, pack_shape, 0)
    pack, low, high = lax.optimization_barrier((pack, *halos))
    late_sum = lax.psum_scatter(pack, "dp", scatter_dimension=0, tiled=False)
    gu, middle_grad, *in_sums_late = conv_back_with(
        low, blocks, high, flags[1], u, inputs[1], cotangent, weights[1], dilations[1]
    )
    chain = Chain(gu)
    own_first, other_first = chain.step(
        lambda *values: share_in_grads(where, *values, ()), act_one, gu
    )

    act_one, u, tap_rows, conv_out, act_three = kept[0]
    short, gv, *out_sums = chain.step(
        lambda value: out_back(value, conv_out, weights[0]), middle_grad
    )
    blocks = gv.reshape(rows, length, -1)
    halos = seq_neighbours(blocks, KER // 2 * dilations[0])
    own_taps, other_taps = share_grads(where, tap_rows, gv, act_three, short)
    low, high, own_taps, other_taps, other_first = lax.optimization_barrier(
        (*halos, own_taps, other_taps, other_first)
    )
    got_taps, got_first = dp_swapped(other_taps, 0), dp_swapped(other_first, 0)
    gu, input_grad, *in_sums = chain.step(
        lambda low, high: conv_back_with(
            low, blocks, high, flags[0], u, inputs[0], middle_grad, weights[0], dilations[0]
        ),
        low,
        high,
    )

    def first_round(sums):
        keep_a, send_a, keep_b, send_b = sums
        return keep_a, dp_swapped(send_a, 1), keep_b, dp_swapped(send_b, 2)

    def second_round(sums):
        kept_a, send_a, kept_b, send_b = sums
        return kept_a, dp_swapped(send_a, 2), kept_b, dp_swapped(send_b, 1)

    all_sums = (*out_sums, *in_sums, *out_sums_late, *in_sums_late)
    own, other = chain.step(
        lambda a, b: share_in_grads(where, a, b, all_sums), act_one, gu
    )
    owns = (own_taps, own_first, own)
    gots = (got_taps, got_first, dp_swapped(other, 0))
    main = first_round(
        chain.step(lambda *values: first_sum(values[:3], values[3:]), *owns, *gots)
    )
    late = seq_exchange(chain.step(lambda value: seq_split(where, folded, 0, value), late_sum))
    main, late = lax.optimization_barrier((main, late))
    main = second_round(second_sum(*main))
    main = seq_exchange(seq_split(where, folded, 2 * VECTOR_ROWS, *main))
    return input_grad, last_sum((("early", main), ("late", late)), out_shapes)


def pack_rows(pack, model, hidden):
    parts = pack.shape[0]
    extra = VECTOR_ROWS if pack_is_aligned(hidden // lax.axis_size("dp")) else 0
    return model // parts, (KER * hidden + model) // parts, extra


def local(
    tokens,
    protein_lengths,
    norm1_gain,
    norm1_bias,
    w_in,
    in_bias,
    norm2_gain,
    norm2_bias,
    w_conv,
    conv_bias,
    norm3_gain,
    norm3_bias,
    w_out,
    out_bias,
    cotangent,
):
    device_shards = (
        norm1_gain,
        norm1_bias,
        w_in,
        in_bias,
        norm2_gain,
        norm2_bias,
        w_conv,
        conv_bias,
        norm3_gain,
        norm3_bias,
        w_out,
        out_bias,
    )
    rows, seq_len, model = tokens.shape
    token_positions = lax.axis_index("seq") * seq_len + jnp.arange(seq_len, dtype=jnp.int32)
    early_flags = kernel_tap_flags(protein_lengths, token_positions, FIRST_DILATION)
    later_flags = kernel_tap_flags(protein_lengths, token_positions, SECOND_DILATION)
    early_weights = gathered_params(0, device_shards)
    late_weights = gathered_params(1, device_shards, early_weights[0])
    flat_tokens = tokens.reshape(rows * seq_len, model)
    middle, early_kept = block_forward(
        flat_tokens, early_weights, early_flags, FIRST_DILATION, jnp.float32
    )
    middle, late_weights = lax.optimization_barrier((middle, late_weights))
    output, late_kept = block_forward(
        middle, late_weights, later_flags, SECOND_DILATION, jnp.bfloat16
    )
    hidden = early_weights[2].shape[1]
    if lax.axis_size("dp") == 8 and pack_is_aligned(hidden // 8):
        shapes = [w.shape for w in (w_in, w_conv, w_out, norm1_gain, norm1_bias, out_bias)]
        shapes += [w.shape for w in (in_bias, norm2_gain, norm2_bias)]
        shapes += [w.shape for w in (conv_bias, norm3_gain, norm3_bias)]
        input_grad, grads = exchanged_backward(
            (flat_tokens, middle),
            (early_weights, late_weights),
            (early_kept, late_kept),
            (early_flags, later_flags),
            (FIRST_DILATION, SECOND_DILATION),
            cotangent.reshape(rows * seq_len, model),
            shapes,
        )
        order = (3, 4, 0, 6, 7, 8, 1, 9, 10, 11, 2, 5)
        return (
            output.reshape(tokens.shape),
            input_grad.reshape(tokens.shape),
            *(grads[i] for i in order),
        )
    middle_grad, mine_late, _ = block_backward(
        middle,
        cotangent.reshape(rows * seq_len, model),
        late_weights,
        late_kept,
        later_flags,
        SECOND_DILATION,
    )
    input_grad, mine_early, mine_late = block_backward(
        flat_tokens,
        middle_grad,
        early_weights,
        early_kept,
        early_flags,
        FIRST_DILATION,
        mine_late,
    )
    reduced_late = reduce_seq(mine_late, model, hidden)
    reduced_early = reduce_seq(mine_early, model, hidden)
    first_early, middle_early, last_early, wide_early, narrow_early = reduced_early
    first_late, middle_late, last_late, wide_late, narrow_late = reduced_late
    return (
        output.reshape(tokens.shape),
        input_grad.reshape(tokens.shape),
        jnp.stack([wide_early[0], wide_late[0]]),
        jnp.stack([wide_early[1], wide_late[1]]),
        jnp.stack([first_early, first_late]),
        jnp.stack([narrow_early[0], narrow_late[0]]),
        jnp.stack([narrow_early[1], narrow_late[1]]),
        jnp.stack([narrow_early[2], narrow_late[2]]),
        jnp.stack([middle_early, middle_late]),
        jnp.stack([narrow_early[3], narrow_late[3]]),
        jnp.stack([narrow_early[4], narrow_late[4]]),
        jnp.stack([narrow_early[5], narrow_late[5]]),
        jnp.stack([last_early, last_late]),
        jnp.stack([wide_early[2], wide_late[2]]),
    )


def solution(mesh):
    placed = (
        P("dp", "seq", None),
        P("dp", None),
        P(None, "dp"),
        P(None, "dp"),
        P(None, "dp", "seq"),
        P(None, "dp"),
        P(None, "dp"),
        P(None, "dp"),
        P(None, None, "dp", "seq"),
        P(None, "dp"),
        P(None, "dp"),
        P(None, "dp"),
        P(None, "dp", "seq"),
        P(None, "dp"),
        P("dp", "seq", None),
    )
    return jax.shard_map(
        local,
        mesh=mesh,
        in_specs=placed,
        out_specs=(
            P("dp", "seq", None),
            P("dp", "seq", None),
            P(None, "dp"),
            P(None, "dp"),
            P(None, "dp", "seq"),
            P(None, "dp"),
            P(None, "dp"),
            P(None, "dp"),
            P(None, None, "dp", "seq"),
            P(None, "dp"),
            P(None, "dp"),
            P(None, "dp"),
            P(None, "dp", "seq"),
            P(None, "dp"),
        ),
        check_vma=False,
    )
```

```python
import functools
import math

import jax
import jax.numpy as jnp
from jax import lax
from jax.experimental import pallas as pl
from jax.experimental.pallas import tpu as pltpu
from jax.sharding import PartitionSpec as P

KER = 5
FIRST_DILATION = 64
SECOND_DILATION = 128


epsilon = 1e-05
CUBIC = 0.044715
SLOPE = math.sqrt(2.0 / math.pi)
VECTOR_ROWS = 16


def seq_neighbours(block, width):
    count = lax.axis_size("seq")
    forward = [(i, i + 1) for i in range(count - 1)]
    backward = [(target, source) for source, target in forward]
    low = lax.ppermute(block[:, block.shape[1] - width :], "seq", forward)
    high = lax.ppermute(block[:, :width], "seq", backward)
    return low, high


def normalized(values):
    centred = values - jnp.mean(values, -1, keepdims=True)
    scale = lax.rsqrt(jnp.mean(centred * centred, -1, keepdims=True) + epsilon)
    return centred * scale, scale


def gelu(h):
    return 0.5 * h * (1.0 + jnp.tanh(SLOPE * (h + CUBIC * (h * h * h))))


def norm_gelu(values, gain_vector, bias_vector):
    return gelu(normalized(values)[0] * gain_vector + bias_vector)


def norm_gelu_back(incoming, values, gain_vector, bias_vector):
    n, scale = normalized(values)
    h = n * gain_vector + bias_vector
    square = h * h
    t = jnp.tanh(SLOPE * (h + CUBIC * (square * h)))
    slope = 0.5 * (1.0 + t) + (0.5 * SLOPE) * h * (1.0 - t * t) * (1.0 + (3.0 * CUBIC) * square)
    dh = incoming * slope
    dn = dh * gain_vector
    back = dn - jnp.mean(dn, -1, keepdims=True) - n * jnp.mean(dn * n, -1, keepdims=True)
    return back * scale, column_sum(dh * n), column_sum(dh)


def column_sum(values):
    return jnp.sum(values, axis=0, keepdims=True)


def matmul(left, right):
    return jnp.dot(left, right, preferred_element_type=jnp.float32)


def matmul_back(left, right):
    return lax.dot_general(
        left, right, (((1,), (1,)), ((), ())), preferred_element_type=jnp.float32
    )


def matmul_rows(left, right):
    return lax.dot_general(
        left, right, (((0,), (0,)), ((), ())), preferred_element_type=jnp.float32
    )


def merged(ref):
    parts, rows, columns = ref.shape
    return ref[...].reshape(parts * rows, columns)


def kernel_tap_flags(lengths, token_positions, dilation_step):
    doc_ends = jnp.cumsum(lengths, axis=1)
    row_total = doc_ends[:, -1:]
    where_pos = token_positions[None, :, None]
    finished = doc_ends[:, None, :] <= where_pos
    doc_start = jnp.sum(jnp.where(finished, lengths[:, None, :], 0), axis=2)
    doc_stop = jnp.min(jnp.where(finished, row_total[:, :, None] + 1, doc_ends[:, None, :]), axis=2)
    is_live = token_positions[None, :] < row_total
    flag_list = []
    for tap_index in range(KER):
        target = token_positions[None, :] + (tap_index - KER // 2) * dilation_step
        flag_list.append(is_live & (target >= doc_start) & (target < doc_stop))
    flag_list += [flag_list[-1]] * (8 - KER)
    return jnp.stack(flag_list, axis=2).astype(jnp.bfloat16)


def project_kernel(x_ref, w_ref, wide_ref, narrow_ref, act_one_ref, u_ref, act_two_ref):
    act_one = norm_gelu(
        x_ref[...].astype(jnp.float32), wide_ref[0:1, :], wide_ref[1:2, :]
    ).astype(jnp.bfloat16)
    act_one_ref[...] = act_one
    u = matmul(act_one, merged(w_ref)) + narrow_ref[0:1, :]
    u_ref[...] = u
    act_two_ref[...] = norm_gelu(u, narrow_ref[1:2, :], narrow_ref[2:3, :]).astype(jnp.bfloat16)


def tap_slices(low_ref, own_ref, high_ref, flag_ref, dilation_step):
    length = own_ref.shape[1]
    width = low_ref.shape[1]
    padded = jnp.concatenate([low_ref[0], own_ref[0], high_ref[0]], axis=0)
    for k in range(KER):
        start = width + (k - KER // 2) * dilation_step
        yield k, padded[start : start + length] * flag_ref[0][:, k : k + 1]


def convolve_kernel(
    dilation_step,
    low_ref,
    own_ref,
    high_ref,
    flag_ref,
    x_ref,
    k0_ref,
    k1_ref,
    k2_ref,
    k3_ref,
    k4_ref,
    left_ref,
    right_ref,
    wide_ref,
    narrow_ref,
    tap_ref,
    v_ref,
    act_three_ref,
    next_ref,
):
    taps = (k0_ref, k1_ref, k2_ref, k3_ref, k4_ref)
    hidden = own_ref.shape[2]
    total = narrow_ref[3:4, :]
    for k, piece in tap_slices(low_ref, own_ref, high_ref, flag_ref, dilation_step):
        tap_ref[:, k * hidden : (k + 1) * hidden] = piece
        total = total + matmul(piece, merged(taps[k]))
    v_ref[...] = total
    act_three = norm_gelu(total, narrow_ref[4:5, :], narrow_ref[5:6, :]).astype(jnp.bfloat16)
    act_three_ref[...] = act_three
    for i, half_ref in enumerate((left_ref, right_ref)):
        columns = slice(i * hidden, (i + 1) * hidden)
        branch = matmul(act_three, merged(half_ref)) + wide_ref[2:3, columns]
        next_ref[:, columns] = (x_ref[:, columns].astype(jnp.float32) + branch).astype(
            next_ref.dtype
        )


def out_back_kernel(
    g_ref, v_ref, left_ref, right_ref, narrow_ref, short_ref, gv_ref, narrow_sum_ref, wide_sum_ref
):
    hidden = v_ref.shape[1]

    @pl.when(pl.program_id(0) == 0)
    def _():
        narrow_sum_ref[...] = jnp.zeros_like(narrow_sum_ref)
        wide_sum_ref[...] = jnp.zeros_like(wide_sum_ref)

    short = g_ref[...].astype(jnp.bfloat16)
    short_ref[...] = short
    wide_sum_ref[0:1, :] += column_sum(short.astype(jnp.float32))
    incoming = matmul_back(short[:, :hidden], merged(left_ref))
    incoming = incoming + matmul_back(short[:, hidden:], merged(right_ref))
    gv, gain_sum, bias_sum = norm_gelu_back(
        incoming, v_ref[...], narrow_ref[4:5, :], narrow_ref[5:6, :]
    )
    gv = gv.astype(jnp.bfloat16)
    gv_ref[...] = gv
    narrow_sum_ref[0:1, :] += column_sum(gv.astype(jnp.float32))
    narrow_sum_ref[1:2, :] += gain_sum
    narrow_sum_ref[2:3, :] += bias_sum


def weight_grad_kernel(tap_ref, gv_ref, act_three_ref, short_ref, pack_ref):
    step = pl.program_id(0)

    def store(value):
        pack_ref[...] = value.astype(jnp.bfloat16).reshape(pack_ref.shape)

    @pl.when(step < KER)
    def _():
        store(matmul_rows(tap_ref[...], gv_ref[...]))

    @pl.when(step >= KER)
    def _():
        store(matmul_rows(act_three_ref[...], short_ref[...]))


def conv_back_kernel(
    dilation_step,
    low_ref,
    own_ref,
    high_ref,
    flag_ref,
    u_ref,
    x_ref,
    g_ref,
    k0_ref,
    k1_ref,
    k2_ref,
    k3_ref,
    k4_ref,
    w_ref,
    wide_ref,
    narrow_ref,
    gu_ref,
    next_ref,
    narrow_sum_ref,
    wide_sum_ref,
):
    @pl.when(pl.program_id(0) == 0)
    def _():
        narrow_sum_ref[...] = jnp.zeros_like(narrow_sum_ref)
        wide_sum_ref[...] = jnp.zeros_like(wide_sum_ref)

    taps = (k0_ref, k1_ref, k2_ref, k3_ref, k4_ref)
    total = None
    for k, piece in tap_slices(low_ref, own_ref, high_ref, flag_ref, dilation_step):
        term = matmul_back(piece, merged(taps[KER - 1 - k]))
        total = term if total is None else total + term
    gu, gain_sum, bias_sum = norm_gelu_back(
        total, u_ref[...], narrow_ref[1:2, :], narrow_ref[2:3, :]
    )
    gu = gu.astype(jnp.bfloat16)
    gu_ref[...] = gu
    narrow_sum_ref[0:1, :] += column_sum(gu.astype(jnp.float32))
    narrow_sum_ref[1:2, :] += gain_sum
    narrow_sum_ref[2:3, :] += bias_sum
    gx, gain_sum, bias_sum = norm_gelu_back(
        matmul_back(gu, merged(w_ref)),
        x_ref[...].astype(jnp.float32),
        wide_ref[0:1, :],
        wide_ref[1:2, :],
    )
    next_ref[...] = g_ref[...].astype(jnp.float32) + gx
    wide_sum_ref[0:1, :] += gain_sum
    wide_sum_ref[1:2, :] += bias_sum


def in_grad_kernel(pack_in_ref, act_one_ref, gu_ref, pack_ref):
    value = matmul_rows(act_one_ref[...], gu_ref[...])
    pack_ref[...] = value.astype(jnp.bfloat16).reshape(pack_ref.shape)


def spread(rows, place_ref, hold_ref, own_ref, other_ref):
    chip, core = place_ref[0] // 2, place_ref[0] % 2
    for i in range(own_ref.shape[0]):
        at = 2 * (chip ^ i)
        own_ref[i] = hold_ref[at + core, rows]
        other_ref[i] = hold_ref[at + 1 - core, rows]


def share_grad_kernel(
    place_ref, tap_ref, gv_ref, act_three_ref, short_ref, own_ref, other_ref, hold_ref
):
    step = pl.program_id(0)

    def store(value):
        hold_ref[...] = value.astype(jnp.bfloat16).reshape(hold_ref.shape)

    @pl.when(step < KER)
    def _():
        store(matmul_rows(tap_ref[...], gv_ref[...]))

    @pl.when(step >= KER)
    def _():
        store(matmul_rows(act_three_ref[...], short_ref[...]))

    spread(slice(None), place_ref, hold_ref, own_ref, other_ref)


def share_in_kernel(place_ref, act_one_ref, gu_ref, *refs):
    *sum_refs, own_ref, other_ref, hold_ref = refs
    parts = hold_ref.shape[0]
    hidden = gu_ref.shape[1]
    depth = act_one_ref.shape[1] // parts
    value = matmul_rows(act_one_ref[...], gu_ref[...]).astype(jnp.bfloat16)
    hold_ref[:, :depth, :] = value.reshape(parts, depth, hidden)
    for block in range(len(sum_refs) // 4):
        narrow_a, wide_a, narrow_b, wide_b = (ref[...] for ref in sum_refs[4 * block : 4 * block + 4])
        wide = jnp.concatenate([wide_b[0:2], wide_a[0:1]], axis=0)
        narrow = jnp.concatenate([narrow_b[0:3], narrow_a[0:3]], axis=0)
        narrow_depth = hidden // parts
        for part in range(parts):
            rows = [
                wide[:, part * depth : (part + 1) * depth],
                jnp.concatenate(
                    [
                        narrow[:, part * narrow_depth : (part + 1) * narrow_depth],
                        jnp.zeros((6, depth - narrow_depth), jnp.float32),
                    ],
                    axis=1,
                ),
                jnp.zeros((VECTOR_ROWS - 9, depth), jnp.float32),
            ]
            rows = jnp.concatenate(rows, axis=0)
            rows = jnp.concatenate(
                [rows, jnp.zeros((VECTOR_ROWS, hidden - depth), jnp.float32)], axis=1
            )
            start = depth + block * VECTOR_ROWS
            hold_ref[part, start : start + VECTOR_ROWS, :] = rows.astype(jnp.bfloat16)
    spread(slice(None), place_ref, hold_ref, own_ref, other_ref)


def plus(left, right):
    return left.astype(jnp.float32) + right.astype(jnp.float32)


def first_sum_kernel(cut, count, *refs):
    step = pl.program_id(0)
    keep_a, send_a, keep_b, send_b = refs[2 * count :]
    pieces = [
        plus(own[0], got[0]).astype(jnp.bfloat16) for own, got in zip(refs[:count], refs[count:])
    ]
    total = pieces[0] if count == 1 else jnp.concatenate(pieces, axis=0)
    upper, lower = total[:cut], total[cut:]

    @pl.when(step % 2 == 0)
    def _():
        keep_a[0] = upper

    @pl.when(step % 2 == 1)
    def _():
        send_a[0] = upper

    @pl.when(step < 2)
    def _():
        keep_b[0] = lower

    @pl.when(step >= 2)
    def _():
        send_b[0] = lower


def second_sum_kernel(keep_a, got_a, keep_b, got_b, kept_a, send_a, kept_b, send_b):
    for keep, got, kept, send in (
        (keep_a, got_a, kept_a, send_a),
        (keep_b, got_b, kept_b, send_b),
    ):
        kept[...] = plus(keep[0], got[0]).astype(jnp.bfloat16)
        send[...] = plus(keep[1], got[1]).astype(jnp.bfloat16)


def lane_packed(rows, depth, count):
    missing = count * depth - rows.shape[0]
    if missing:
        rows = jnp.concatenate([rows, jnp.zeros((missing, rows.shape[1]), rows.dtype)], axis=0)
    return jnp.concatenate([rows[i * depth : (i + 1) * depth] for i in range(count)], axis=1)


def lane_unpacked(packed, count):
    width = packed.shape[1] // count
    return jnp.concatenate([packed[:, i * width : (i + 1) * width] for i in range(count)], axis=0)


def packed_depth(rows, count):
    return -(-rows // (16 * count)) * 16


def seq_split_kernel(folded_rows, vector_rows, place_ref, *refs):
    *in_refs, out_ref = refs
    if len(in_refs) == 1:
        total = in_refs[0][...]
    else:
        halves = [plus(in_refs[i][...], in_refs[i + 1][...]) for i in range(0, len(in_refs), 2)]
        total = jnp.concatenate(halves, axis=0)
    total = total.astype(jnp.float32)
    count, width = out_ref.shape[0], total.shape[1] // out_ref.shape[0]
    rows = total.shape[0]
    at, end = folded_rows
    fold = (end - at) // 2
    for s in range(count):
        columns = total[:, s * width : (s + 1) * width]
        if end > at:
            unit = at + (s // 2) * fold
            left = (s % 2) * 2 * width
            pair = total[unit : unit + fold, left : left + 2 * width]
            pieces = [columns[:at], pair[:, :width], pair[:, width:], columns[end:]]
            columns = jnp.concatenate([p for p in pieces if p.shape[0]], axis=0)
        if vector_rows:
            columns = jnp.concatenate(
                [columns[: rows - vector_rows], total[rows - vector_rows :, :width]], axis=0
            )
        packed = lane_packed(columns, out_ref.shape[1], count)
        out_ref[(s - place_ref[1] + count) % count] = packed.astype(jnp.bfloat16)


def last_sum_kernel(layout, *refs):
    sums = {}
    at = 0
    for name, count in layout:
        own, one, two, three = (ref[...].astype(jnp.float32) for ref in refs[at : at + 4])
        at += 4
        sums[name] = lane_unpacked((own + two) + (one + three), 4)
    first_ref, taps_ref, last_ref = refs[at : at + 3]
    vector_refs = refs[at + 3 :]
    depth = taps_ref.shape[2]
    straight = KER * depth
    first_rows = first_ref.shape[1]
    for block, piece in ((0, sums["early"]), (1, sums["late"])):
        for k in range(KER):
            taps_ref[block, k] = piece[k * depth : (k + 1) * depth]
        last_ref[block] = jnp.concatenate(
            [piece[straight : straight + depth], piece[straight + depth : straight + 2 * depth]],
            axis=1,
        )
    rest = sums["early"][straight + 2 * depth :]
    first_ref[0] = rest[first_rows : 2 * first_rows]
    first_ref[1] = rest[:first_rows]
    for block in range(2):
        start = 2 * first_rows + block * VECTOR_ROWS
        for i, ref in enumerate(vector_refs):
            row = rest[start + i : start + i + 1]
            ref[block : block + 1, :] = row[:, : ref.shape[1]]


def main_pack_kernel(w_conv, w_out, early_ref, late_ref):
    width = w_conv.shape[3]
    count = early_ref.shape[1] // width
    for block, ref in ((0, early_ref), (1, late_ref)):
        rows = [w_conv[block, k] for k in range(KER)]
        rows += [w_out[block][:, :width], w_out[block][:, width:]]
        ref[...] = lane_packed(jnp.concatenate(rows, axis=0), ref.shape[0], count)


def lead_pack_kernel(w_in, wide, narrow, lead_ref, vector_ref):
    count = lead_ref.shape[1] // w_in.shape[2]
    lead = jnp.concatenate([w_in[0], w_in[1]], axis=0)
    lead_ref[...] = lane_packed(lead, lead_ref.shape[0], count)
    hidden = vector_ref.shape[1]
    for block in range(2):
        rows = []
        for ref in (wide, narrow):
            part = ref[block].astype(jnp.float32)
            rows.append(
                jnp.concatenate(
                    [part, jnp.zeros((part.shape[0], hidden - part.shape[1]), jnp.float32)], axis=1
                )
            )
        rows.append(jnp.zeros((VECTOR_ROWS - 9, hidden), jnp.float32))
        start = block * VECTOR_ROWS
        vector_ref[start : start + VECTOR_ROWS, :] = jnp.concatenate(rows, axis=0).astype(
            jnp.bfloat16
        )


def seq_join_kernel(folded_rows, vector_rows, place_ref, *refs):
    *in_refs, out_ref, hold_ref = refs
    vector_in = in_refs.pop() if vector_rows else None
    count = len(in_refs)
    for step, ref in enumerate(in_refs):
        hold_ref[(place_ref[1] - step + count) % count] = ref[...]
    shares = [lane_unpacked(hold_ref[s], count) for s in range(count)]
    rows = out_ref.shape[0] - vector_rows
    at, end = folded_rows
    if at:
        out_ref[:at, :] = jnp.concatenate([share[:at] for share in shares], axis=1)
    if end > at:
        fold = (end - at) // 2
        for half in range(2):
            columns = []
            for share in shares[half * count // 2 : (half + 1) * count // 2]:
                columns += [share[at : at + fold], share[at + fold : end]]
            start = at + half * fold
            out_ref[start : start + fold, :] = jnp.concatenate(columns, axis=1)
    if vector_in is not None:
        out_ref[rows:, :] = vector_in[...]


def place_kernel(place_ref, *refs):
    *in_refs, out_ref = refs
    chip, core = place_ref[0] // 2, place_ref[0] % 2
    cut = in_refs[0].shape[1]
    for at, share_core in ((0, core), (4, 1 - core)):
        near_a, far_a, near_b, far_b = in_refs[at : at + 4]
        for i in range(2):
            out_ref[2 * (chip ^ i) + share_core, :cut] = near_a[i]
            out_ref[2 * (chip ^ (2 + i)) + share_core, :cut] = far_a[i]
            out_ref[2 * (chip ^ (2 * i)) + share_core, cut:] = near_b[i]
            out_ref[2 * (chip ^ (2 * i + 1)) + share_core, cut:] = far_b[i]


def tiled(rows, columns):
    return pl.BlockSpec((rows, columns), lambda i: (i, 0))


def fixed(*shape):
    return pl.BlockSpec(shape, lambda i: (0,) * len(shape))


def row_block(shape):
    return pl.BlockSpec((1,) + shape[1:], lambda i: (i, 0, 0))


def pack_block(parts, rows, columns, index):
    return pl.BlockSpec((parts, rows, columns), lambda i: (0, index, 0))


def cost(flops, width):
    return pl.CostEstimate(flops=flops, bytes_accessed=width, transcendentals=0)


def call(kernel, grid, in_specs, out_specs, out_shape, flops, moved, name, aliases=None, scratch=()):
    return pl.pallas_call(
        kernel,
        grid=(grid,),
        in_specs=in_specs,
        out_specs=out_specs,
        out_shape=out_shape,
        scratch_shapes=list(scratch),
        input_output_aliases=aliases or {},
        cost_estimate=cost(flops, moved),
        compiler_params=pltpu.CompilerParams(vmem_limit_bytes=32 * 1024 * 1024),
        name=name,
    )


def shape_of(shape, dtype):
    return jax.ShapeDtypeStruct(shape, dtype)


class Weights:
    def __init__(self, first, taps, last, wide, narrow):
        self.first, self.taps, self.last = first, taps, last
        self.wide, self.narrow = wide, narrow
        self.model, self.hidden = wide.shape[1], narrow.shape[1]

    def first_spec(self):
        array, index = self.first
        return pack_block(array.shape[0], self.model // array.shape[0], self.hidden, index)

    def specs(self, units):
        return [
            pack_block(array.shape[0], self.hidden // array.shape[0], self.hidden, index)
            for array, index in units
        ]


def arrays(units):
    return [array for array, _ in units]


def pack_weights(pack, wide, narrow):
    folds = wide.shape[1] // narrow.shape[1]
    units = [(pack, folds + i) for i in range(KER + folds)]
    return Weights((pack, 0), units[:KER], units[KER:], wide, narrow)


class Sizes:
    def __init__(self, pack, model, hidden):
        self.parts = pack.shape[0]
        self.model, self.hidden = model, hidden
        self.first_rows = model // self.parts
        self.middle_rows = hidden // self.parts
        self.folds = model // hidden
        self.conv_at = self.first_rows // self.middle_rows

    def first(self):
        return pack_block(self.parts, self.first_rows, self.hidden, 0)


def project(inputs, weights):
    tokens, model = inputs.shape
    hidden = weights.hidden
    tile = min(128, tokens)
    return call(
        project_kernel,
        tokens // tile,
        [tiled(tile, model), weights.first_spec(), fixed(3, model), fixed(6, hidden)],
        [tiled(tile, model), tiled(tile, hidden), tiled(tile, hidden)],
        [
            shape_of((tokens, model), jnp.bfloat16),
            shape_of((tokens, hidden), jnp.float32),
            shape_of((tokens, hidden), jnp.bfloat16),
        ],
        4 * tokens * model * hidden,
        12 * tokens * model,
        "project",
    )(inputs, weights.first[0], weights.wide, weights.narrow)


def convolve(act_two, flags, inputs, weights, dilation_step, next_dtype):
    rows, length, hidden = act_two.shape
    tokens, model = inputs.shape
    low, high = seq_neighbours(act_two, KER // 2 * dilation_step)
    return call(
        functools.partial(convolve_kernel, dilation_step),
        rows,
        [
            row_block(low.shape),
            row_block(act_two.shape),
            row_block(high.shape),
            row_block(flags.shape),
            tiled(length, model),
            *weights.specs(weights.taps + weights.last),
            fixed(3, model),
            fixed(6, hidden),
        ],
        [
            tiled(length, KER * hidden),
            tiled(length, hidden),
            tiled(length, hidden),
            tiled(length, model),
        ],
        [
            shape_of((tokens, KER * hidden), jnp.bfloat16),
            shape_of((tokens, hidden), jnp.float32),
            shape_of((tokens, hidden), jnp.bfloat16),
            shape_of((tokens, model), next_dtype),
        ],
        2 * tokens * hidden * (KER * hidden + model),
        16 * tokens * model,
        "convolve",
    )(
        low,
        act_two,
        high,
        flags,
        inputs,
        *arrays(weights.taps + weights.last),
        weights.wide,
        weights.narrow,
    )


def out_back(upstream, conv_out, weights):
    tokens, model = upstream.shape
    hidden = weights.hidden
    tile = min(128, tokens)
    return call(
        out_back_kernel,
        tokens // tile,
        [
            tiled(tile, model),
            tiled(tile, hidden),
            *weights.specs(weights.last),
            fixed(6, hidden),
        ],
        [tiled(tile, model), tiled(tile, hidden), fixed(8, hidden), fixed(8, model)],
        [
            shape_of((tokens, model), jnp.bfloat16),
            shape_of((tokens, hidden), jnp.bfloat16),
            shape_of((8, hidden), jnp.float32),
            shape_of((8, model), jnp.float32),
        ],
        4 * tokens * model * hidden,
        10 * tokens * model,
        "out_back",
    )(upstream, conv_out, *arrays(weights.last), weights.narrow)


def weight_grads(tap_rows, gv, act_three, short, pack, conv_at=None):
    tokens, hidden = gv.shape
    model = short.shape[1]
    sizes = Sizes(pack, model, hidden)
    conv_at = sizes.conv_at if conv_at is None else conv_at
    whole = pl.BlockSpec((tokens, hidden), lambda s: (0, 0))
    return call(
        weight_grad_kernel,
        KER + sizes.folds,
        [
            pl.BlockSpec((tokens, hidden), lambda s: (0, jnp.minimum(s, KER - 1))),
            whole,
            whole,
            pl.BlockSpec((tokens, hidden), lambda s: (0, jnp.maximum(s - KER, 0))),
        ],
        pl.BlockSpec(
            (sizes.parts, sizes.middle_rows, hidden), lambda s: (0, conv_at + s, 0)
        ),
        shape_of(pack.shape, jnp.bfloat16),
        2 * tokens * hidden * (KER * hidden + model),
        8 * tokens * model,
        "weight_grads",
    )(tap_rows, gv, act_three, short)


def conv_back(gv, flags, u, inputs, upstream, weights, dilation_step):
    low, high = seq_neighbours(gv, KER // 2 * dilation_step)
    return conv_back_with(low, gv, high, flags, u, inputs, upstream, weights, dilation_step)


def conv_back_with(low, gv, high, flags, u, inputs, upstream, weights, dilation_step):
    rows, length, hidden = gv.shape
    tokens, model = inputs.shape
    return call(
        functools.partial(conv_back_kernel, dilation_step),
        rows,
        [
            row_block(low.shape),
            row_block(gv.shape),
            row_block(high.shape),
            row_block(flags.shape),
            tiled(length, hidden),
            tiled(length, model),
            tiled(length, model),
            *weights.specs(weights.taps),
            weights.first_spec(),
            fixed(3, model),
            fixed(6, hidden),
        ],
        [tiled(length, hidden), tiled(length, model), fixed(8, hidden), fixed(8, model)],
        [
            shape_of((tokens, hidden), jnp.bfloat16),
            shape_of((tokens, model), jnp.float32),
            shape_of((8, hidden), jnp.float32),
            shape_of((8, model), jnp.float32),
        ],
        2 * tokens * hidden * (KER * hidden + model),
        16 * tokens * model,
        "conv_back",
    )(
        low,
        gv,
        high,
        flags,
        u,
        inputs,
        upstream,
        *arrays(weights.taps),
        weights.first[0],
        weights.wide,
        weights.narrow,
    )


def in_grads(grad_pack, act_one, gu):
    tokens, model = act_one.shape
    hidden = gu.shape[1]
    sizes = Sizes(grad_pack, model, hidden)
    return call(
        in_grad_kernel,
        1,
        [pl.BlockSpec(memory_space=pl.ANY), fixed(tokens, model), fixed(tokens, hidden)],
        sizes.first(),
        shape_of(grad_pack.shape, jnp.bfloat16),
        2 * tokens * hidden * model,
        4 * tokens * model,
        "in_grads",
        {0: 0},
    )(grad_pack, act_one, gu)


def scalars():
    return pl.BlockSpec(memory_space=pltpu.SMEM)


def place():
    return jnp.stack([lax.axis_index("dp"), lax.axis_index("seq")]).astype(jnp.int32)


def share_grads(where, tap_rows, gv, act_three, short):
    tokens, hidden = gv.shape
    model = short.shape[1]
    parts = lax.axis_size("dp")
    folds = model // hidden
    depth = hidden // parts
    whole = pl.BlockSpec((tokens, hidden), lambda s: (0, 0))
    share = pl.BlockSpec((parts // 2, depth, hidden), lambda s: (0, s, 0))
    shape = shape_of((parts // 2, (KER + folds) * depth, hidden), jnp.bfloat16)
    return call(
        share_grad_kernel,
        KER + folds,
        [
            scalars(),
            pl.BlockSpec((tokens, hidden), lambda s: (0, jnp.minimum(s, KER - 1))),
            whole,
            whole,
            pl.BlockSpec((tokens, hidden), lambda s: (0, jnp.maximum(s - KER, 0))),
        ],
        [share, share],
        [shape, shape],
        2 * tokens * hidden * (KER * hidden + model),
        8 * tokens * model,
        "share_grads",
        scratch=[pltpu.VMEM((parts, depth, hidden), jnp.bfloat16)],
    )(where, tap_rows, gv, act_three, short)


def share_in_grads(where, act_one, gu, sums):
    tokens, model = act_one.shape
    hidden = gu.shape[1]
    parts = lax.axis_size("dp")
    rows = model // parts + len(sums) // 4 * VECTOR_ROWS
    shape = shape_of((parts // 2, rows, hidden), jnp.bfloat16)
    return call(
        share_in_kernel,
        1,
        [scalars()] + [fixed(*array.shape) for array in (act_one, gu, *sums)],
        [fixed(*shape.shape)] * 2,
        [shape, shape],
        2 * tokens * hidden * model,
        4 * tokens * model,
        "share_in_grads",
        scratch=[pltpu.VMEM((parts, rows, hidden), jnp.bfloat16)],
    )(where, act_one, gu, *sums)


def chip_slot(shape, index):
    return pl.BlockSpec((1,) + shape[1:], lambda i: (index(i), 0, 0))


def first_sum(owns, gots):
    hidden = owns[0].shape[2]
    rows = sum(own.shape[1] for own in owns)
    cut = rows // 32 * 16
    a, b = (2, cut, hidden), (2, rows - cut, hidden)
    outs = [
        (a, lambda i: i // 2),
        (a, lambda i: i // 2),
        (b, lambda i: jnp.minimum(i, 1)),
        (b, lambda i: jnp.maximum(i - 2, 0)),
    ]
    return call(
        functools.partial(first_sum_kernel, cut, len(owns)),
        4,
        [chip_slot(array.shape, lambda i: i) for array in (*owns, *gots)],
        [chip_slot(shape, index) for shape, index in outs],
        [shape_of(shape, jnp.bfloat16) for shape, _ in outs],
        4 * rows * hidden,
        24 * rows * hidden,
        "first_sum",
    )(*owns, *gots)


def second_sum(keep_a, got_a, keep_b, got_b):
    ins = (keep_a, got_a, keep_b, got_b)
    outs = [shape_of(array.shape[1:], jnp.bfloat16) for array in ins]
    return call(
        second_sum_kernel,
        1,
        [fixed(*array.shape) for array in ins],
        [fixed(*out.shape) for out in outs],
        outs,
        2 * keep_a.size,
        12 * keep_a.size,
        "second_sum",
    )(*ins)


def seq_split(where, folded_rows, vector_rows, *ins):
    count = lax.axis_size("seq")
    rows = sum(array.shape[0] for array in ins[:: 2 if len(ins) > 1 else 1])
    hidden = ins[0].shape[1]
    shape = (count, packed_depth(rows, count), hidden)
    return call(
        functools.partial(seq_split_kernel, folded_rows, vector_rows),
        1,
        [scalars()] + [fixed(*array.shape) for array in ins],
        fixed(*shape),
        shape_of(shape, jnp.bfloat16),
        rows * hidden,
        6 * rows * hidden,
        "seq_split",
    )(where, *ins)


def seq_exchange(split):
    return [split[0]] + [shifted(split[step], step) for step in range(1, split.shape[0])]


def last_sum(pieces, out_shapes):
    flat = [array for _, piece in pieces for array in piece]
    outs = [shape_of(shape, jnp.float32) for shape in out_shapes]
    return call(
        functools.partial(last_sum_kernel, [(name, len(piece)) for name, piece in pieces]),
        1,
        [fixed(*array.shape) for array in flat],
        [fixed(*shape) for shape in out_shapes],
        outs,
        4 * flat[0].size,
        8 * flat[0].size,
        "last_sum",
    )(*flat)


def dp_swapped(block, bit):
    count = lax.axis_size("dp")
    return lax.ppermute(block, "dp", [(i, i ^ (1 << bit)) for i in range(count)])


class Chain:
    def __init__(self, token):
        self.token = token

    def hold(self, *values):
        return lax.optimization_barrier((*values, self.token))[:-1]

    def step(self, function, *values):
        out = function(*self.hold(*values))
        self.token = out[0] if isinstance(out, (list, tuple)) else out
        return out


def shifted(block, step):
    count = lax.axis_size("seq")
    return lax.ppermute(block, "seq", [(i, (i + step) % count) for i in range(count)])


def weight_pack(block_number, device_shards):
    w_in, w_conv, w_out = (device_shards[i][block_number] for i in (2, 6, 10))
    width = w_in.shape[1]
    folds = w_out.shape[1] // width
    pieces = [w_in, w_conv.reshape(-1, width)]
    pieces += [w_out[:, i * width : (i + 1) * width] for i in range(folds)]
    return jnp.concatenate(pieces, axis=0)


def vector_pack(block_number, device_shards, width):
    order = (0, 1, 11, 3, 4, 5, 7, 8, 9)
    rows = [device_shards[i][block_number] for i in order]
    rows = [jnp.pad(row, (0, width - row.shape[0])) for row in rows]
    return jnp.pad(jnp.stack(rows), ((0, VECTOR_ROWS - len(rows)), (0, 0)))


def seq_gathered(packed):
    count = lax.axis_size("seq")
    me = lax.axis_index("seq")
    held = [packed] + [shifted(packed, step) for step in range(1, count)]
    ring = jnp.stack(held[::-1] + held[::-1])
    return lax.dynamic_slice_in_dim(ring, (count - 1 - me) % count, count, axis=0)


def folded_columns(out_parts):
    count, folds, depth, width = out_parts.shape
    per_fold = count // folds
    return (
        out_parts.reshape(folds, per_fold, folds, depth, width)
        .transpose(0, 3, 1, 2, 4)
        .reshape(folds * depth, per_fold * folds * width)
    )


def unfolded_columns(out_rows, folds, count):
    per_fold = count // folds
    depth = out_rows.shape[0] // folds
    width = out_rows.shape[1] // count
    return (
        out_rows.reshape(folds, depth, per_fold, folds, width)
        .transpose(0, 2, 3, 1, 4)
        .reshape(count, folds * depth, width)
    )


def pack_is_aligned(middle_rows):
    return middle_rows % 16 == 0


def gathered_params(block_number, device_shards, after=None):
    w_in, w_conv, w_out = (device_shards[i][block_number] for i in (2, 6, 10))
    first_rows = w_in.shape[0]
    taps, middle_rows, width = w_conv.shape
    folds = w_out.shape[1] // width
    count = lax.axis_size("seq")
    hidden = width * count
    by_seq = seq_gathered(weight_pack(block_number, device_shards))
    straight = first_rows + taps * middle_rows
    total = straight + folds * middle_rows
    upper = by_seq[:, :straight].transpose(1, 0, 2).reshape(straight, hidden)
    lower = folded_columns(by_seq[:, straight:].reshape(count, folds, middle_rows, width))
    vectors = vector_pack(block_number, device_shards, hidden)
    packed = jnp.concatenate([upper, lower, vectors])
    if after is not None:
        packed, after = lax.optimization_barrier((packed, after))
    whole = lax.all_gather(packed, "dp")
    tail = whole[:, total:].astype(jnp.float32)
    wide = tail[:, :3, :first_rows].transpose(1, 0, 2).reshape(3, -1)
    narrow = tail[:, 3:9, :middle_rows].transpose(1, 0, 2).reshape(6, -1)
    if not pack_is_aligned(middle_rows):
        bounds = [0, first_rows]
        bounds += [first_rows + (k + 1) * middle_rows for k in range(taps + folds)]
        whole = jnp.concatenate(
            [whole[:, a:b].reshape(1, -1, hidden) for a, b in zip(bounds, bounds[1:])], axis=1
        )
    return pack_weights(whole, wide, narrow)


def reduce_dp(grad_pack, wide_grads, narrow_grads):
    parts = lax.axis_size("dp")
    hidden = narrow_grads.shape[1]
    model = wide_grads.shape[1]
    first_rows = model // parts
    middle_rows = hidden // parts
    folds = model // hidden
    total = first_rows + (KER + folds) * middle_rows
    if not pack_is_aligned(middle_rows):
        bounds = [0, model] + [model + (k + 1) * hidden for k in range(KER + folds)]
        grad_pack = jnp.concatenate(
            [grad_pack[0, a:b].reshape(parts, -1, hidden) for a, b in zip(bounds, bounds[1:])]
            + [jnp.zeros((parts, VECTOR_ROWS, hidden), jnp.bfloat16)],
            axis=1,
        )
    vectors = jnp.concatenate(
        [
            jnp.pad(
                block.reshape(-1, parts, rows).transpose(1, 0, 2),
                ((0, 0), (0, 0), (0, hidden - rows)),
            )
            for block, rows in ((wide_grads, first_rows), (narrow_grads, middle_rows))
        ]
        + [jnp.zeros((parts, VECTOR_ROWS - 9, hidden), jnp.float32)],
        axis=1,
    ).astype(jnp.bfloat16)
    grad_pack = lax.dynamic_update_slice(grad_pack, vectors, (0, total, 0))
    return lax.psum_scatter(grad_pack, "dp", scatter_dimension=0, tiled=False)


def reduce_seq(mine, model, hidden):
    parts = lax.axis_size("dp")
    count = lax.axis_size("seq")
    me = lax.axis_index("seq")
    first_rows = model // parts
    middle_rows = hidden // parts
    width = hidden // count
    folds = model // hidden
    straight = first_rows + KER * middle_rows
    total = straight + folds * middle_rows
    upper = mine[:straight].reshape(straight, count, width).transpose(1, 0, 2)
    lower = unfolded_columns(mine[straight:total], folds, count)
    fold = -(-first_rows // width)
    tail = mine[total:, : fold * width].reshape(1, VECTOR_ROWS * fold, width)
    tail = jnp.broadcast_to(tail, (count,) + tail.shape[1:])
    ring = jnp.concatenate([upper, lower, tail], axis=1)
    ring = jnp.concatenate([ring, ring])
    ring = lax.dynamic_slice_in_dim(ring, me, count, axis=0)
    held = [ring[0]] + [shifted(ring[step], step) for step in range(1, count)]
    held = [block.astype(jnp.float32) for block in held]
    while len(held) > 1:
        half = len(held) // 2
        held = [held[i] + held[i + half] for i in range(half)]
    summed = held[0]
    last = summed[straight:total].reshape(folds, middle_rows, width).transpose(1, 0, 2)
    tail = summed[total:].reshape(VECTOR_ROWS, fold * width)
    return (
        summed[:first_rows],
        summed[first_rows:straight].reshape(KER, middle_rows, width),
        last.reshape(middle_rows, folds * width),
        tail[:3, :first_rows],
        tail[3:9, :middle_rows],
    )


def block_forward(inputs, weights, flags, dilation_step, next_dtype):
    rows, length, _ = flags.shape
    act_one, u, act_two = project(inputs, weights)
    tap_rows, conv_out, act_three, output = convolve(
        act_two.reshape(rows, length, -1), flags, inputs, weights, dilation_step, next_dtype
    )
    return output, (act_one, u, tap_rows, conv_out, act_three)


def block_backward(inputs, upstream, weights, kept, flags, dilation_step, before=None):
    act_one, u, tap_rows, conv_out, act_three = kept
    rows, length, _ = flags.shape
    short, gv, narrow_a, wide_a = out_back(upstream, conv_out, weights)
    pack = weights.first[0]
    grad_shape = shape_of(
        (pack.shape[0], sum(pack_rows(pack, inputs.shape[1], gv.shape[1])), gv.shape[1]),
        jnp.bfloat16,
    )
    grad_pack = weight_grads(tap_rows, gv, act_three, short, grad_shape)
    gu, result, narrow_b, wide_b = conv_back(
        gv.reshape(rows, length, -1), flags, u, inputs, upstream, weights, dilation_step
    )
    if before is not None:
        gu, before = lax.optimization_barrier((gu, before))
    grad_pack = in_grads(grad_pack, act_one, gu)
    wide = jnp.concatenate([wide_b[0:2], wide_a[0:1]])
    narrow = jnp.concatenate([narrow_b[0:3], narrow_a[0:3]])
    return result, reduce_dp(grad_pack, wide, narrow), before


def main_pack(w_conv, w_out):
    count = lax.axis_size("seq")
    depth, width = w_conv.shape[2:]
    rows = packed_depth((KER + w_out.shape[2] // width) * depth, count)
    out = shape_of((rows, width * count), jnp.bfloat16)
    return call(
        main_pack_kernel,
        1,
        [fixed(*w_conv.shape), fixed(*w_out.shape)],
        [fixed(*out.shape)] * 2,
        [out, out],
        out.size,
        8 * out.size,
        "main_pack",
    )(w_conv, w_out)


def lead_pack(w_in, wide, narrow):
    count = lax.axis_size("seq")
    hidden = w_in.shape[2] * count
    ins = (w_in, jnp.stack(wide, axis=1), jnp.stack(narrow, axis=1))
    rows = packed_depth(2 * w_in.shape[1], count)
    outs = [shape_of((n, hidden), jnp.bfloat16) for n in (rows, 2 * VECTOR_ROWS)]
    return call(
        lead_pack_kernel,
        1,
        [fixed(*array.shape) for array in ins],
        [fixed(*out.shape) for out in outs],
        outs,
        rows * hidden,
        8 * rows * hidden,
        "lead_pack",
    )(*ins)


def seq_shares(packed):
    return [packed] + [shifted(packed, step) for step in range(1, lax.axis_size("seq"))]


def seq_join(where, folded_rows, held, vectors=None):
    count = len(held)
    packed = held[0]
    extra = [] if vectors is None else [vectors]
    vector_rows = 0 if vectors is None else vectors.shape[0]
    rows = folded_rows[1] + vector_rows
    hidden = packed.shape[1]
    return call(
        functools.partial(seq_join_kernel, folded_rows, vector_rows),
        1,
        [scalars()] + [fixed(*array.shape) for array in held + extra],
        fixed(rows, hidden),
        shape_of((rows, hidden), jnp.bfloat16),
        rows * hidden,
        4 * rows * hidden,
        "seq_join",
        scratch=[pltpu.VMEM((count,) + packed.shape, jnp.bfloat16)],
    )(where, *held, *extra)


class Exchange:
    def __init__(self, block):
        self.block = block
        self.cut = block.shape[0] // 32 * 16
        a, b = block[: self.cut], block[self.cut :]
        got_a, got_b = lax.optimization_barrier((dp_swapped(a, 1), dp_swapped(b, 2)))
        self.near = (jnp.stack([a, got_a]), jnp.stack([b, got_b]))

    def finish(self, where, beside):
        rows, hidden = self.block.shape
        near_a, near_b = self.near
        far_a, far_b, *beside = lax.optimization_barrier(
            (dp_swapped(near_a, 2), dp_swapped(near_b, 1), *beside)
        )
        near = (near_a, far_a, near_b, far_b)
        ins = near + tuple(dp_swapped(share, 0) for share in near)
        parts = lax.axis_size("dp")
        return call(
            place_kernel,
            1,
            [scalars()] + [fixed(*array.shape) for array in ins],
            fixed(parts, rows, hidden),
            shape_of((parts, rows, hidden), jnp.bfloat16),
            parts * rows * hidden,
            4 * parts * rows * hidden,
            "place",
        )(where, *ins), beside


def after(value, *earlier):
    return lax.optimization_barrier((value, *earlier))[0]


def exchanged_weights(where, shards):
    w_in, w_conv, w_out = shards[2], shards[6], shards[10]
    first_rows = w_in.shape[1]
    depth, width = w_conv.shape[2:]
    folds = w_out.shape[2] // width
    folded = (KER * depth, (KER + folds) * depth)
    plain = (2 * first_rows, 2 * first_rows)
    early, late = main_pack(w_conv, w_out)
    wide = [shards[i] for i in (0, 1, 11)]
    lead, vectors = lead_pack(w_in, wide, [shards[i] for i in (3, 4, 5, 7, 8, 9)])

    early = seq_join(where, folded, seq_shares(early))
    early_whole = lax.all_gather(early, "dp")
    exchange = Exchange(seq_join(where, plain, seq_shares(after(lead, early)), vectors))
    late = seq_shares(after(late, *exchange.near))
    lead, late = exchange.finish(where, late)
    late = seq_join(where, folded, late)
    late_whole = lax.all_gather(after(late, early_whole), "dp")

    tail = lead[:, 2 * first_rows :].astype(jnp.float32)
    out = []
    for block, whole in ((0, early_whole), (1, late_whole)):
        start = block * VECTOR_ROWS
        wide = tail[:, start : start + 3, :first_rows].transpose(1, 0, 2).reshape(3, -1)
        narrow = tail[:, start + 3 : start + 9, :depth].transpose(1, 0, 2).reshape(6, -1)
        units = [(whole, i) for i in range(KER + folds)]
        out.append(Weights((lead, block), units[:KER], units[KER:], wide, narrow))
    return out


def exchanged_backward(inputs, weights, kept, flags, dilations, cotangent, out_shapes):
    where = place()
    parts = lax.axis_size("dp")
    hidden = weights[1].hidden
    model = inputs[0].shape[1]
    depth = hidden // parts
    folded = (KER * depth, (KER + model // hidden) * depth)
    rows, length, _ = flags[0].shape

    act_one, u, tap_rows, conv_out, act_three = kept[1]
    short, gv, *out_sums_late = out_back(cotangent, conv_out, weights[1])
    blocks = gv.reshape(rows, length, -1)
    halos = seq_neighbours(blocks, KER // 2 * dilations[1])
    pack_shape = shape_of((parts, folded[1], hidden), jnp.bfloat16)
    pack = weight_grads(tap_rows, gv, act_three, short, pack_shape, 0)
    pack, low, high = lax.optimization_barrier((pack, *halos))
    late_sum = lax.psum_scatter(pack, "dp", scatter_dimension=0, tiled=False)
    gu, middle_grad, *in_sums_late = conv_back_with(
        low, blocks, high, flags[1], u, inputs[1], cotangent, weights[1], dilations[1]
    )
    chain = Chain(gu)
    own_first, other_first = chain.step(
        lambda *values: share_in_grads(where, *values, ()), act_one, gu
    )

    act_one, u, tap_rows, conv_out, act_three = kept[0]
    short, gv, *out_sums = chain.step(
        lambda value: out_back(value, conv_out, weights[0]), middle_grad
    )
    blocks = gv.reshape(rows, length, -1)
    halos = seq_neighbours(blocks, KER // 2 * dilations[0])
    own_taps, other_taps = share_grads(where, tap_rows, gv, act_three, short)
    low, high, own_taps, other_taps, other_first = lax.optimization_barrier(
        (*halos, own_taps, other_taps, other_first)
    )
    got_taps, got_first = dp_swapped(other_taps, 0), dp_swapped(other_first, 0)
    gu, input_grad, *in_sums = chain.step(
        lambda low, high: conv_back_with(
            low, blocks, high, flags[0], u, inputs[0], middle_grad, weights[0], dilations[0]
        ),
        low,
        high,
    )

    def first_round(sums):
        keep_a, send_a, keep_b, send_b = sums
        return keep_a, dp_swapped(send_a, 1), keep_b, dp_swapped(send_b, 2)

    def second_round(sums):
        kept_a, send_a, kept_b, send_b = sums
        return kept_a, dp_swapped(send_a, 2), kept_b, dp_swapped(send_b, 1)

    all_sums = (*out_sums, *in_sums, *out_sums_late, *in_sums_late)
    own, other = chain.step(
        lambda a, b: share_in_grads(where, a, b, all_sums), act_one, gu
    )
    owns = (own_taps, own_first, own)
    gots = (got_taps, got_first, dp_swapped(other, 0))
    main = first_round(
        chain.step(lambda *values: first_sum(values[:3], values[3:]), *owns, *gots)
    )
    late = seq_exchange(chain.step(lambda value: seq_split(where, folded, 0, value), late_sum))
    main, late = lax.optimization_barrier((main, late))
    main = second_round(second_sum(*main))
    main = seq_exchange(seq_split(where, folded, 2 * VECTOR_ROWS, *main))
    return input_grad, last_sum((("early", main), ("late", late)), out_shapes)


def pack_rows(pack, model, hidden):
    parts = pack.shape[0]
    extra = VECTOR_ROWS if pack_is_aligned(hidden // lax.axis_size("dp")) else 0
    return model // parts, (KER * hidden + model) // parts, extra


def local(
    tokens,
    protein_lengths,
    norm1_gain,
    norm1_bias,
    w_in,
    in_bias,
    norm2_gain,
    norm2_bias,
    w_conv,
    conv_bias,
    norm3_gain,
    norm3_bias,
    w_out,
    out_bias,
    cotangent,
):
    device_shards = (
        norm1_gain,
        norm1_bias,
        w_in,
        in_bias,
        norm2_gain,
        norm2_bias,
        w_conv,
        conv_bias,
        norm3_gain,
        norm3_bias,
        w_out,
        out_bias,
    )
    rows, seq_len, model = tokens.shape
    token_positions = lax.axis_index("seq") * seq_len + jnp.arange(seq_len, dtype=jnp.int32)
    early_flags = kernel_tap_flags(protein_lengths, token_positions, FIRST_DILATION)
    later_flags = kernel_tap_flags(protein_lengths, token_positions, SECOND_DILATION)
    parts = lax.axis_size("dp")
    fast = parts == 8 and pack_is_aligned(in_bias.shape[1])
    if fast:
        early_weights, late_weights = exchanged_weights(place(), device_shards)
    else:
        early_weights = gathered_params(0, device_shards)
        late_weights = gathered_params(1, device_shards, early_weights.first[0])
    flat_tokens = tokens.reshape(rows * seq_len, model)
    middle, early_kept = block_forward(
        flat_tokens, early_weights, early_flags, FIRST_DILATION, jnp.float32
    )
    output, late_kept = block_forward(
        middle, late_weights, later_flags, SECOND_DILATION, jnp.bfloat16
    )
    hidden = early_weights.hidden
    if fast:
        shapes = [w.shape for w in (w_in, w_conv, w_out, norm1_gain, norm1_bias, out_bias)]
        shapes += [w.shape for w in (in_bias, norm2_gain, norm2_bias)]
        shapes += [w.shape for w in (conv_bias, norm3_gain, norm3_bias)]
        input_grad, grads = exchanged_backward(
            (flat_tokens, middle),
            (early_weights, late_weights),
            (early_kept, late_kept),
            (early_flags, later_flags),
            (FIRST_DILATION, SECOND_DILATION),
            cotangent.reshape(rows * seq_len, model),
            shapes,
        )
        order = (3, 4, 0, 6, 7, 8, 1, 9, 10, 11, 2, 5)
        return (
            output.reshape(tokens.shape),
            input_grad.reshape(tokens.shape),
            *(grads[i] for i in order),
        )
    middle_grad, mine_late, _ = block_backward(
        middle,
        cotangent.reshape(rows * seq_len, model),
        late_weights,
        late_kept,
        later_flags,
        SECOND_DILATION,
    )
    input_grad, mine_early, mine_late = block_backward(
        flat_tokens,
        middle_grad,
        early_weights,
        early_kept,
        early_flags,
        FIRST_DILATION,
        mine_late,
    )
    reduced_late = reduce_seq(mine_late, model, hidden)
    reduced_early = reduce_seq(mine_early, model, hidden)
    first_early, middle_early, last_early, wide_early, narrow_early = reduced_early
    first_late, middle_late, last_late, wide_late, narrow_late = reduced_late
    return (
        output.reshape(tokens.shape),
        input_grad.reshape(tokens.shape),
        jnp.stack([wide_early[0], wide_late[0]]),
        jnp.stack([wide_early[1], wide_late[1]]),
        jnp.stack([first_early, first_late]),
        jnp.stack([narrow_early[0], narrow_late[0]]),
        jnp.stack([narrow_early[1], narrow_late[1]]),
        jnp.stack([narrow_early[2], narrow_late[2]]),
        jnp.stack([middle_early, middle_late]),
        jnp.stack([narrow_early[3], narrow_late[3]]),
        jnp.stack([narrow_early[4], narrow_late[4]]),
        jnp.stack([narrow_early[5], narrow_late[5]]),
        jnp.stack([last_early, last_late]),
        jnp.stack([wide_early[2], wide_late[2]]),
    )


def solution(mesh):
    placed = (
        P("dp", "seq", None),
        P("dp", None),
        P(None, "dp"),
        P(None, "dp"),
        P(None, "dp", "seq"),
        P(None, "dp"),
        P(None, "dp"),
        P(None, "dp"),
        P(None, None, "dp", "seq"),
        P(None, "dp"),
        P(None, "dp"),
        P(None, "dp"),
        P(None, "dp", "seq"),
        P(None, "dp"),
        P("dp", "seq", None),
    )
    return jax.shard_map(
        local,
        mesh=mesh,
        in_specs=placed,
        out_specs=(
            P("dp", "seq", None),
            P("dp", "seq", None),
            P(None, "dp"),
            P(None, "dp"),
            P(None, "dp", "seq"),
            P(None, "dp"),
            P(None, "dp"),
            P(None, "dp"),
            P(None, None, "dp", "seq"),
            P(None, "dp"),
            P(None, "dp"),
            P(None, "dp"),
            P(None, "dp", "seq"),
            P(None, "dp"),
        ),
        check_vma=False,
    )
```

```python
import functools
import math

import jax
import jax.numpy as jnp
from jax import lax
from jax.experimental import pallas as pl
from jax.experimental.pallas import tpu as pltpu
from jax.sharding import PartitionSpec as P

KER = 5
FIRST_DILATION = 64
SECOND_DILATION = 128


epsilon = 1e-05
CUBIC = 0.044715
SLOPE = math.sqrt(2.0 / math.pi)
VECTOR_ROWS = 16


def seq_neighbours(block, width):
    count = lax.axis_size("seq")
    forward = [(i, i + 1) for i in range(count - 1)]
    backward = [(target, source) for source, target in forward]
    low = lax.ppermute(block[:, block.shape[1] - width :], "seq", forward)
    high = lax.ppermute(block[:, :width], "seq", backward)
    return low, high


def normalized(values):
    centred = values - jnp.mean(values, -1, keepdims=True)
    scale = lax.rsqrt(jnp.mean(centred * centred, -1, keepdims=True) + epsilon)
    return centred * scale, scale


def gelu(h):
    return 0.5 * h * (1.0 + jnp.tanh(SLOPE * (h + CUBIC * (h * h * h))))


def norm_gelu(values, gain_vector, bias_vector):
    return gelu(normalized(values)[0] * gain_vector + bias_vector)


def norm_gelu_back(incoming, values, gain_vector, bias_vector):
    n, scale = normalized(values)
    h = n * gain_vector + bias_vector
    square = h * h
    t = jnp.tanh(SLOPE * (h + CUBIC * (square * h)))
    slope = 0.5 * (1.0 + t) + (0.5 * SLOPE) * h * (1.0 - t * t) * (1.0 + (3.0 * CUBIC) * square)
    dh = incoming * slope
    dn = dh * gain_vector
    back = dn - jnp.mean(dn, -1, keepdims=True) - n * jnp.mean(dn * n, -1, keepdims=True)
    return back * scale, column_sum(dh * n), column_sum(dh)


def column_sum(values):
    return jnp.sum(values, axis=0, keepdims=True)


def matmul(left, right):
    return jnp.dot(left, right, preferred_element_type=jnp.float32)


def matmul_back(left, right):
    return lax.dot_general(
        left, right, (((1,), (1,)), ((), ())), preferred_element_type=jnp.float32
    )


def matmul_rows(left, right):
    return lax.dot_general(
        left, right, (((0,), (0,)), ((), ())), preferred_element_type=jnp.float32
    )


def merged(ref):
    parts, rows, columns = ref.shape
    return ref[...].reshape(parts * rows, columns)


def kernel_tap_flags(lengths, token_positions, dilation_step):
    doc_ends = jnp.cumsum(lengths, axis=1)
    row_total = doc_ends[:, -1:]
    where_pos = token_positions[None, :, None]
    finished = doc_ends[:, None, :] <= where_pos
    doc_start = jnp.sum(jnp.where(finished, lengths[:, None, :], 0), axis=2)
    doc_stop = jnp.min(jnp.where(finished, row_total[:, :, None] + 1, doc_ends[:, None, :]), axis=2)
    is_live = token_positions[None, :] < row_total
    flag_list = []
    for tap_index in range(KER):
        target = token_positions[None, :] + (tap_index - KER // 2) * dilation_step
        flag_list.append(is_live & (target >= doc_start) & (target < doc_stop))
    flag_list += [flag_list[-1]] * (8 - KER)
    return jnp.stack(flag_list, axis=2).astype(jnp.bfloat16)


def project_kernel(x_ref, w_ref, wide_ref, narrow_ref, act_one_ref, u_ref, act_two_ref):
    act_one = norm_gelu(
        x_ref[...].astype(jnp.float32), wide_ref[0:1, :], wide_ref[1:2, :]
    ).astype(jnp.bfloat16)
    act_one_ref[...] = act_one
    u = matmul(act_one, merged(w_ref)) + narrow_ref[0:1, :]
    u_ref[...] = u
    act_two_ref[...] = norm_gelu(u, narrow_ref[1:2, :], narrow_ref[2:3, :]).astype(jnp.bfloat16)


def tap_slices(low_ref, own_ref, high_ref, flag_ref, dilation_step):
    length = own_ref.shape[1]
    width = low_ref.shape[1]
    padded = jnp.concatenate([low_ref[0], own_ref[0], high_ref[0]], axis=0)
    for k in range(KER):
        start = width + (k - KER // 2) * dilation_step
        yield k, padded[start : start + length] * flag_ref[0][:, k : k + 1]


def convolve_kernel(
    dilation_step,
    low_ref,
    own_ref,
    high_ref,
    flag_ref,
    x_ref,
    k0_ref,
    k1_ref,
    k2_ref,
    k3_ref,
    k4_ref,
    left_ref,
    right_ref,
    wide_ref,
    narrow_ref,
    tap_ref,
    v_ref,
    act_three_ref,
    next_ref,
):
    taps = (k0_ref, k1_ref, k2_ref, k3_ref, k4_ref)
    hidden = own_ref.shape[2]
    total = narrow_ref[3:4, :]
    for k, piece in tap_slices(low_ref, own_ref, high_ref, flag_ref, dilation_step):
        tap_ref[:, k * hidden : (k + 1) * hidden] = piece
        total = total + matmul(piece, merged(taps[k]))
    v_ref[...] = total
    act_three = norm_gelu(total, narrow_ref[4:5, :], narrow_ref[5:6, :]).astype(jnp.bfloat16)
    act_three_ref[...] = act_three
    for i, half_ref in enumerate((left_ref, right_ref)):
        columns = slice(i * hidden, (i + 1) * hidden)
        branch = matmul(act_three, merged(half_ref)) + wide_ref[2:3, columns]
        next_ref[:, columns] = (x_ref[:, columns].astype(jnp.float32) + branch).astype(
            next_ref.dtype
        )


def out_back_kernel(
    g_ref, v_ref, left_ref, right_ref, narrow_ref, short_ref, gv_ref, narrow_sum_ref, wide_sum_ref
):
    hidden = v_ref.shape[1]

    @pl.when(pl.program_id(0) == 0)
    def _():
        narrow_sum_ref[...] = jnp.zeros_like(narrow_sum_ref)
        wide_sum_ref[...] = jnp.zeros_like(wide_sum_ref)

    short = g_ref[...].astype(jnp.bfloat16)
    short_ref[...] = short
    wide_sum_ref[0:1, :] += column_sum(short.astype(jnp.float32))
    incoming = matmul_back(short[:, :hidden], merged(left_ref))
    incoming = incoming + matmul_back(short[:, hidden:], merged(right_ref))
    gv, gain_sum, bias_sum = norm_gelu_back(
        incoming, v_ref[...], narrow_ref[4:5, :], narrow_ref[5:6, :]
    )
    gv = gv.astype(jnp.bfloat16)
    gv_ref[...] = gv
    narrow_sum_ref[0:1, :] += column_sum(gv.astype(jnp.float32))
    narrow_sum_ref[1:2, :] += gain_sum
    narrow_sum_ref[2:3, :] += bias_sum


def weight_grad_kernel(tap_ref, gv_ref, act_three_ref, short_ref, pack_ref):
    step = pl.program_id(0)

    def store(value):
        pack_ref[...] = value.astype(jnp.bfloat16).reshape(pack_ref.shape)

    @pl.when(step < KER)
    def _():
        store(matmul_rows(tap_ref[...], gv_ref[...]))

    @pl.when(step >= KER)
    def _():
        store(matmul_rows(act_three_ref[...], short_ref[...]))


def conv_back_kernel(
    dilation_step,
    low_ref,
    own_ref,
    high_ref,
    flag_ref,
    u_ref,
    x_ref,
    g_ref,
    k0_ref,
    k1_ref,
    k2_ref,
    k3_ref,
    k4_ref,
    w_ref,
    wide_ref,
    narrow_ref,
    gu_ref,
    next_ref,
    narrow_sum_ref,
    wide_sum_ref,
):
    @pl.when(pl.program_id(0) == 0)
    def _():
        narrow_sum_ref[...] = jnp.zeros_like(narrow_sum_ref)
        wide_sum_ref[...] = jnp.zeros_like(wide_sum_ref)

    taps = (k0_ref, k1_ref, k2_ref, k3_ref, k4_ref)
    total = None
    for k, piece in tap_slices(low_ref, own_ref, high_ref, flag_ref, dilation_step):
        term = matmul_back(piece, merged(taps[KER - 1 - k]))
        total = term if total is None else total + term
    gu, gain_sum, bias_sum = norm_gelu_back(
        total, u_ref[...], narrow_ref[1:2, :], narrow_ref[2:3, :]
    )
    gu = gu.astype(jnp.bfloat16)
    gu_ref[...] = gu
    narrow_sum_ref[0:1, :] += column_sum(gu.astype(jnp.float32))
    narrow_sum_ref[1:2, :] += gain_sum
    narrow_sum_ref[2:3, :] += bias_sum
    gx, gain_sum, bias_sum = norm_gelu_back(
        matmul_back(gu, merged(w_ref)),
        x_ref[...].astype(jnp.float32),
        wide_ref[0:1, :],
        wide_ref[1:2, :],
    )
    next_ref[...] = g_ref[...].astype(jnp.float32) + gx
    wide_sum_ref[0:1, :] += gain_sum
    wide_sum_ref[1:2, :] += bias_sum


def in_grad_kernel(pack_in_ref, act_one_ref, gu_ref, pack_ref):
    value = matmul_rows(act_one_ref[...], gu_ref[...])
    pack_ref[...] = value.astype(jnp.bfloat16).reshape(pack_ref.shape)


def spread(rows, place_ref, hold_ref, own_ref, other_ref):
    chip, core = place_ref[0] // 2, place_ref[0] % 2
    for i in range(own_ref.shape[0]):
        at = 2 * (chip ^ i)
        own_ref[i] = hold_ref[at + core, rows]
        other_ref[i] = hold_ref[at + 1 - core, rows]


def share_grad_kernel(
    place_ref, tap_ref, gv_ref, act_three_ref, short_ref, own_ref, other_ref, hold_ref
):
    step = pl.program_id(0)

    def store(value):
        hold_ref[...] = value.astype(jnp.bfloat16).reshape(hold_ref.shape)

    @pl.when(step < KER)
    def _():
        store(matmul_rows(tap_ref[...], gv_ref[...]))

    @pl.when(step >= KER)
    def _():
        store(matmul_rows(act_three_ref[...], short_ref[...]))

    spread(slice(None), place_ref, hold_ref, own_ref, other_ref)


def share_in_kernel(place_ref, act_one_ref, gu_ref, *refs):
    *sum_refs, own_ref, other_ref, hold_ref = refs
    parts = hold_ref.shape[0]
    hidden = gu_ref.shape[1]
    depth = act_one_ref.shape[1] // parts
    value = matmul_rows(act_one_ref[...], gu_ref[...]).astype(jnp.bfloat16)
    hold_ref[:, :depth, :] = value.reshape(parts, depth, hidden)
    for block in range(len(sum_refs) // 4):
        narrow_a, wide_a, narrow_b, wide_b = (ref[...] for ref in sum_refs[4 * block : 4 * block + 4])
        wide = jnp.concatenate([wide_b[0:2], wide_a[0:1]], axis=0)
        narrow = jnp.concatenate([narrow_b[0:3], narrow_a[0:3]], axis=0)
        narrow_depth = hidden // parts
        for part in range(parts):
            rows = [
                wide[:, part * depth : (part + 1) * depth],
                jnp.concatenate(
                    [
                        narrow[:, part * narrow_depth : (part + 1) * narrow_depth],
                        jnp.zeros((6, depth - narrow_depth), jnp.float32),
                    ],
                    axis=1,
                ),
                jnp.zeros((VECTOR_ROWS - 9, depth), jnp.float32),
            ]
            rows = jnp.concatenate(rows, axis=0)
            rows = jnp.concatenate(
                [rows, jnp.zeros((VECTOR_ROWS, hidden - depth), jnp.float32)], axis=1
            )
            start = depth + block * VECTOR_ROWS
            hold_ref[part, start : start + VECTOR_ROWS, :] = rows.astype(jnp.bfloat16)
    spread(slice(None), place_ref, hold_ref, own_ref, other_ref)


def plus(left, right):
    return left.astype(jnp.float32) + right.astype(jnp.float32)


def first_sum_kernel(cut, count, *refs):
    step = pl.program_id(0)
    keep_a, send_a, keep_b, send_b = refs[2 * count :]
    pieces = [
        plus(own[0], got[0]).astype(jnp.bfloat16) for own, got in zip(refs[:count], refs[count:])
    ]
    total = pieces[0] if count == 1 else jnp.concatenate(pieces, axis=0)
    upper, lower = total[:cut], total[cut:]

    @pl.when(step % 2 == 0)
    def _():
        keep_a[0] = upper

    @pl.when(step % 2 == 1)
    def _():
        send_a[0] = upper

    @pl.when(step < 2)
    def _():
        keep_b[0] = lower

    @pl.when(step >= 2)
    def _():
        send_b[0] = lower


def second_sum_kernel(keep_a, got_a, keep_b, got_b, kept_a, send_a, kept_b, send_b):
    for keep, got, kept, send in (
        (keep_a, got_a, kept_a, send_a),
        (keep_b, got_b, kept_b, send_b),
    ):
        kept[...] = plus(keep[0], got[0]).astype(jnp.bfloat16)
        send[...] = plus(keep[1], got[1]).astype(jnp.bfloat16)


def lane_packed(rows, depth, count):
    missing = count * depth - rows.shape[0]
    if missing:
        rows = jnp.concatenate([rows, jnp.zeros((missing, rows.shape[1]), rows.dtype)], axis=0)
    return jnp.concatenate([rows[i * depth : (i + 1) * depth] for i in range(count)], axis=1)


def lane_unpacked(packed, count):
    width = packed.shape[1] // count
    return jnp.concatenate([packed[:, i * width : (i + 1) * width] for i in range(count)], axis=0)


def packed_depth(rows, count):
    return -(-rows // (16 * count)) * 16


def seq_split_kernel(folded_rows, vector_rows, place_ref, *refs):
    *in_refs, out_ref = refs
    if len(in_refs) == 1:
        total = in_refs[0][...]
    else:
        halves = [plus(in_refs[i][...], in_refs[i + 1][...]) for i in range(0, len(in_refs), 2)]
        total = jnp.concatenate(halves, axis=0)
    total = total.astype(jnp.float32)
    count, width = out_ref.shape[0], total.shape[1] // out_ref.shape[0]
    rows = total.shape[0]
    at, end = folded_rows
    fold = (end - at) // 2
    for s in range(count):
        columns = total[:, s * width : (s + 1) * width]
        if end > at:
            unit = at + (s // 2) * fold
            left = (s % 2) * 2 * width
            pair = total[unit : unit + fold, left : left + 2 * width]
            pieces = [columns[:at], pair[:, :width], pair[:, width:], columns[end:]]
            columns = jnp.concatenate([p for p in pieces if p.shape[0]], axis=0)
        if vector_rows:
            columns = jnp.concatenate(
                [columns[: rows - vector_rows], total[rows - vector_rows :, :width]], axis=0
            )
        packed = lane_packed(columns, out_ref.shape[1], count)
        out_ref[(s - place_ref[1] + count) % count] = packed.astype(jnp.bfloat16)


def last_sum_kernel(layout, *refs):
    sums = {}
    at = 0
    for name, count in layout:
        own, one, two, three = (ref[...].astype(jnp.float32) for ref in refs[at : at + 4])
        at += 4
        sums[name] = lane_unpacked((own + two) + (one + three), 4)
    first_ref, taps_ref, last_ref = refs[at : at + 3]
    vector_refs = refs[at + 3 :]
    depth = taps_ref.shape[2]
    straight = KER * depth
    first_rows = first_ref.shape[1]
    for block, piece in ((0, sums["early"]), (1, sums["late"])):
        for k in range(KER):
            taps_ref[block, k] = piece[k * depth : (k + 1) * depth]
        last_ref[block] = jnp.concatenate(
            [piece[straight : straight + depth], piece[straight + depth : straight + 2 * depth]],
            axis=1,
        )
    rest = sums["early"][straight + 2 * depth :]
    first_ref[0] = rest[first_rows : 2 * first_rows]
    first_ref[1] = rest[:first_rows]
    for block in range(2):
        start = 2 * first_rows + block * VECTOR_ROWS
        for i, ref in enumerate(vector_refs):
            row = rest[start + i : start + i + 1]
            ref[block : block + 1, :] = row[:, : ref.shape[1]]


def shard_pack_kernel(w_in, w_conv, w_out, lead_ref, early_ref, late_ref):
    count = lead_ref.shape[1] // w_in.shape[2]
    lead = jnp.concatenate([w_in[0], w_in[1]], axis=0)
    lead_ref[...] = lane_packed(lead, lead_ref.shape[0], count)
    width = w_conv.shape[3]
    count = early_ref.shape[1] // width
    for block, ref in ((0, early_ref), (1, late_ref)):
        rows = [w_conv[block, k] for k in range(KER)]
        rows += [w_out[block][:, :width], w_out[block][:, width:]]
        ref[...] = lane_packed(jnp.concatenate(rows, axis=0), ref.shape[0], count)


def vector_pack_kernel(wide, narrow, vector_ref):
    hidden = vector_ref.shape[1]
    for block in range(2):
        rows = []
        for ref in (wide, narrow):
            part = ref[block].astype(jnp.float32)
            rows.append(
                jnp.concatenate(
                    [part, jnp.zeros((part.shape[0], hidden - part.shape[1]), jnp.float32)], axis=1
                )
            )
        rows.append(jnp.zeros((VECTOR_ROWS - 9, hidden), jnp.float32))
        start = block * VECTOR_ROWS
        vector_ref[start : start + VECTOR_ROWS, :] = jnp.concatenate(rows, axis=0).astype(
            jnp.bfloat16
        )


def seq_join_kernel(folded_rows, vector_rows, place_ref, *refs):
    *in_refs, out_ref, hold_ref = refs
    vector_in = in_refs.pop() if vector_rows else None
    count = len(in_refs)
    for step, ref in enumerate(in_refs):
        hold_ref[(place_ref[1] - step + count) % count] = ref[...]
    shares = [lane_unpacked(hold_ref[s], count) for s in range(count)]
    rows = out_ref.shape[0] - vector_rows
    at, end = folded_rows
    if at:
        out_ref[:at, :] = jnp.concatenate([share[:at] for share in shares], axis=1)
    if end > at:
        fold = (end - at) // 2
        for half in range(2):
            columns = []
            for share in shares[half * count // 2 : (half + 1) * count // 2]:
                columns += [share[at : at + fold], share[at + fold : end]]
            start = at + half * fold
            out_ref[start : start + fold, :] = jnp.concatenate(columns, axis=1)
    if vector_in is not None:
        out_ref[rows:, :] = vector_in[...]


def place_kernel(place_ref, *refs):
    *in_refs, out_ref = refs
    chip, core = place_ref[0] // 2, place_ref[0] % 2
    cut = in_refs[0].shape[1]
    for at, share_core in ((0, core), (4, 1 - core)):
        near_a, far_a, near_b, far_b = in_refs[at : at + 4]
        for i in range(2):
            out_ref[2 * (chip ^ i) + share_core, :cut] = near_a[i]
            out_ref[2 * (chip ^ (2 + i)) + share_core, :cut] = far_a[i]
            out_ref[2 * (chip ^ (2 * i)) + share_core, cut:] = near_b[i]
            out_ref[2 * (chip ^ (2 * i + 1)) + share_core, cut:] = far_b[i]


def tiled(rows, columns):
    return pl.BlockSpec((rows, columns), lambda i: (i, 0))


def fixed(*shape):
    return pl.BlockSpec(shape, lambda i: (0,) * len(shape))


def row_block(shape):
    return pl.BlockSpec((1,) + shape[1:], lambda i: (i, 0, 0))


def pack_block(parts, rows, columns, index):
    return pl.BlockSpec((parts, rows, columns), lambda i: (0, index, 0))


def cost(flops, width):
    return pl.CostEstimate(flops=flops, bytes_accessed=width, transcendentals=0)


def call(kernel, grid, in_specs, out_specs, out_shape, flops, moved, name, aliases=None, scratch=()):
    return pl.pallas_call(
        kernel,
        grid=(grid,),
        in_specs=in_specs,
        out_specs=out_specs,
        out_shape=out_shape,
        scratch_shapes=list(scratch),
        input_output_aliases=aliases or {},
        cost_estimate=cost(flops, moved),
        compiler_params=pltpu.CompilerParams(vmem_limit_bytes=32 * 1024 * 1024),
        name=name,
    )


def shape_of(shape, dtype):
    return jax.ShapeDtypeStruct(shape, dtype)


class Weights:
    def __init__(self, first, taps, last, wide, narrow):
        self.first, self.taps, self.last = first, taps, last
        self.wide, self.narrow = wide, narrow
        self.model, self.hidden = wide.shape[1], narrow.shape[1]

    def first_spec(self):
        array, index = self.first
        return pack_block(array.shape[0], self.model // array.shape[0], self.hidden, index)

    def specs(self, units):
        return [
            pack_block(array.shape[0], self.hidden // array.shape[0], self.hidden, index)
            for array, index in units
        ]


def arrays(units):
    return [array for array, _ in units]


def pack_weights(pack, wide, narrow):
    folds = wide.shape[1] // narrow.shape[1]
    units = [(pack, folds + i) for i in range(KER + folds)]
    return Weights((pack, 0), units[:KER], units[KER:], wide, narrow)


class Sizes:
    def __init__(self, pack, model, hidden):
        self.parts = pack.shape[0]
        self.model, self.hidden = model, hidden
        self.first_rows = model // self.parts
        self.middle_rows = hidden // self.parts
        self.folds = model // hidden
        self.conv_at = self.first_rows // self.middle_rows

    def first(self):
        return pack_block(self.parts, self.first_rows, self.hidden, 0)


def project(inputs, weights):
    tokens, model = inputs.shape
    hidden = weights.hidden
    tile = min(128, tokens)
    return call(
        project_kernel,
        tokens // tile,
        [tiled(tile, model), weights.first_spec(), fixed(3, model), fixed(6, hidden)],
        [tiled(tile, model), tiled(tile, hidden), tiled(tile, hidden)],
        [
            shape_of((tokens, model), jnp.bfloat16),
            shape_of((tokens, hidden), jnp.float32),
            shape_of((tokens, hidden), jnp.bfloat16),
        ],
        4 * tokens * model * hidden,
        12 * tokens * model,
        "project",
    )(inputs, weights.first[0], weights.wide, weights.narrow)


def convolve(act_two, halos, flags, inputs, weights, dilation_step, next_dtype):
    rows, length, hidden = act_two.shape
    tokens, model = inputs.shape
    low, high = halos
    return call(
        functools.partial(convolve_kernel, dilation_step),
        rows,
        [
            row_block(low.shape),
            row_block(act_two.shape),
            row_block(high.shape),
            row_block(flags.shape),
            tiled(length, model),
            *weights.specs(weights.taps + weights.last),
            fixed(3, model),
            fixed(6, hidden),
        ],
        [
            tiled(length, KER * hidden),
            tiled(length, hidden),
            tiled(length, hidden),
            tiled(length, model),
        ],
        [
            shape_of((tokens, KER * hidden), jnp.bfloat16),
            shape_of((tokens, hidden), jnp.float32),
            shape_of((tokens, hidden), jnp.bfloat16),
            shape_of((tokens, model), next_dtype),
        ],
        2 * tokens * hidden * (KER * hidden + model),
        16 * tokens * model,
        "convolve",
    )(
        low,
        act_two,
        high,
        flags,
        inputs,
        *arrays(weights.taps + weights.last),
        weights.wide,
        weights.narrow,
    )


def out_back(upstream, conv_out, weights):
    tokens, model = upstream.shape
    hidden = weights.hidden
    tile = min(128, tokens)
    return call(
        out_back_kernel,
        tokens // tile,
        [
            tiled(tile, model),
            tiled(tile, hidden),
            *weights.specs(weights.last),
            fixed(6, hidden),
        ],
        [tiled(tile, model), tiled(tile, hidden), fixed(8, hidden), fixed(8, model)],
        [
            shape_of((tokens, model), jnp.bfloat16),
            shape_of((tokens, hidden), jnp.bfloat16),
            shape_of((8, hidden), jnp.float32),
            shape_of((8, model), jnp.float32),
        ],
        4 * tokens * model * hidden,
        10 * tokens * model,
        "out_back",
    )(upstream, conv_out, *arrays(weights.last), weights.narrow)


def weight_grads(tap_rows, gv, act_three, short, pack, conv_at=None):
    tokens, hidden = gv.shape
    model = short.shape[1]
    sizes = Sizes(pack, model, hidden)
    conv_at = sizes.conv_at if conv_at is None else conv_at
    whole = pl.BlockSpec((tokens, hidden), lambda s: (0, 0))
    return call(
        weight_grad_kernel,
        KER + sizes.folds,
        [
            pl.BlockSpec((tokens, hidden), lambda s: (0, jnp.minimum(s, KER - 1))),
            whole,
            whole,
            pl.BlockSpec((tokens, hidden), lambda s: (0, jnp.maximum(s - KER, 0))),
        ],
        pl.BlockSpec(
            (sizes.parts, sizes.middle_rows, hidden), lambda s: (0, conv_at + s, 0)
        ),
        shape_of(pack.shape, jnp.bfloat16),
        2 * tokens * hidden * (KER * hidden + model),
        8 * tokens * model,
        "weight_grads",
    )(tap_rows, gv, act_three, short)


def conv_back(gv, flags, u, inputs, upstream, weights, dilation_step):
    low, high = seq_neighbours(gv, KER // 2 * dilation_step)
    return conv_back_with(low, gv, high, flags, u, inputs, upstream, weights, dilation_step)


def conv_back_with(low, gv, high, flags, u, inputs, upstream, weights, dilation_step):
    rows, length, hidden = gv.shape
    tokens, model = inputs.shape
    return call(
        functools.partial(conv_back_kernel, dilation_step),
        rows,
        [
            row_block(low.shape),
            row_block(gv.shape),
            row_block(high.shape),
            row_block(flags.shape),
            tiled(length, hidden),
            tiled(length, model),
            tiled(length, model),
            *weights.specs(weights.taps),
            weights.first_spec(),
            fixed(3, model),
            fixed(6, hidden),
        ],
        [tiled(length, hidden), tiled(length, model), fixed(8, hidden), fixed(8, model)],
        [
            shape_of((tokens, hidden), jnp.bfloat16),
            shape_of((tokens, model), jnp.float32),
            shape_of((8, hidden), jnp.float32),
            shape_of((8, model), jnp.float32),
        ],
        2 * tokens * hidden * (KER * hidden + model),
        16 * tokens * model,
        "conv_back",
    )(
        low,
        gv,
        high,
        flags,
        u,
        inputs,
        upstream,
        *arrays(weights.taps),
        weights.first[0],
        weights.wide,
        weights.narrow,
    )


def in_grads(grad_pack, act_one, gu):
    tokens, model = act_one.shape
    hidden = gu.shape[1]
    sizes = Sizes(grad_pack, model, hidden)
    return call(
        in_grad_kernel,
        1,
        [pl.BlockSpec(memory_space=pl.ANY), fixed(tokens, model), fixed(tokens, hidden)],
        sizes.first(),
        shape_of(grad_pack.shape, jnp.bfloat16),
        2 * tokens * hidden * model,
        4 * tokens * model,
        "in_grads",
        {0: 0},
    )(grad_pack, act_one, gu)


def scalars():
    return pl.BlockSpec(memory_space=pltpu.SMEM)


def place():
    return jnp.stack([lax.axis_index("dp"), lax.axis_index("seq")]).astype(jnp.int32)


def share_grads(where, tap_rows, gv, act_three, short):
    tokens, hidden = gv.shape
    model = short.shape[1]
    parts = lax.axis_size("dp")
    folds = model // hidden
    depth = hidden // parts
    whole = pl.BlockSpec((tokens, hidden), lambda s: (0, 0))
    share = pl.BlockSpec((parts // 2, depth, hidden), lambda s: (0, s, 0))
    shape = shape_of((parts // 2, (KER + folds) * depth, hidden), jnp.bfloat16)
    return call(
        share_grad_kernel,
        KER + folds,
        [
            scalars(),
            pl.BlockSpec((tokens, hidden), lambda s: (0, jnp.minimum(s, KER - 1))),
            whole,
            whole,
            pl.BlockSpec((tokens, hidden), lambda s: (0, jnp.maximum(s - KER, 0))),
        ],
        [share, share],
        [shape, shape],
        2 * tokens * hidden * (KER * hidden + model),
        8 * tokens * model,
        "share_grads",
        scratch=[pltpu.VMEM((parts, depth, hidden), jnp.bfloat16)],
    )(where, tap_rows, gv, act_three, short)


def share_in_grads(where, act_one, gu, sums):
    tokens, model = act_one.shape
    hidden = gu.shape[1]
    parts = lax.axis_size("dp")
    rows = model // parts + len(sums) // 4 * VECTOR_ROWS
    shape = shape_of((parts // 2, rows, hidden), jnp.bfloat16)
    return call(
        share_in_kernel,
        1,
        [scalars()] + [fixed(*array.shape) for array in (act_one, gu, *sums)],
        [fixed(*shape.shape)] * 2,
        [shape, shape],
        2 * tokens * hidden * model,
        4 * tokens * model,
        "share_in_grads",
        scratch=[pltpu.VMEM((parts, rows, hidden), jnp.bfloat16)],
    )(where, act_one, gu, *sums)


def chip_slot(shape, index):
    return pl.BlockSpec((1,) + shape[1:], lambda i: (index(i), 0, 0))


def first_sum(owns, gots):
    hidden = owns[0].shape[2]
    rows = sum(own.shape[1] for own in owns)
    cut = rows // 32 * 16
    a, b = (2, cut, hidden), (2, rows - cut, hidden)
    outs = [
        (a, lambda i: i // 2),
        (a, lambda i: i // 2),
        (b, lambda i: jnp.minimum(i, 1)),
        (b, lambda i: jnp.maximum(i - 2, 0)),
    ]
    return call(
        functools.partial(first_sum_kernel, cut, len(owns)),
        4,
        [chip_slot(array.shape, lambda i: i) for array in (*owns, *gots)],
        [chip_slot(shape, index) for shape, index in outs],
        [shape_of(shape, jnp.bfloat16) for shape, _ in outs],
        4 * rows * hidden,
        24 * rows * hidden,
        "first_sum",
    )(*owns, *gots)


def second_sum(keep_a, got_a, keep_b, got_b):
    ins = (keep_a, got_a, keep_b, got_b)
    outs = [shape_of(array.shape[1:], jnp.bfloat16) for array in ins]
    return call(
        second_sum_kernel,
        1,
        [fixed(*array.shape) for array in ins],
        [fixed(*out.shape) for out in outs],
        outs,
        2 * keep_a.size,
        12 * keep_a.size,
        "second_sum",
    )(*ins)


def seq_split(where, folded_rows, vector_rows, *ins):
    count = lax.axis_size("seq")
    rows = sum(array.shape[0] for array in ins[:: 2 if len(ins) > 1 else 1])
    hidden = ins[0].shape[1]
    shape = (count, packed_depth(rows, count), hidden)
    return call(
        functools.partial(seq_split_kernel, folded_rows, vector_rows),
        1,
        [scalars()] + [fixed(*array.shape) for array in ins],
        fixed(*shape),
        shape_of(shape, jnp.bfloat16),
        rows * hidden,
        6 * rows * hidden,
        "seq_split",
    )(where, *ins)


def seq_exchange(split):
    return [split[0]] + [shifted(split[step], step) for step in range(1, split.shape[0])]


def last_sum(pieces, out_shapes):
    flat = [array for _, piece in pieces for array in piece]
    outs = [shape_of(shape, jnp.float32) for shape in out_shapes]
    return call(
        functools.partial(last_sum_kernel, [(name, len(piece)) for name, piece in pieces]),
        1,
        [fixed(*array.shape) for array in flat],
        [fixed(*shape) for shape in out_shapes],
        outs,
        4 * flat[0].size,
        8 * flat[0].size,
        "last_sum",
    )(*flat)


def dp_swapped(block, bit):
    count = lax.axis_size("dp")
    return lax.ppermute(block, "dp", [(i, i ^ (1 << bit)) for i in range(count)])


class Chain:
    def __init__(self, token):
        self.token = token

    def hold(self, *values):
        return lax.optimization_barrier((*values, self.token))[:-1]

    def step(self, function, *values):
        out = function(*self.hold(*values))
        self.token = out[0] if isinstance(out, (list, tuple)) else out
        return out


def shifted(block, step):
    count = lax.axis_size("seq")
    return lax.ppermute(block, "seq", [(i, (i + step) % count) for i in range(count)])


def weight_pack(block_number, device_shards):
    w_in, w_conv, w_out = (device_shards[i][block_number] for i in (2, 6, 10))
    width = w_in.shape[1]
    folds = w_out.shape[1] // width
    pieces = [w_in, w_conv.reshape(-1, width)]
    pieces += [w_out[:, i * width : (i + 1) * width] for i in range(folds)]
    return jnp.concatenate(pieces, axis=0)


def vector_pack(block_number, device_shards, width):
    order = (0, 1, 11, 3, 4, 5, 7, 8, 9)
    rows = [device_shards[i][block_number] for i in order]
    rows = [jnp.pad(row, (0, width - row.shape[0])) for row in rows]
    return jnp.pad(jnp.stack(rows), ((0, VECTOR_ROWS - len(rows)), (0, 0)))


def seq_gathered(packed):
    count = lax.axis_size("seq")
    me = lax.axis_index("seq")
    held = [packed] + [shifted(packed, step) for step in range(1, count)]
    ring = jnp.stack(held[::-1] + held[::-1])
    return lax.dynamic_slice_in_dim(ring, (count - 1 - me) % count, count, axis=0)


def folded_columns(out_parts):
    count, folds, depth, width = out_parts.shape
    per_fold = count // folds
    return (
        out_parts.reshape(folds, per_fold, folds, depth, width)
        .transpose(0, 3, 1, 2, 4)
        .reshape(folds * depth, per_fold * folds * width)
    )


def unfolded_columns(out_rows, folds, count):
    per_fold = count // folds
    depth = out_rows.shape[0] // folds
    width = out_rows.shape[1] // count
    return (
        out_rows.reshape(folds, depth, per_fold, folds, width)
        .transpose(0, 2, 3, 1, 4)
        .reshape(count, folds * depth, width)
    )


def pack_is_aligned(middle_rows):
    return middle_rows % 16 == 0


def gathered_params(block_number, device_shards, after=None):
    w_in, w_conv, w_out = (device_shards[i][block_number] for i in (2, 6, 10))
    first_rows = w_in.shape[0]
    taps, middle_rows, width = w_conv.shape
    folds = w_out.shape[1] // width
    count = lax.axis_size("seq")
    hidden = width * count
    by_seq = seq_gathered(weight_pack(block_number, device_shards))
    straight = first_rows + taps * middle_rows
    total = straight + folds * middle_rows
    upper = by_seq[:, :straight].transpose(1, 0, 2).reshape(straight, hidden)
    lower = folded_columns(by_seq[:, straight:].reshape(count, folds, middle_rows, width))
    vectors = vector_pack(block_number, device_shards, hidden)
    packed = jnp.concatenate([upper, lower, vectors])
    if after is not None:
        packed, after = lax.optimization_barrier((packed, after))
    whole = lax.all_gather(packed, "dp")
    tail = whole[:, total:].astype(jnp.float32)
    wide = tail[:, :3, :first_rows].transpose(1, 0, 2).reshape(3, -1)
    narrow = tail[:, 3:9, :middle_rows].transpose(1, 0, 2).reshape(6, -1)
    if not pack_is_aligned(middle_rows):
        bounds = [0, first_rows]
        bounds += [first_rows + (k + 1) * middle_rows for k in range(taps + folds)]
        whole = jnp.concatenate(
            [whole[:, a:b].reshape(1, -1, hidden) for a, b in zip(bounds, bounds[1:])], axis=1
        )
    return pack_weights(whole, wide, narrow)


def reduce_dp(grad_pack, wide_grads, narrow_grads):
    parts = lax.axis_size("dp")
    hidden = narrow_grads.shape[1]
    model = wide_grads.shape[1]
    first_rows = model // parts
    middle_rows = hidden // parts
    folds = model // hidden
    total = first_rows + (KER + folds) * middle_rows
    if not pack_is_aligned(middle_rows):
        bounds = [0, model] + [model + (k + 1) * hidden for k in range(KER + folds)]
        grad_pack = jnp.concatenate(
            [grad_pack[0, a:b].reshape(parts, -1, hidden) for a, b in zip(bounds, bounds[1:])]
            + [jnp.zeros((parts, VECTOR_ROWS, hidden), jnp.bfloat16)],
            axis=1,
        )
    vectors = jnp.concatenate(
        [
            jnp.pad(
                block.reshape(-1, parts, rows).transpose(1, 0, 2),
                ((0, 0), (0, 0), (0, hidden - rows)),
            )
            for block, rows in ((wide_grads, first_rows), (narrow_grads, middle_rows))
        ]
        + [jnp.zeros((parts, VECTOR_ROWS - 9, hidden), jnp.float32)],
        axis=1,
    ).astype(jnp.bfloat16)
    grad_pack = lax.dynamic_update_slice(grad_pack, vectors, (0, total, 0))
    return lax.psum_scatter(grad_pack, "dp", scatter_dimension=0, tiled=False)


def reduce_seq(mine, model, hidden):
    parts = lax.axis_size("dp")
    count = lax.axis_size("seq")
    me = lax.axis_index("seq")
    first_rows = model // parts
    middle_rows = hidden // parts
    width = hidden // count
    folds = model // hidden
    straight = first_rows + KER * middle_rows
    total = straight + folds * middle_rows
    upper = mine[:straight].reshape(straight, count, width).transpose(1, 0, 2)
    lower = unfolded_columns(mine[straight:total], folds, count)
    fold = -(-first_rows // width)
    tail = mine[total:, : fold * width].reshape(1, VECTOR_ROWS * fold, width)
    tail = jnp.broadcast_to(tail, (count,) + tail.shape[1:])
    ring = jnp.concatenate([upper, lower, tail], axis=1)
    ring = jnp.concatenate([ring, ring])
    ring = lax.dynamic_slice_in_dim(ring, me, count, axis=0)
    held = [ring[0]] + [shifted(ring[step], step) for step in range(1, count)]
    held = [block.astype(jnp.float32) for block in held]
    while len(held) > 1:
        half = len(held) // 2
        held = [held[i] + held[i + half] for i in range(half)]
    summed = held[0]
    last = summed[straight:total].reshape(folds, middle_rows, width).transpose(1, 0, 2)
    tail = summed[total:].reshape(VECTOR_ROWS, fold * width)
    return (
        summed[:first_rows],
        summed[first_rows:straight].reshape(KER, middle_rows, width),
        last.reshape(middle_rows, folds * width),
        tail[:3, :first_rows],
        tail[3:9, :middle_rows],
    )


def block_forward(inputs, projected, halos, weights, flags, dilation_step, next_dtype):
    rows, length, _ = flags.shape
    act_one, u, act_two = projected
    tap_rows, conv_out, act_three, output = convolve(
        act_two.reshape(rows, length, -1), halos, flags, inputs, weights, dilation_step, next_dtype
    )
    return output, (act_one, u, tap_rows, conv_out, act_three)


def block_backward(inputs, upstream, weights, kept, flags, dilation_step, before=None):
    act_one, u, tap_rows, conv_out, act_three = kept
    rows, length, _ = flags.shape
    short, gv, narrow_a, wide_a = out_back(upstream, conv_out, weights)
    pack = weights.first[0]
    grad_shape = shape_of(
        (pack.shape[0], sum(pack_rows(pack, inputs.shape[1], gv.shape[1])), gv.shape[1]),
        jnp.bfloat16,
    )
    grad_pack = weight_grads(tap_rows, gv, act_three, short, grad_shape)
    gu, result, narrow_b, wide_b = conv_back(
        gv.reshape(rows, length, -1), flags, u, inputs, upstream, weights, dilation_step
    )
    if before is not None:
        gu, before = lax.optimization_barrier((gu, before))
    grad_pack = in_grads(grad_pack, act_one, gu)
    wide = jnp.concatenate([wide_b[0:2], wide_a[0:1]])
    narrow = jnp.concatenate([narrow_b[0:3], narrow_a[0:3]])
    return result, reduce_dp(grad_pack, wide, narrow), before


def shard_pack(w_in, w_conv, w_out):
    count = lax.axis_size("seq")
    depth, width = w_conv.shape[2:]
    ins = (w_in, w_conv, w_out)
    rest = packed_depth((KER + w_out.shape[2] // width) * depth, count)
    lead = packed_depth(2 * w_in.shape[1], count)
    outs = [shape_of((n, width * count), jnp.bfloat16) for n in (lead, rest, rest)]
    return call(
        shard_pack_kernel,
        1,
        [fixed(*array.shape) for array in ins],
        [fixed(*out.shape) for out in outs],
        outs,
        rest * width,
        8 * rest * width,
        "shard_pack",
    )(*ins)


def pack_vectors(wide, narrow, hidden):
    ins = (jnp.stack(wide, axis=1), jnp.stack(narrow, axis=1))
    out = (2 * VECTOR_ROWS, hidden)
    return call(
        vector_pack_kernel,
        1,
        [fixed(*array.shape) for array in ins],
        fixed(*out),
        shape_of(out, jnp.bfloat16),
        hidden,
        hidden,
        "pack_vectors",
    )(*ins)


def seq_shares(packed):
    return [packed] + [shifted(packed, step) for step in range(1, lax.axis_size("seq"))]


def seq_join(where, folded_rows, held, vectors=None):
    count = len(held)
    packed = held[0]
    extra = [] if vectors is None else [vectors]
    vector_rows = 0 if vectors is None else vectors.shape[0]
    rows = folded_rows[1] + vector_rows
    hidden = packed.shape[1]
    return call(
        functools.partial(seq_join_kernel, folded_rows, vector_rows),
        1,
        [scalars()] + [fixed(*array.shape) for array in held + extra],
        fixed(rows, hidden),
        shape_of((rows, hidden), jnp.bfloat16),
        rows * hidden,
        4 * rows * hidden,
        "seq_join",
        scratch=[pltpu.VMEM((count,) + packed.shape, jnp.bfloat16)],
    )(where, *held, *extra)


class Exchange:
    def __init__(self, block, beside):
        self.block = block
        self.cut = block.shape[0] // 32 * 16
        a, b = block[: self.cut], block[self.cut :]
        got_a, got_b, *self.beside = lax.optimization_barrier(
            (dp_swapped(a, 1), dp_swapped(b, 2), *beside)
        )
        self.near = (jnp.stack([a, got_a]), jnp.stack([b, got_b]))

    def finish(self, where, beside):
        rows, hidden = self.block.shape
        near_a, near_b = self.near
        far_a, far_b, *beside = lax.optimization_barrier(
            (dp_swapped(near_a, 2), dp_swapped(near_b, 1), *beside)
        )
        near = (near_a, far_a, near_b, far_b)
        ins = near + tuple(dp_swapped(share, 0) for share in near)
        parts = lax.axis_size("dp")
        return call(
            place_kernel,
            1,
            [scalars()] + [fixed(*array.shape) for array in ins],
            fixed(parts, rows, hidden),
            shape_of((parts, rows, hidden), jnp.bfloat16),
            parts * rows * hidden,
            4 * parts * rows * hidden,
            "place",
        )(where, *ins), beside


def after(value, *earlier):
    return lax.optimization_barrier((value, *earlier))[0]


def exchanged_weights(where, shards):
    w_in, w_conv, w_out = shards[2], shards[6], shards[10]
    first_rows = w_in.shape[1]
    depth, width = w_conv.shape[2:]
    folds = w_out.shape[2] // width
    folded = (KER * depth, (KER + folds) * depth)
    plain = (2 * first_rows, 2 * first_rows)
    lead, early, late = shard_pack(w_in, w_conv, w_out)
    wide = [shards[i] for i in (0, 1, 11)]
    narrow = [shards[i] for i in (3, 4, 5, 7, 8, 9)]
    vectors = pack_vectors(wide, narrow, width * lax.axis_size("seq"))
    lead = seq_join(where, plain, seq_shares(lead), vectors)
    exchange = Exchange(lead, seq_shares(after(early, lead)))
    early = seq_join(where, folded, exchange.beside)
    early_whole = lax.all_gather(early, "dp")
    lead, late = exchange.finish(where, seq_shares(after(late, early)))
    tail = lead[:, 2 * first_rows :].astype(jnp.float32)

    def weights(block, whole):
        start = block * VECTOR_ROWS
        wide = tail[:, start : start + 3, :first_rows].transpose(1, 0, 2).reshape(3, -1)
        narrow = tail[:, start + 3 : start + 9, :depth].transpose(1, 0, 2).reshape(6, -1)
        units = [(whole, i) for i in range(KER + folds)]
        return Weights((lead, block), units[:KER], units[KER:], wide, narrow)

    def late_weights(projected):
        rows = seq_join(where, folded, list(after(tuple(late), lead)))
        return weights(1, lax.all_gather(after(rows, early_whole, projected), "dp"))

    return weights(0, early_whole), late_weights


def exchanged_backward(inputs, weights, kept, flags, dilations, cotangent, out_shapes):
    where = place()
    parts = lax.axis_size("dp")
    hidden = weights[1].hidden
    model = inputs[0].shape[1]
    depth = hidden // parts
    folded = (KER * depth, (KER + model // hidden) * depth)
    rows, length, _ = flags[0].shape

    act_one, u, tap_rows, conv_out, act_three = kept[1]
    short, gv, *out_sums_late = out_back(cotangent, conv_out, weights[1])
    blocks = gv.reshape(rows, length, -1)
    halos = seq_neighbours(blocks, KER // 2 * dilations[1])
    pack_shape = shape_of((parts, folded[1], hidden), jnp.bfloat16)
    pack = weight_grads(tap_rows, gv, act_three, short, pack_shape, 0)
    pack, low, high = lax.optimization_barrier((pack, *halos))
    late_sum = lax.psum_scatter(pack, "dp", scatter_dimension=0, tiled=False)
    gu, middle_grad, *in_sums_late = conv_back_with(
        low, blocks, high, flags[1], u, inputs[1], cotangent, weights[1], dilations[1]
    )
    chain = Chain(gu)
    own_first, other_first = chain.step(
        lambda *values: share_in_grads(where, *values, ()), act_one, gu
    )

    act_one, u, tap_rows, conv_out, act_three = kept[0]
    short, gv, *out_sums = chain.step(
        lambda value: out_back(value, conv_out, weights[0]), middle_grad
    )
    blocks = gv.reshape(rows, length, -1)
    halos = seq_neighbours(blocks, KER // 2 * dilations[0])
    own_taps, other_taps = share_grads(where, tap_rows, gv, act_three, short)
    low, high, own_taps, other_taps, other_first = lax.optimization_barrier(
        (*halos, own_taps, other_taps, other_first)
    )
    got_taps, got_first = dp_swapped(other_taps, 0), dp_swapped(other_first, 0)
    gu, input_grad, *in_sums = chain.step(
        lambda low, high: conv_back_with(
            low, blocks, high, flags[0], u, inputs[0], middle_grad, weights[0], dilations[0]
        ),
        low,
        high,
    )

    def first_round(sums):
        keep_a, send_a, keep_b, send_b = sums
        return keep_a, dp_swapped(send_a, 1), keep_b, dp_swapped(send_b, 2)

    def second_round(sums):
        kept_a, send_a, kept_b, send_b = sums
        return kept_a, dp_swapped(send_a, 2), kept_b, dp_swapped(send_b, 1)

    all_sums = (*out_sums, *in_sums, *out_sums_late, *in_sums_late)
    own, other = chain.step(
        lambda a, b: share_in_grads(where, a, b, all_sums), act_one, gu
    )
    owns = (own_taps, own_first, own)
    gots = (got_taps, got_first, dp_swapped(other, 0))
    main = first_round(
        chain.step(lambda *values: first_sum(values[:3], values[3:]), *owns, *gots)
    )
    late = seq_exchange(chain.step(lambda value: seq_split(where, folded, 0, value), late_sum))
    main, late = lax.optimization_barrier((main, late))
    main = second_round(second_sum(*main))
    main = seq_exchange(seq_split(where, folded, 2 * VECTOR_ROWS, *main))
    return input_grad, last_sum((("early", main), ("late", late)), out_shapes)


def pack_rows(pack, model, hidden):
    parts = pack.shape[0]
    extra = VECTOR_ROWS if pack_is_aligned(hidden // lax.axis_size("dp")) else 0
    return model // parts, (KER * hidden + model) // parts, extra


def local(
    tokens,
    protein_lengths,
    norm1_gain,
    norm1_bias,
    w_in,
    in_bias,
    norm2_gain,
    norm2_bias,
    w_conv,
    conv_bias,
    norm3_gain,
    norm3_bias,
    w_out,
    out_bias,
    cotangent,
):
    device_shards = (
        norm1_gain,
        norm1_bias,
        w_in,
        in_bias,
        norm2_gain,
        norm2_bias,
        w_conv,
        conv_bias,
        norm3_gain,
        norm3_bias,
        w_out,
        out_bias,
    )
    rows, seq_len, model = tokens.shape
    token_positions = lax.axis_index("seq") * seq_len + jnp.arange(seq_len, dtype=jnp.int32)
    early_flags = kernel_tap_flags(protein_lengths, token_positions, FIRST_DILATION)
    later_flags = kernel_tap_flags(protein_lengths, token_positions, SECOND_DILATION)
    parts = lax.axis_size("dp")
    fast = parts == 8 and pack_is_aligned(in_bias.shape[1])
    if fast:
        early_weights, late_weights = exchanged_weights(place(), device_shards)
    else:
        early_weights = gathered_params(0, device_shards)
        late_weights = gathered_params(1, device_shards, early_weights.first[0])
    flat_tokens = tokens.reshape(rows * seq_len, model)
    projected = project(flat_tokens, early_weights)
    halos = seq_neighbours(projected[2].reshape(rows, seq_len, -1), KER // 2 * FIRST_DILATION)
    if fast:
        late_weights = late_weights(halos)
    middle, early_kept = block_forward(
        flat_tokens, projected, halos, early_weights, early_flags, FIRST_DILATION, jnp.float32
    )
    projected = project(middle, late_weights)
    halos = seq_neighbours(projected[2].reshape(rows, seq_len, -1), KER // 2 * SECOND_DILATION)
    output, late_kept = block_forward(
        middle, projected, halos, late_weights, later_flags, SECOND_DILATION, jnp.bfloat16
    )
    hidden = early_weights.hidden
    if fast:
        shapes = [w.shape for w in (w_in, w_conv, w_out, norm1_gain, norm1_bias, out_bias)]
        shapes += [w.shape for w in (in_bias, norm2_gain, norm2_bias)]
        shapes += [w.shape for w in (conv_bias, norm3_gain, norm3_bias)]
        input_grad, grads = exchanged_backward(
            (flat_tokens, middle),
            (early_weights, late_weights),
            (early_kept, late_kept),
            (early_flags, later_flags),
            (FIRST_DILATION, SECOND_DILATION),
            cotangent.reshape(rows * seq_len, model),
            shapes,
        )
        order = (3, 4, 0, 6, 7, 8, 1, 9, 10, 11, 2, 5)
        return (
            output.reshape(tokens.shape),
            input_grad.reshape(tokens.shape),
            *(grads[i] for i in order),
        )
    middle_grad, mine_late, _ = block_backward(
        middle,
        cotangent.reshape(rows * seq_len, model),
        late_weights,
        late_kept,
        later_flags,
        SECOND_DILATION,
    )
    input_grad, mine_early, mine_late = block_backward(
        flat_tokens,
        middle_grad,
        early_weights,
        early_kept,
        early_flags,
        FIRST_DILATION,
        mine_late,
    )
    reduced_late = reduce_seq(mine_late, model, hidden)
    reduced_early = reduce_seq(mine_early, model, hidden)
    first_early, middle_early, last_early, wide_early, narrow_early = reduced_early
    first_late, middle_late, last_late, wide_late, narrow_late = reduced_late
    return (
        output.reshape(tokens.shape),
        input_grad.reshape(tokens.shape),
        jnp.stack([wide_early[0], wide_late[0]]),
        jnp.stack([wide_early[1], wide_late[1]]),
        jnp.stack([first_early, first_late]),
        jnp.stack([narrow_early[0], narrow_late[0]]),
        jnp.stack([narrow_early[1], narrow_late[1]]),
        jnp.stack([narrow_early[2], narrow_late[2]]),
        jnp.stack([middle_early, middle_late]),
        jnp.stack([narrow_early[3], narrow_late[3]]),
        jnp.stack([narrow_early[4], narrow_late[4]]),
        jnp.stack([narrow_early[5], narrow_late[5]]),
        jnp.stack([last_early, last_late]),
        jnp.stack([wide_early[2], wide_late[2]]),
    )


def solution(mesh):
    placed = (
        P("dp", "seq", None),
        P("dp", None),
        P(None, "dp"),
        P(None, "dp"),
        P(None, "dp", "seq"),
        P(None, "dp"),
        P(None, "dp"),
        P(None, "dp"),
        P(None, None, "dp", "seq"),
        P(None, "dp"),
        P(None, "dp"),
        P(None, "dp"),
        P(None, "dp", "seq"),
        P(None, "dp"),
        P("dp", "seq", None),
    )
    return jax.shard_map(
        local,
        mesh=mesh,
        in_specs=placed,
        out_specs=(
            P("dp", "seq", None),
            P("dp", "seq", None),
            P(None, "dp"),
            P(None, "dp"),
            P(None, "dp", "seq"),
            P(None, "dp"),
            P(None, "dp"),
            P(None, "dp"),
            P(None, None, "dp", "seq"),
            P(None, "dp"),
            P(None, "dp"),
            P(None, "dp"),
            P(None, "dp", "seq"),
            P(None, "dp"),
        ),
        check_vma=False,
    )
```

```python
import functools
import math

import jax
import jax.numpy as jnp
from jax import lax
from jax.experimental import pallas as pl
from jax.experimental.pallas import tpu as pltpu
from jax.sharding import PartitionSpec as P

KER = 5
FIRST_DILATION = 64
SECOND_DILATION = 128


epsilon = 1e-05
CUBIC = 0.044715
SLOPE = math.sqrt(2.0 / math.pi)
VECTOR_ROWS = 16


def seq_neighbours(block, width):
    count = lax.axis_size("seq")
    forward = [(i, i + 1) for i in range(count - 1)]
    backward = [(target, source) for source, target in forward]
    low = lax.ppermute(block[:, block.shape[1] - width :], "seq", forward)
    high = lax.ppermute(block[:, :width], "seq", backward)
    return low, high


def normalized(values):
    centred = values - jnp.mean(values, -1, keepdims=True)
    scale = lax.rsqrt(jnp.mean(centred * centred, -1, keepdims=True) + epsilon)
    return centred * scale, scale


def gelu(h):
    half = 0.5 * h
    return half + half * jnp.tanh(h * (SLOPE + (SLOPE * CUBIC) * (h * h)))


def norm_gelu(values, gain_vector, bias_vector):
    return gelu(normalized(values)[0] * gain_vector + bias_vector)


def norm_gelu_back(incoming, values, gain_vector, bias_vector):
    n, scale = normalized(values)
    h = n * gain_vector + bias_vector
    square = h * h
    rise = 0.5 + 0.5 * jnp.tanh(h * (SLOPE + (SLOPE * CUBIC) * square))
    bend = h * (2.0 * SLOPE + (6.0 * SLOPE * CUBIC) * square)
    slope = rise + (rise - rise * rise) * bend
    dh = incoming * slope
    dn = dh * gain_vector
    back = dn - jnp.mean(dn, -1, keepdims=True) - n * jnp.mean(dn * n, -1, keepdims=True)
    return back * scale, column_sum(dh * n), column_sum(dh)


def column_sum(values):
    return jnp.sum(values, axis=0, keepdims=True)


def matmul(left, right):
    return jnp.dot(left, right, preferred_element_type=jnp.float32)


def matmul_back(left, right):
    return lax.dot_general(
        left, right, (((1,), (1,)), ((), ())), preferred_element_type=jnp.float32
    )


def matmul_rows(left, right):
    return lax.dot_general(
        left, right, (((0,), (0,)), ((), ())), preferred_element_type=jnp.float32
    )


def merged(ref):
    parts, rows, columns = ref.shape
    return ref[...].reshape(parts * rows, columns)


def kernel_tap_flags(lengths, token_positions, dilation_step):
    doc_ends = jnp.cumsum(lengths, axis=1)
    row_total = doc_ends[:, -1:]
    where_pos = token_positions[None, :, None]
    finished = doc_ends[:, None, :] <= where_pos
    doc_start = jnp.sum(jnp.where(finished, lengths[:, None, :], 0), axis=2)
    doc_stop = jnp.min(jnp.where(finished, row_total[:, :, None] + 1, doc_ends[:, None, :]), axis=2)
    is_live = token_positions[None, :] < row_total
    flag_list = []
    for tap_index in range(KER):
        target = token_positions[None, :] + (tap_index - KER // 2) * dilation_step
        flag_list.append(is_live & (target >= doc_start) & (target < doc_stop))
    flag_list += [flag_list[-1]] * (8 - KER)
    return jnp.stack(flag_list, axis=2).astype(jnp.bfloat16)


def project_kernel(x_ref, w_ref, wide_ref, narrow_ref, act_one_ref, u_ref, act_two_ref):
    act_one = norm_gelu(
        x_ref[...].astype(jnp.float32), wide_ref[0:1, :], wide_ref[1:2, :]
    ).astype(jnp.bfloat16)
    act_one_ref[...] = act_one
    u = matmul(act_one, merged(w_ref)) + narrow_ref[0:1, :]
    u_ref[...] = u
    act_two_ref[...] = norm_gelu(u, narrow_ref[1:2, :], narrow_ref[2:3, :]).astype(jnp.bfloat16)


def tap_slices(low_ref, own_ref, high_ref, flag_ref, dilation_step):
    length = own_ref.shape[1]
    width = low_ref.shape[1]
    padded = jnp.concatenate([low_ref[0], own_ref[0], high_ref[0]], axis=0)
    for k in range(KER):
        start = width + (k - KER // 2) * dilation_step
        yield k, padded[start : start + length] * flag_ref[0][:, k : k + 1]


def convolve_kernel(
    dilation_step,
    low_ref,
    own_ref,
    high_ref,
    flag_ref,
    x_ref,
    k0_ref,
    k1_ref,
    k2_ref,
    k3_ref,
    k4_ref,
    left_ref,
    right_ref,
    wide_ref,
    narrow_ref,
    tap_ref,
    v_ref,
    act_three_ref,
    next_ref,
):
    taps = (k0_ref, k1_ref, k2_ref, k3_ref, k4_ref)
    hidden = own_ref.shape[2]
    total = narrow_ref[3:4, :]
    for k, piece in tap_slices(low_ref, own_ref, high_ref, flag_ref, dilation_step):
        tap_ref[:, k * hidden : (k + 1) * hidden] = piece
        total = total + matmul(piece, merged(taps[k]))
    v_ref[...] = total
    act_three = norm_gelu(total, narrow_ref[4:5, :], narrow_ref[5:6, :]).astype(jnp.bfloat16)
    act_three_ref[...] = act_three
    for i, half_ref in enumerate((left_ref, right_ref)):
        columns = slice(i * hidden, (i + 1) * hidden)
        branch = matmul(act_three, merged(half_ref)) + wide_ref[2:3, columns]
        next_ref[:, columns] = (x_ref[:, columns].astype(jnp.float32) + branch).astype(
            next_ref.dtype
        )


def out_back_kernel(
    g_ref, v_ref, left_ref, right_ref, narrow_ref, short_ref, gv_ref, narrow_sum_ref, wide_sum_ref
):
    hidden = v_ref.shape[1]

    @pl.when(pl.program_id(0) == 0)
    def _():
        narrow_sum_ref[...] = jnp.zeros_like(narrow_sum_ref)
        wide_sum_ref[...] = jnp.zeros_like(wide_sum_ref)

    short = g_ref[...].astype(jnp.bfloat16)
    short_ref[...] = short
    wide_sum_ref[0:1, :] += column_sum(short.astype(jnp.float32))
    incoming = matmul_back(short[:, :hidden], merged(left_ref))
    incoming = incoming + matmul_back(short[:, hidden:], merged(right_ref))
    gv, gain_sum, bias_sum = norm_gelu_back(
        incoming, v_ref[...], narrow_ref[4:5, :], narrow_ref[5:6, :]
    )
    gv = gv.astype(jnp.bfloat16)
    gv_ref[...] = gv
    narrow_sum_ref[0:1, :] += column_sum(gv.astype(jnp.float32))
    narrow_sum_ref[1:2, :] += gain_sum
    narrow_sum_ref[2:3, :] += bias_sum


def weight_grad_kernel(tap_ref, gv_ref, act_three_ref, short_ref, pack_ref):
    step = pl.program_id(0)

    def store(value):
        pack_ref[...] = value.astype(jnp.bfloat16).reshape(pack_ref.shape)

    @pl.when(step < KER)
    def _():
        store(matmul_rows(tap_ref[...], gv_ref[...]))

    @pl.when(step >= KER)
    def _():
        store(matmul_rows(act_three_ref[...], short_ref[...]))


def conv_back_kernel(
    dilation_step,
    low_ref,
    own_ref,
    high_ref,
    flag_ref,
    u_ref,
    x_ref,
    g_ref,
    k0_ref,
    k1_ref,
    k2_ref,
    k3_ref,
    k4_ref,
    w_ref,
    wide_ref,
    narrow_ref,
    gu_ref,
    next_ref,
    narrow_sum_ref,
    wide_sum_ref,
):
    @pl.when(pl.program_id(0) == 0)
    def _():
        narrow_sum_ref[...] = jnp.zeros_like(narrow_sum_ref)
        wide_sum_ref[...] = jnp.zeros_like(wide_sum_ref)

    taps = (k0_ref, k1_ref, k2_ref, k3_ref, k4_ref)
    total = None
    for k, piece in tap_slices(low_ref, own_ref, high_ref, flag_ref, dilation_step):
        term = matmul_back(piece, merged(taps[KER - 1 - k]))
        total = term if total is None else total + term
    gu, gain_sum, bias_sum = norm_gelu_back(
        total, u_ref[...], narrow_ref[1:2, :], narrow_ref[2:3, :]
    )
    gu = gu.astype(jnp.bfloat16)
    gu_ref[...] = gu
    narrow_sum_ref[0:1, :] += column_sum(gu.astype(jnp.float32))
    narrow_sum_ref[1:2, :] += gain_sum
    narrow_sum_ref[2:3, :] += bias_sum
    gx, gain_sum, bias_sum = norm_gelu_back(
        matmul_back(gu, merged(w_ref)),
        x_ref[...].astype(jnp.float32),
        wide_ref[0:1, :],
        wide_ref[1:2, :],
    )
    next_ref[...] = g_ref[...].astype(jnp.float32) + gx
    wide_sum_ref[0:1, :] += gain_sum
    wide_sum_ref[1:2, :] += bias_sum


def in_grad_kernel(pack_in_ref, act_one_ref, gu_ref, pack_ref):
    value = matmul_rows(act_one_ref[...], gu_ref[...])
    pack_ref[...] = value.astype(jnp.bfloat16).reshape(pack_ref.shape)


def spread(rows, place_ref, hold_ref, own_ref, other_ref):
    chip, core = place_ref[0] // 2, place_ref[0] % 2
    for i in range(own_ref.shape[0]):
        at = 2 * (chip ^ i)
        own_ref[i] = hold_ref[at + core, rows]
        other_ref[i] = hold_ref[at + 1 - core, rows]


def share_grad_kernel(
    place_ref, tap_ref, gv_ref, act_three_ref, short_ref, own_ref, other_ref, hold_ref
):
    step = pl.program_id(0)

    def store(value):
        hold_ref[...] = value.astype(jnp.bfloat16).reshape(hold_ref.shape)

    @pl.when(step < KER)
    def _():
        store(matmul_rows(tap_ref[...], gv_ref[...]))

    @pl.when(step >= KER)
    def _():
        store(matmul_rows(act_three_ref[...], short_ref[...]))

    spread(slice(None), place_ref, hold_ref, own_ref, other_ref)


def share_in_kernel(place_ref, act_one_ref, gu_ref, *refs):
    *sum_refs, own_ref, other_ref, hold_ref = refs
    parts = hold_ref.shape[0]
    hidden = gu_ref.shape[1]
    depth = act_one_ref.shape[1] // parts
    value = matmul_rows(act_one_ref[...], gu_ref[...]).astype(jnp.bfloat16)
    hold_ref[:, :depth, :] = value.reshape(parts, depth, hidden)
    for block in range(len(sum_refs) // 4):
        narrow_a, wide_a, narrow_b, wide_b = (ref[...] for ref in sum_refs[4 * block : 4 * block + 4])
        wide = jnp.concatenate([wide_b[0:2], wide_a[0:1]], axis=0)
        narrow = jnp.concatenate([narrow_b[0:3], narrow_a[0:3]], axis=0)
        narrow_depth = hidden // parts
        for part in range(parts):
            rows = [
                wide[:, part * depth : (part + 1) * depth],
                jnp.concatenate(
                    [
                        narrow[:, part * narrow_depth : (part + 1) * narrow_depth],
                        jnp.zeros((6, depth - narrow_depth), jnp.float32),
                    ],
                    axis=1,
                ),
                jnp.zeros((VECTOR_ROWS - 9, depth), jnp.float32),
            ]
            rows = jnp.concatenate(rows, axis=0)
            rows = jnp.concatenate(
                [rows, jnp.zeros((VECTOR_ROWS, hidden - depth), jnp.float32)], axis=1
            )
            start = depth + block * VECTOR_ROWS
            hold_ref[part, start : start + VECTOR_ROWS, :] = rows.astype(jnp.bfloat16)
    spread(slice(None), place_ref, hold_ref, own_ref, other_ref)


def plus(left, right):
    return left.astype(jnp.float32) + right.astype(jnp.float32)


def first_sum_kernel(cut, count, *refs):
    step = pl.program_id(0)
    keep_a, send_a, keep_b, send_b = refs[2 * count :]
    pieces = [
        plus(own[0], got[0]).astype(jnp.bfloat16) for own, got in zip(refs[:count], refs[count:])
    ]
    total = pieces[0] if count == 1 else jnp.concatenate(pieces, axis=0)
    upper, lower = total[:cut], total[cut:]

    @pl.when(step % 2 == 0)
    def _():
        keep_a[0] = upper

    @pl.when(step % 2 == 1)
    def _():
        send_a[0] = upper

    @pl.when(step < 2)
    def _():
        keep_b[0] = lower

    @pl.when(step >= 2)
    def _():
        send_b[0] = lower


def second_sum_kernel(keep_a, got_a, keep_b, got_b, kept_a, send_a, kept_b, send_b):
    for keep, got, kept, send in (
        (keep_a, got_a, kept_a, send_a),
        (keep_b, got_b, kept_b, send_b),
    ):
        kept[...] = plus(keep[0], got[0]).astype(jnp.bfloat16)
        send[...] = plus(keep[1], got[1]).astype(jnp.bfloat16)


def lane_packed(rows, depth, count):
    missing = count * depth - rows.shape[0]
    if missing:
        rows = jnp.concatenate([rows, jnp.zeros((missing, rows.shape[1]), rows.dtype)], axis=0)
    return jnp.concatenate([rows[i * depth : (i + 1) * depth] for i in range(count)], axis=1)


def lane_unpacked(packed, count):
    width = packed.shape[1] // count
    return jnp.concatenate([packed[:, i * width : (i + 1) * width] for i in range(count)], axis=0)


def packed_depth(rows, count):
    return -(-rows // (16 * count)) * 16


def seq_split_kernel(folded_rows, vector_rows, place_ref, *refs):
    *in_refs, out_ref = refs
    if len(in_refs) == 1:
        total = in_refs[0][...]
    else:
        halves = [plus(in_refs[i][...], in_refs[i + 1][...]) for i in range(0, len(in_refs), 2)]
        total = jnp.concatenate(halves, axis=0)
    total = total.astype(jnp.float32)
    count, width = out_ref.shape[0], total.shape[1] // out_ref.shape[0]
    rows = total.shape[0]
    at, end = folded_rows
    fold = (end - at) // 2
    for s in range(count):
        columns = total[:, s * width : (s + 1) * width]
        if end > at:
            unit = at + (s // 2) * fold
            left = (s % 2) * 2 * width
            pair = total[unit : unit + fold, left : left + 2 * width]
            pieces = [columns[:at], pair[:, :width], pair[:, width:], columns[end:]]
            columns = jnp.concatenate([p for p in pieces if p.shape[0]], axis=0)
        if vector_rows:
            columns = jnp.concatenate(
                [columns[: rows - vector_rows], total[rows - vector_rows :, :width]], axis=0
            )
        packed = lane_packed(columns, out_ref.shape[1], count)
        out_ref[(s - place_ref[1] + count) % count] = packed.astype(jnp.bfloat16)


def last_sum_kernel(layout, *refs):
    sums = {}
    at = 0
    for name, count in layout:
        own, one, two, three = (ref[...].astype(jnp.float32) for ref in refs[at : at + 4])
        at += 4
        sums[name] = lane_unpacked((own + two) + (one + three), 4)
    first_ref, taps_ref, last_ref = refs[at : at + 3]
    vector_refs = refs[at + 3 :]
    depth = taps_ref.shape[2]
    straight = KER * depth
    first_rows = first_ref.shape[1]
    for block, piece in ((0, sums["early"]), (1, sums["late"])):
        for k in range(KER):
            taps_ref[block, k] = piece[k * depth : (k + 1) * depth]
        last_ref[block] = jnp.concatenate(
            [piece[straight : straight + depth], piece[straight + depth : straight + 2 * depth]],
            axis=1,
        )
    rest = sums["early"][straight + 2 * depth :]
    first_ref[0] = rest[first_rows : 2 * first_rows]
    first_ref[1] = rest[:first_rows]
    for block in range(2):
        start = 2 * first_rows + block * VECTOR_ROWS
        for i, ref in enumerate(vector_refs):
            row = rest[start + i : start + i + 1]
            ref[block : block + 1, :] = row[:, : ref.shape[1]]


def shard_pack_kernel(w_in, w_conv, w_out, lead_ref, early_ref, late_ref):
    count = lead_ref.shape[1] // w_in.shape[2]
    lead = jnp.concatenate([w_in[0], w_in[1]], axis=0)
    lead_ref[...] = lane_packed(lead, lead_ref.shape[0], count)
    width = w_conv.shape[3]
    count = early_ref.shape[1] // width
    for block, ref in ((0, early_ref), (1, late_ref)):
        rows = [w_conv[block, k] for k in range(KER)]
        rows += [w_out[block][:, :width], w_out[block][:, width:]]
        ref[...] = lane_packed(jnp.concatenate(rows, axis=0), ref.shape[0], count)


def vector_pack_kernel(wide, narrow, vector_ref):
    hidden = vector_ref.shape[1]
    for block in range(2):
        rows = []
        for ref in (wide, narrow):
            part = ref[block].astype(jnp.float32)
            rows.append(
                jnp.concatenate(
                    [part, jnp.zeros((part.shape[0], hidden - part.shape[1]), jnp.float32)], axis=1
                )
            )
        rows.append(jnp.zeros((VECTOR_ROWS - 9, hidden), jnp.float32))
        start = block * VECTOR_ROWS
        vector_ref[start : start + VECTOR_ROWS, :] = jnp.concatenate(rows, axis=0).astype(
            jnp.bfloat16
        )


def seq_join_kernel(folded_rows, vector_rows, place_ref, *refs):
    *in_refs, out_ref, hold_ref = refs
    vector_in = in_refs.pop() if vector_rows else None
    count = len(in_refs)
    for step, ref in enumerate(in_refs):
        hold_ref[(place_ref[1] - step + count) % count] = ref[...]
    shares = [lane_unpacked(hold_ref[s], count) for s in range(count)]
    rows = out_ref.shape[0] - vector_rows
    at, end = folded_rows
    if at:
        out_ref[:at, :] = jnp.concatenate([share[:at] for share in shares], axis=1)
    if end > at:
        fold = (end - at) // 2
        for half in range(2):
            columns = []
            for share in shares[half * count // 2 : (half + 1) * count // 2]:
                columns += [share[at : at + fold], share[at + fold : end]]
            start = at + half * fold
            out_ref[start : start + fold, :] = jnp.concatenate(columns, axis=1)
    if vector_in is not None:
        out_ref[rows:, :] = vector_in[...]


def place_kernel(place_ref, *refs):
    *in_refs, out_ref = refs
    chip, core = place_ref[0] // 2, place_ref[0] % 2
    cut = in_refs[0].shape[1]
    for at, share_core in ((0, core), (4, 1 - core)):
        near_a, far_a, near_b, far_b = in_refs[at : at + 4]
        for i in range(2):
            out_ref[2 * (chip ^ i) + share_core, :cut] = near_a[i]
            out_ref[2 * (chip ^ (2 + i)) + share_core, :cut] = far_a[i]
            out_ref[2 * (chip ^ (2 * i)) + share_core, cut:] = near_b[i]
            out_ref[2 * (chip ^ (2 * i + 1)) + share_core, cut:] = far_b[i]


def tiled(rows, columns):
    return pl.BlockSpec((rows, columns), lambda i: (i, 0))


def fixed(*shape):
    return pl.BlockSpec(shape, lambda i: (0,) * len(shape))


def row_block(shape):
    return pl.BlockSpec((1,) + shape[1:], lambda i: (i, 0, 0))


def pack_block(parts, rows, columns, index):
    return pl.BlockSpec((parts, rows, columns), lambda i: (0, index, 0))


def cost(flops, width):
    return pl.CostEstimate(flops=flops, bytes_accessed=width, transcendentals=0)


def call(kernel, grid, in_specs, out_specs, out_shape, flops, moved, name, aliases=None, scratch=(), room=32):
    return pl.pallas_call(
        kernel,
        grid=(grid,),
        in_specs=in_specs,
        out_specs=out_specs,
        out_shape=out_shape,
        scratch_shapes=list(scratch),
        input_output_aliases=aliases or {},
        cost_estimate=cost(flops, moved),
        compiler_params=pltpu.CompilerParams(vmem_limit_bytes=room * 1024 * 1024),
        name=name,
    )


def shape_of(shape, dtype):
    return jax.ShapeDtypeStruct(shape, dtype)


class Weights:
    def __init__(self, first, taps, last, wide, narrow):
        self.first, self.taps, self.last = first, taps, last
        self.wide, self.narrow = wide, narrow
        self.model, self.hidden = wide.shape[1], narrow.shape[1]

    def first_spec(self):
        array, index = self.first
        return pack_block(array.shape[0], self.model // array.shape[0], self.hidden, index)

    def specs(self, units):
        return [
            pack_block(array.shape[0], self.hidden // array.shape[0], self.hidden, index)
            for array, index in units
        ]


def arrays(units):
    return [array for array, _ in units]


def pack_weights(pack, wide, narrow):
    folds = wide.shape[1] // narrow.shape[1]
    units = [(pack, folds + i) for i in range(KER + folds)]
    return Weights((pack, 0), units[:KER], units[KER:], wide, narrow)


class Sizes:
    def __init__(self, pack, model, hidden):
        self.parts = pack.shape[0]
        self.model, self.hidden = model, hidden
        self.first_rows = model // self.parts
        self.middle_rows = hidden // self.parts
        self.folds = model // hidden
        self.conv_at = self.first_rows // self.middle_rows

    def first(self):
        return pack_block(self.parts, self.first_rows, self.hidden, 0)


def project(inputs, weights):
    tokens, model = inputs.shape
    hidden = weights.hidden
    tile = min(128, tokens)
    return call(
        project_kernel,
        tokens // tile,
        [tiled(tile, model), weights.first_spec(), fixed(3, model), fixed(6, hidden)],
        [tiled(tile, model), tiled(tile, hidden), tiled(tile, hidden)],
        [
            shape_of((tokens, model), jnp.bfloat16),
            shape_of((tokens, hidden), jnp.float32),
            shape_of((tokens, hidden), jnp.bfloat16),
        ],
        4 * tokens * model * hidden,
        12 * tokens * model,
        "project",
    )(inputs, weights.first[0], weights.wide, weights.narrow)


def convolve(act_two, halos, flags, inputs, weights, dilation_step, next_dtype):
    rows, length, hidden = act_two.shape
    tokens, model = inputs.shape
    low, high = halos
    return call(
        functools.partial(convolve_kernel, dilation_step),
        rows,
        [
            row_block(low.shape),
            row_block(act_two.shape),
            row_block(high.shape),
            row_block(flags.shape),
            tiled(length, model),
            *weights.specs(weights.taps + weights.last),
            fixed(3, model),
            fixed(6, hidden),
        ],
        [
            tiled(length, KER * hidden),
            tiled(length, hidden),
            tiled(length, hidden),
            tiled(length, model),
        ],
        [
            shape_of((tokens, KER * hidden), jnp.bfloat16),
            shape_of((tokens, hidden), jnp.float32),
            shape_of((tokens, hidden), jnp.bfloat16),
            shape_of((tokens, model), next_dtype),
        ],
        2 * tokens * hidden * (KER * hidden + model),
        16 * tokens * model,
        "convolve",
    )(
        low,
        act_two,
        high,
        flags,
        inputs,
        *arrays(weights.taps + weights.last),
        weights.wide,
        weights.narrow,
    )


def out_back(upstream, conv_out, weights):
    tokens, model = upstream.shape
    hidden = weights.hidden
    tile = min(128, tokens)
    return call(
        out_back_kernel,
        tokens // tile,
        [
            tiled(tile, model),
            tiled(tile, hidden),
            *weights.specs(weights.last),
            fixed(6, hidden),
        ],
        [tiled(tile, model), tiled(tile, hidden), fixed(8, hidden), fixed(8, model)],
        [
            shape_of((tokens, model), jnp.bfloat16),
            shape_of((tokens, hidden), jnp.bfloat16),
            shape_of((8, hidden), jnp.float32),
            shape_of((8, model), jnp.float32),
        ],
        4 * tokens * model * hidden,
        10 * tokens * model,
        "out_back",
    )(upstream, conv_out, *arrays(weights.last), weights.narrow)


def weight_grads(tap_rows, gv, act_three, short, pack, conv_at=None):
    tokens, hidden = gv.shape
    model = short.shape[1]
    sizes = Sizes(pack, model, hidden)
    conv_at = sizes.conv_at if conv_at is None else conv_at
    whole = pl.BlockSpec((tokens, hidden), lambda s: (0, 0))
    return call(
        weight_grad_kernel,
        KER + sizes.folds,
        [
            pl.BlockSpec((tokens, hidden), lambda s: (0, jnp.minimum(s, KER - 1))),
            whole,
            whole,
            pl.BlockSpec((tokens, hidden), lambda s: (0, jnp.maximum(s - KER, 0))),
        ],
        pl.BlockSpec(
            (sizes.parts, sizes.middle_rows, hidden), lambda s: (0, conv_at + s, 0)
        ),
        shape_of(pack.shape, jnp.bfloat16),
        2 * tokens * hidden * (KER * hidden + model),
        8 * tokens * model,
        "weight_grads",
    )(tap_rows, gv, act_three, short)


def conv_back(gv, flags, u, inputs, upstream, weights, dilation_step):
    low, high = seq_neighbours(gv, KER // 2 * dilation_step)
    return conv_back_with(low, gv, high, flags, u, inputs, upstream, weights, dilation_step)


def conv_back_with(low, gv, high, flags, u, inputs, upstream, weights, dilation_step):
    rows, length, hidden = gv.shape
    tokens, model = inputs.shape
    return call(
        functools.partial(conv_back_kernel, dilation_step),
        rows,
        [
            row_block(low.shape),
            row_block(gv.shape),
            row_block(high.shape),
            row_block(flags.shape),
            tiled(length, hidden),
            tiled(length, model),
            tiled(length, model),
            *weights.specs(weights.taps),
            weights.first_spec(),
            fixed(3, model),
            fixed(6, hidden),
        ],
        [tiled(length, hidden), tiled(length, model), fixed(8, hidden), fixed(8, model)],
        [
            shape_of((tokens, hidden), jnp.bfloat16),
            shape_of((tokens, model), jnp.float32),
            shape_of((8, hidden), jnp.float32),
            shape_of((8, model), jnp.float32),
        ],
        2 * tokens * hidden * (KER * hidden + model),
        16 * tokens * model,
        "conv_back",
        room=56 if dilation_step == SECOND_DILATION else 32,
    )(
        low,
        gv,
        high,
        flags,
        u,
        inputs,
        upstream,
        *arrays(weights.taps),
        weights.first[0],
        weights.wide,
        weights.narrow,
    )


def in_grads(grad_pack, act_one, gu):
    tokens, model = act_one.shape
    hidden = gu.shape[1]
    sizes = Sizes(grad_pack, model, hidden)
    return call(
        in_grad_kernel,
        1,
        [pl.BlockSpec(memory_space=pl.ANY), fixed(tokens, model), fixed(tokens, hidden)],
        sizes.first(),
        shape_of(grad_pack.shape, jnp.bfloat16),
        2 * tokens * hidden * model,
        4 * tokens * model,
        "in_grads",
        {0: 0},
    )(grad_pack, act_one, gu)


def scalars():
    return pl.BlockSpec(memory_space=pltpu.SMEM)


def place():
    return jnp.stack([lax.axis_index("dp"), lax.axis_index("seq")]).astype(jnp.int32)


def share_grads(where, tap_rows, gv, act_three, short):
    tokens, hidden = gv.shape
    model = short.shape[1]
    parts = lax.axis_size("dp")
    folds = model // hidden
    depth = hidden // parts
    whole = pl.BlockSpec((tokens, hidden), lambda s: (0, 0))
    share = pl.BlockSpec((parts // 2, depth, hidden), lambda s: (0, s, 0))
    shape = shape_of((parts // 2, (KER + folds) * depth, hidden), jnp.bfloat16)
    return call(
        share_grad_kernel,
        KER + folds,
        [
            scalars(),
            pl.BlockSpec((tokens, hidden), lambda s: (0, jnp.minimum(s, KER - 1))),
            whole,
            whole,
            pl.BlockSpec((tokens, hidden), lambda s: (0, jnp.maximum(s - KER, 0))),
        ],
        [share, share],
        [shape, shape],
        2 * tokens * hidden * (KER * hidden + model),
        8 * tokens * model,
        "share_grads",
        scratch=[pltpu.VMEM((parts, depth, hidden), jnp.bfloat16)],
    )(where, tap_rows, gv, act_three, short)


def share_in_grads(where, act_one, gu, sums):
    tokens, model = act_one.shape
    hidden = gu.shape[1]
    parts = lax.axis_size("dp")
    rows = model // parts + len(sums) // 4 * VECTOR_ROWS
    shape = shape_of((parts // 2, rows, hidden), jnp.bfloat16)
    return call(
        share_in_kernel,
        1,
        [scalars()] + [fixed(*array.shape) for array in (act_one, gu, *sums)],
        [fixed(*shape.shape)] * 2,
        [shape, shape],
        2 * tokens * hidden * model,
        4 * tokens * model,
        "share_in_grads",
        scratch=[pltpu.VMEM((parts, rows, hidden), jnp.bfloat16)],
    )(where, act_one, gu, *sums)


def chip_slot(shape, index):
    return pl.BlockSpec((1,) + shape[1:], lambda i: (index(i), 0, 0))


def first_sum(owns, gots):
    hidden = owns[0].shape[2]
    rows = sum(own.shape[1] for own in owns)
    cut = rows // 32 * 16
    a, b = (2, cut, hidden), (2, rows - cut, hidden)
    outs = [
        (a, lambda i: i // 2),
        (a, lambda i: i // 2),
        (b, lambda i: jnp.minimum(i, 1)),
        (b, lambda i: jnp.maximum(i - 2, 0)),
    ]
    return call(
        functools.partial(first_sum_kernel, cut, len(owns)),
        4,
        [chip_slot(array.shape, lambda i: i) for array in (*owns, *gots)],
        [chip_slot(shape, index) for shape, index in outs],
        [shape_of(shape, jnp.bfloat16) for shape, _ in outs],
        4 * rows * hidden,
        24 * rows * hidden,
        "first_sum",
    )(*owns, *gots)


def second_sum(keep_a, got_a, keep_b, got_b):
    ins = (keep_a, got_a, keep_b, got_b)
    outs = [shape_of(array.shape[1:], jnp.bfloat16) for array in ins]
    return call(
        second_sum_kernel,
        1,
        [fixed(*array.shape) for array in ins],
        [fixed(*out.shape) for out in outs],
        outs,
        2 * keep_a.size,
        12 * keep_a.size,
        "second_sum",
    )(*ins)


def seq_split(where, folded_rows, vector_rows, *ins):
    count = lax.axis_size("seq")
    rows = sum(array.shape[0] for array in ins[:: 2 if len(ins) > 1 else 1])
    hidden = ins[0].shape[1]
    shape = (count, packed_depth(rows, count), hidden)
    return call(
        functools.partial(seq_split_kernel, folded_rows, vector_rows),
        1,
        [scalars()] + [fixed(*array.shape) for array in ins],
        fixed(*shape),
        shape_of(shape, jnp.bfloat16),
        rows * hidden,
        6 * rows * hidden,
        "seq_split",
    )(where, *ins)


def seq_exchange(split):
    return [split[0]] + [shifted(split[step], step) for step in range(1, split.shape[0])]


def last_sum(pieces, out_shapes):
    flat = [array for _, piece in pieces for array in piece]
    outs = [shape_of(shape, jnp.float32) for shape in out_shapes]
    return call(
        functools.partial(last_sum_kernel, [(name, len(piece)) for name, piece in pieces]),
        1,
        [fixed(*array.shape) for array in flat],
        [fixed(*shape) for shape in out_shapes],
        outs,
        4 * flat[0].size,
        8 * flat[0].size,
        "last_sum",
    )(*flat)


def dp_swapped(block, bit):
    count = lax.axis_size("dp")
    return lax.ppermute(block, "dp", [(i, i ^ (1 << bit)) for i in range(count)])


class Chain:
    def __init__(self, token):
        self.token = token

    def hold(self, *values):
        return lax.optimization_barrier((*values, self.token))[:-1]

    def step(self, function, *values):
        out = function(*self.hold(*values))
        self.token = out[0] if isinstance(out, (list, tuple)) else out
        return out


def shifted(block, step):
    count = lax.axis_size("seq")
    return lax.ppermute(block, "seq", [(i, (i + step) % count) for i in range(count)])


def weight_pack(block_number, device_shards):
    w_in, w_conv, w_out = (device_shards[i][block_number] for i in (2, 6, 10))
    width = w_in.shape[1]
    folds = w_out.shape[1] // width
    pieces = [w_in, w_conv.reshape(-1, width)]
    pieces += [w_out[:, i * width : (i + 1) * width] for i in range(folds)]
    return jnp.concatenate(pieces, axis=0)


def vector_pack(block_number, device_shards, width):
    order = (0, 1, 11, 3, 4, 5, 7, 8, 9)
    rows = [device_shards[i][block_number] for i in order]
    rows = [jnp.pad(row, (0, width - row.shape[0])) for row in rows]
    return jnp.pad(jnp.stack(rows), ((0, VECTOR_ROWS - len(rows)), (0, 0)))


def seq_gathered(packed):
    count = lax.axis_size("seq")
    me = lax.axis_index("seq")
    held = [packed] + [shifted(packed, step) for step in range(1, count)]
    ring = jnp.stack(held[::-1] + held[::-1])
    return lax.dynamic_slice_in_dim(ring, (count - 1 - me) % count, count, axis=0)


def folded_columns(out_parts):
    count, folds, depth, width = out_parts.shape
    per_fold = count // folds
    return (
        out_parts.reshape(folds, per_fold, folds, depth, width)
        .transpose(0, 3, 1, 2, 4)
        .reshape(folds * depth, per_fold * folds * width)
    )


def unfolded_columns(out_rows, folds, count):
    per_fold = count // folds
    depth = out_rows.shape[0] // folds
    width = out_rows.shape[1] // count
    return (
        out_rows.reshape(folds, depth, per_fold, folds, width)
        .transpose(0, 2, 3, 1, 4)
        .reshape(count, folds * depth, width)
    )


def pack_is_aligned(middle_rows):
    return middle_rows % 16 == 0


def gathered_params(block_number, device_shards, after=None):
    w_in, w_conv, w_out = (device_shards[i][block_number] for i in (2, 6, 10))
    first_rows = w_in.shape[0]
    taps, middle_rows, width = w_conv.shape
    folds = w_out.shape[1] // width
    count = lax.axis_size("seq")
    hidden = width * count
    by_seq = seq_gathered(weight_pack(block_number, device_shards))
    straight = first_rows + taps * middle_rows
    total = straight + folds * middle_rows
    upper = by_seq[:, :straight].transpose(1, 0, 2).reshape(straight, hidden)
    lower = folded_columns(by_seq[:, straight:].reshape(count, folds, middle_rows, width))
    vectors = vector_pack(block_number, device_shards, hidden)
    packed = jnp.concatenate([upper, lower, vectors])
    if after is not None:
        packed, after = lax.optimization_barrier((packed, after))
    whole = lax.all_gather(packed, "dp")
    tail = whole[:, total:].astype(jnp.float32)
    wide = tail[:, :3, :first_rows].transpose(1, 0, 2).reshape(3, -1)
    narrow = tail[:, 3:9, :middle_rows].transpose(1, 0, 2).reshape(6, -1)
    if not pack_is_aligned(middle_rows):
        bounds = [0, first_rows]
        bounds += [first_rows + (k + 1) * middle_rows for k in range(taps + folds)]
        whole = jnp.concatenate(
            [whole[:, a:b].reshape(1, -1, hidden) for a, b in zip(bounds, bounds[1:])], axis=1
        )
    return pack_weights(whole, wide, narrow)


def reduce_dp(grad_pack, wide_grads, narrow_grads):
    parts = lax.axis_size("dp")
    hidden = narrow_grads.shape[1]
    model = wide_grads.shape[1]
    first_rows = model // parts
    middle_rows = hidden // parts
    folds = model // hidden
    total = first_rows + (KER + folds) * middle_rows
    if not pack_is_aligned(middle_rows):
        bounds = [0, model] + [model + (k + 1) * hidden for k in range(KER + folds)]
        grad_pack = jnp.concatenate(
            [grad_pack[0, a:b].reshape(parts, -1, hidden) for a, b in zip(bounds, bounds[1:])]
            + [jnp.zeros((parts, VECTOR_ROWS, hidden), jnp.bfloat16)],
            axis=1,
        )
    vectors = jnp.concatenate(
        [
            jnp.pad(
                block.reshape(-1, parts, rows).transpose(1, 0, 2),
                ((0, 0), (0, 0), (0, hidden - rows)),
            )
            for block, rows in ((wide_grads, first_rows), (narrow_grads, middle_rows))
        ]
        + [jnp.zeros((parts, VECTOR_ROWS - 9, hidden), jnp.float32)],
        axis=1,
    ).astype(jnp.bfloat16)
    grad_pack = lax.dynamic_update_slice(grad_pack, vectors, (0, total, 0))
    return lax.psum_scatter(grad_pack, "dp", scatter_dimension=0, tiled=False)


def reduce_seq(mine, model, hidden):
    parts = lax.axis_size("dp")
    count = lax.axis_size("seq")
    me = lax.axis_index("seq")
    first_rows = model // parts
    middle_rows = hidden // parts
    width = hidden // count
    folds = model // hidden
    straight = first_rows + KER * middle_rows
    total = straight + folds * middle_rows
    upper = mine[:straight].reshape(straight, count, width).transpose(1, 0, 2)
    lower = unfolded_columns(mine[straight:total], folds, count)
    fold = -(-first_rows // width)
    tail = mine[total:, : fold * width].reshape(1, VECTOR_ROWS * fold, width)
    tail = jnp.broadcast_to(tail, (count,) + tail.shape[1:])
    ring = jnp.concatenate([upper, lower, tail], axis=1)
    ring = jnp.concatenate([ring, ring])
    ring = lax.dynamic_slice_in_dim(ring, me, count, axis=0)
    held = [ring[0]] + [shifted(ring[step], step) for step in range(1, count)]
    held = [block.astype(jnp.float32) for block in held]
    while len(held) > 1:
        half = len(held) // 2
        held = [held[i] + held[i + half] for i in range(half)]
    summed = held[0]
    last = summed[straight:total].reshape(folds, middle_rows, width).transpose(1, 0, 2)
    tail = summed[total:].reshape(VECTOR_ROWS, fold * width)
    return (
        summed[:first_rows],
        summed[first_rows:straight].reshape(KER, middle_rows, width),
        last.reshape(middle_rows, folds * width),
        tail[:3, :first_rows],
        tail[3:9, :middle_rows],
    )


def block_forward(inputs, projected, halos, weights, flags, dilation_step, next_dtype):
    rows, length, _ = flags.shape
    act_one, u, act_two = projected
    tap_rows, conv_out, act_three, output = convolve(
        act_two.reshape(rows, length, -1), halos, flags, inputs, weights, dilation_step, next_dtype
    )
    return output, (act_one, u, tap_rows, conv_out, act_three)


def block_backward(inputs, upstream, weights, kept, flags, dilation_step, before=None):
    act_one, u, tap_rows, conv_out, act_three = kept
    rows, length, _ = flags.shape
    short, gv, narrow_a, wide_a = out_back(upstream, conv_out, weights)
    pack = weights.first[0]
    grad_shape = shape_of(
        (pack.shape[0], sum(pack_rows(pack, inputs.shape[1], gv.shape[1])), gv.shape[1]),
        jnp.bfloat16,
    )
    grad_pack = weight_grads(tap_rows, gv, act_three, short, grad_shape)
    gu, result, narrow_b, wide_b = conv_back(
        gv.reshape(rows, length, -1), flags, u, inputs, upstream, weights, dilation_step
    )
    if before is not None:
        gu, before = lax.optimization_barrier((gu, before))
    grad_pack = in_grads(grad_pack, act_one, gu)
    wide = jnp.concatenate([wide_b[0:2], wide_a[0:1]])
    narrow = jnp.concatenate([narrow_b[0:3], narrow_a[0:3]])
    return result, reduce_dp(grad_pack, wide, narrow), before


def shard_pack(w_in, w_conv, w_out):
    count = lax.axis_size("seq")
    depth, width = w_conv.shape[2:]
    ins = (w_in, w_conv, w_out)
    rest = packed_depth((KER + w_out.shape[2] // width) * depth, count)
    lead = packed_depth(2 * w_in.shape[1], count)
    outs = [shape_of((n, width * count), jnp.bfloat16) for n in (lead, rest, rest)]
    return call(
        shard_pack_kernel,
        1,
        [fixed(*array.shape) for array in ins],
        [fixed(*out.shape) for out in outs],
        outs,
        rest * width,
        8 * rest * width,
        "shard_pack",
        room=60,
    )(*ins)


def pack_vectors(wide, narrow, hidden):
    ins = (jnp.stack(wide, axis=1), jnp.stack(narrow, axis=1))
    out = (2 * VECTOR_ROWS, hidden)
    return call(
        vector_pack_kernel,
        1,
        [fixed(*array.shape) for array in ins],
        fixed(*out),
        shape_of(out, jnp.bfloat16),
        hidden,
        hidden,
        "pack_vectors",
    )(*ins)


def seq_shares(packed):
    return [packed] + [shifted(packed, step) for step in range(1, lax.axis_size("seq"))]


def seq_join(where, folded_rows, held, vectors=None):
    count = len(held)
    packed = held[0]
    extra = [] if vectors is None else [vectors]
    vector_rows = 0 if vectors is None else vectors.shape[0]
    rows = folded_rows[1] + vector_rows
    hidden = packed.shape[1]
    return call(
        functools.partial(seq_join_kernel, folded_rows, vector_rows),
        1,
        [scalars()] + [fixed(*array.shape) for array in held + extra],
        fixed(rows, hidden),
        shape_of((rows, hidden), jnp.bfloat16),
        rows * hidden,
        4 * rows * hidden,
        "seq_join",
        scratch=[pltpu.VMEM((count,) + packed.shape, jnp.bfloat16)],
    )(where, *held, *extra)


class Exchange:
    def __init__(self, block, beside):
        self.block = block
        self.cut = block.shape[0] // 32 * 16
        a, b = block[: self.cut], block[self.cut :]
        got_a, got_b, *self.beside = lax.optimization_barrier(
            (dp_swapped(a, 1), dp_swapped(b, 2), *beside)
        )
        self.near = (jnp.stack([a, got_a]), jnp.stack([b, got_b]))

    def finish(self, where, beside):
        rows, hidden = self.block.shape
        near_a, near_b = self.near
        far_a, far_b, *beside = lax.optimization_barrier(
            (dp_swapped(near_a, 2), dp_swapped(near_b, 1), *beside)
        )
        near = (near_a, far_a, near_b, far_b)
        ins = near + tuple(dp_swapped(share, 0) for share in near)
        parts = lax.axis_size("dp")
        return call(
            place_kernel,
            1,
            [scalars()] + [fixed(*array.shape) for array in ins],
            fixed(parts, rows, hidden),
            shape_of((parts, rows, hidden), jnp.bfloat16),
            parts * rows * hidden,
            4 * parts * rows * hidden,
            "place",
        )(where, *ins), beside


def after(value, *earlier):
    return lax.optimization_barrier((value, *earlier))[0]


def exchanged_weights(where, shards):
    w_in, w_conv, w_out = shards[2], shards[6], shards[10]
    first_rows = w_in.shape[1]
    depth, width = w_conv.shape[2:]
    folds = w_out.shape[2] // width
    folded = (KER * depth, (KER + folds) * depth)
    plain = (2 * first_rows, 2 * first_rows)
    lead, early, late = shard_pack(w_in, w_conv, w_out)
    wide = [shards[i] for i in (0, 1, 11)]
    narrow = [shards[i] for i in (3, 4, 5, 7, 8, 9)]
    vectors = pack_vectors(wide, narrow, width * lax.axis_size("seq"))
    lead = seq_join(where, plain, seq_shares(lead), vectors)
    exchange = Exchange(lead, seq_shares(after(early, lead)))
    early = seq_join(where, folded, exchange.beside)
    early_whole = lax.all_gather(early, "dp")
    lead, late = exchange.finish(where, seq_shares(after(late, early)))
    tail = lead[:, 2 * first_rows :].astype(jnp.float32)

    def weights(block, whole):
        start = block * VECTOR_ROWS
        wide = tail[:, start : start + 3, :first_rows].transpose(1, 0, 2).reshape(3, -1)
        narrow = tail[:, start + 3 : start + 9, :depth].transpose(1, 0, 2).reshape(6, -1)
        units = [(whole, i) for i in range(KER + folds)]
        return Weights((lead, block), units[:KER], units[KER:], wide, narrow)

    def late_weights(projected):
        rows = seq_join(where, folded, list(after(tuple(late), lead)))
        return weights(1, lax.all_gather(after(rows, early_whole, projected), "dp"))

    return weights(0, early_whole), late_weights


def exchanged_backward(inputs, weights, kept, flags, dilations, cotangent, out_shapes):
    where = place()
    parts = lax.axis_size("dp")
    hidden = weights[1].hidden
    model = inputs[0].shape[1]
    depth = hidden // parts
    folded = (KER * depth, (KER + model // hidden) * depth)
    rows, length, _ = flags[0].shape

    act_one, u, tap_rows, conv_out, act_three = kept[1]
    short, gv, *out_sums_late = out_back(cotangent, conv_out, weights[1])
    blocks = gv.reshape(rows, length, -1)
    halos = seq_neighbours(blocks, KER // 2 * dilations[1])
    pack_shape = shape_of((parts, folded[1], hidden), jnp.bfloat16)
    pack = weight_grads(tap_rows, gv, act_three, short, pack_shape, 0)
    pack, low, high = lax.optimization_barrier((pack, *halos))
    late_sum = lax.psum_scatter(pack, "dp", scatter_dimension=0, tiled=False)
    gu, middle_grad, *in_sums_late = conv_back_with(
        low, blocks, high, flags[1], u, inputs[1], cotangent, weights[1], dilations[1]
    )
    chain = Chain(gu)
    own_first, other_first = chain.step(
        lambda *values: share_in_grads(where, *values, ()), act_one, gu
    )

    act_one, u, tap_rows, conv_out, act_three = kept[0]
    short, gv, *out_sums = chain.step(
        lambda value: out_back(value, conv_out, weights[0]), middle_grad
    )
    blocks = gv.reshape(rows, length, -1)
    halos = seq_neighbours(blocks, KER // 2 * dilations[0])
    own_taps, other_taps = share_grads(where, tap_rows, gv, act_three, short)
    low, high, own_taps, other_taps, other_first = lax.optimization_barrier(
        (*halos, own_taps, other_taps, other_first)
    )
    got_taps, got_first = dp_swapped(other_taps, 0), dp_swapped(other_first, 0)
    gu, input_grad, *in_sums = chain.step(
        lambda low, high: conv_back_with(
            low, blocks, high, flags[0], u, inputs[0], middle_grad, weights[0], dilations[0]
        ),
        low,
        high,
    )

    def first_round(sums):
        keep_a, send_a, keep_b, send_b = sums
        return keep_a, dp_swapped(send_a, 1), keep_b, dp_swapped(send_b, 2)

    def second_round(sums):
        kept_a, send_a, kept_b, send_b = sums
        return kept_a, dp_swapped(send_a, 2), kept_b, dp_swapped(send_b, 1)

    all_sums = (*out_sums, *in_sums, *out_sums_late, *in_sums_late)
    own, other = chain.step(
        lambda a, b: share_in_grads(where, a, b, all_sums), act_one, gu
    )
    owns = (own_taps, own_first, own)
    gots = (got_taps, got_first, dp_swapped(other, 0))
    main = first_round(
        chain.step(lambda *values: first_sum(values[:3], values[3:]), *owns, *gots)
    )
    late = seq_exchange(chain.step(lambda value: seq_split(where, folded, 0, value), late_sum))
    main, late = lax.optimization_barrier((main, late))
    main = second_round(second_sum(*main))
    main = seq_exchange(seq_split(where, folded, 2 * VECTOR_ROWS, *main))
    return input_grad, last_sum((("early", main), ("late", late)), out_shapes)


def pack_rows(pack, model, hidden):
    parts = pack.shape[0]
    extra = VECTOR_ROWS if pack_is_aligned(hidden // lax.axis_size("dp")) else 0
    return model // parts, (KER * hidden + model) // parts, extra


def local(
    tokens,
    protein_lengths,
    norm1_gain,
    norm1_bias,
    w_in,
    in_bias,
    norm2_gain,
    norm2_bias,
    w_conv,
    conv_bias,
    norm3_gain,
    norm3_bias,
    w_out,
    out_bias,
    cotangent,
):
    device_shards = (
        norm1_gain,
        norm1_bias,
        w_in,
        in_bias,
        norm2_gain,
        norm2_bias,
        w_conv,
        conv_bias,
        norm3_gain,
        norm3_bias,
        w_out,
        out_bias,
    )
    rows, seq_len, model = tokens.shape
    token_positions = lax.axis_index("seq") * seq_len + jnp.arange(seq_len, dtype=jnp.int32)
    early_flags = kernel_tap_flags(protein_lengths, token_positions, FIRST_DILATION)
    later_flags = kernel_tap_flags(protein_lengths, token_positions, SECOND_DILATION)
    parts = lax.axis_size("dp")
    fast = parts == 8 and pack_is_aligned(in_bias.shape[1])
    if fast:
        early_weights, late_weights = exchanged_weights(place(), device_shards)
    else:
        early_weights = gathered_params(0, device_shards)
        late_weights = gathered_params(1, device_shards, early_weights.first[0])
    flat_tokens = tokens.reshape(rows * seq_len, model)
    projected = project(flat_tokens, early_weights)
    halos = seq_neighbours(projected[2].reshape(rows, seq_len, -1), KER // 2 * FIRST_DILATION)
    if fast:
        late_weights = late_weights(halos)
    middle, early_kept = block_forward(
        flat_tokens, projected, halos, early_weights, early_flags, FIRST_DILATION, jnp.float32
    )
    projected = project(middle, late_weights)
    halos = seq_neighbours(projected[2].reshape(rows, seq_len, -1), KER // 2 * SECOND_DILATION)
    output, late_kept = block_forward(
        middle, projected, halos, late_weights, later_flags, SECOND_DILATION, jnp.bfloat16
    )
    hidden = early_weights.hidden
    if fast:
        shapes = [w.shape for w in (w_in, w_conv, w_out, norm1_gain, norm1_bias, out_bias)]
        shapes += [w.shape for w in (in_bias, norm2_gain, norm2_bias)]
        shapes += [w.shape for w in (conv_bias, norm3_gain, norm3_bias)]
        input_grad, grads = exchanged_backward(
            (flat_tokens, middle),
            (early_weights, late_weights),
            (early_kept, late_kept),
            (early_flags, later_flags),
            (FIRST_DILATION, SECOND_DILATION),
            cotangent.reshape(rows * seq_len, model),
            shapes,
        )
        order = (3, 4, 0, 6, 7, 8, 1, 9, 10, 11, 2, 5)
        return (
            output.reshape(tokens.shape),
            input_grad.reshape(tokens.shape),
            *(grads[i] for i in order),
        )
    middle_grad, mine_late, _ = block_backward(
        middle,
        cotangent.reshape(rows * seq_len, model),
        late_weights,
        late_kept,
        later_flags,
        SECOND_DILATION,
    )
    input_grad, mine_early, mine_late = block_backward(
        flat_tokens,
        middle_grad,
        early_weights,
        early_kept,
        early_flags,
        FIRST_DILATION,
        mine_late,
    )
    reduced_late = reduce_seq(mine_late, model, hidden)
    reduced_early = reduce_seq(mine_early, model, hidden)
    first_early, middle_early, last_early, wide_early, narrow_early = reduced_early
    first_late, middle_late, last_late, wide_late, narrow_late = reduced_late
    return (
        output.reshape(tokens.shape),
        input_grad.reshape(tokens.shape),
        jnp.stack([wide_early[0], wide_late[0]]),
        jnp.stack([wide_early[1], wide_late[1]]),
        jnp.stack([first_early, first_late]),
        jnp.stack([narrow_early[0], narrow_late[0]]),
        jnp.stack([narrow_early[1], narrow_late[1]]),
        jnp.stack([narrow_early[2], narrow_late[2]]),
        jnp.stack([middle_early, middle_late]),
        jnp.stack([narrow_early[3], narrow_late[3]]),
        jnp.stack([narrow_early[4], narrow_late[4]]),
        jnp.stack([narrow_early[5], narrow_late[5]]),
        jnp.stack([last_early, last_late]),
        jnp.stack([wide_early[2], wide_late[2]]),
    )


def solution(mesh):
    placed = (
        P("dp", "seq", None),
        P("dp", None),
        P(None, "dp"),
        P(None, "dp"),
        P(None, "dp", "seq"),
        P(None, "dp"),
        P(None, "dp"),
        P(None, "dp"),
        P(None, None, "dp", "seq"),
        P(None, "dp"),
        P(None, "dp"),
        P(None, "dp"),
        P(None, "dp", "seq"),
        P(None, "dp"),
        P("dp", "seq", None),
    )
    return jax.shard_map(
        local,
        mesh=mesh,
        in_specs=placed,
        out_specs=(
            P("dp", "seq", None),
            P("dp", "seq", None),
            P(None, "dp"),
            P(None, "dp"),
            P(None, "dp", "seq"),
            P(None, "dp"),
            P(None, "dp"),
            P(None, "dp"),
            P(None, None, "dp", "seq"),
            P(None, "dp"),
            P(None, "dp"),
            P(None, "dp"),
            P(None, "dp", "seq"),
            P(None, "dp"),
        ),
        check_vma=False,
    )
```

```python
import functools
import math

import jax
import jax.numpy as jnp
from jax import lax
from jax.experimental import pallas as pl
from jax.experimental.pallas import tpu as pltpu
from jax.sharding import PartitionSpec as P

KER = 5
FIRST_DILATION = 64
SECOND_DILATION = 128


epsilon = 1e-05
CUBIC = 0.044715
SLOPE = math.sqrt(2.0 / math.pi)
VECTOR_ROWS = 16


def seq_neighbours(block, width):
    count = lax.axis_size("seq")
    forward = [(i, i + 1) for i in range(count - 1)]
    backward = [(target, source) for source, target in forward]
    low = lax.ppermute(block[:, block.shape[1] - width :], "seq", forward)
    high = lax.ppermute(block[:, :width], "seq", backward)
    return low, high


def normalized(values):
    centred = values - jnp.mean(values, -1, keepdims=True)
    scale = lax.rsqrt(jnp.mean(centred * centred, -1, keepdims=True) + epsilon)
    return centred * scale, scale


def gelu(h):
    half = 0.5 * h
    return half + half * jnp.tanh(h * (SLOPE + (SLOPE * CUBIC) * (h * h)))


def norm_gelu(values, gain_vector, bias_vector):
    return gelu(normalized(values)[0] * gain_vector + bias_vector)


def norm_gelu_back(incoming, values, gain_vector, bias_vector):
    n, scale = normalized(values)
    h = n * gain_vector + bias_vector
    square = h * h
    rise = 0.5 + 0.5 * jnp.tanh(h * (SLOPE + (SLOPE * CUBIC) * square))
    bend = h * (2.0 * SLOPE + (6.0 * SLOPE * CUBIC) * square)
    slope = rise + (rise - rise * rise) * bend
    dh = incoming * slope
    dn = dh * gain_vector
    back = dn - jnp.mean(dn, -1, keepdims=True) - n * jnp.mean(dn * n, -1, keepdims=True)
    return back * scale, column_sum(dh * n), column_sum(dh)


def column_sum(values):
    return jnp.sum(values, axis=0, keepdims=True)


def matmul(left, right):
    return jnp.dot(left, right, preferred_element_type=jnp.float32)


def matmul_back(left, right):
    return lax.dot_general(
        left, right, (((1,), (1,)), ((), ())), preferred_element_type=jnp.float32
    )


def matmul_rows(left, right):
    return lax.dot_general(
        left, right, (((0,), (0,)), ((), ())), preferred_element_type=jnp.float32
    )


def merged(ref):
    parts, rows, columns = ref.shape
    return ref[...].reshape(parts * rows, columns)


def kernel_tap_flags(lengths, token_positions, dilation_step):
    doc_ends = jnp.cumsum(lengths, axis=1)
    row_total = doc_ends[:, -1:]
    where_pos = token_positions[None, :, None]
    finished = doc_ends[:, None, :] <= where_pos
    doc_start = jnp.sum(jnp.where(finished, lengths[:, None, :], 0), axis=2)
    doc_stop = jnp.min(jnp.where(finished, row_total[:, :, None] + 1, doc_ends[:, None, :]), axis=2)
    is_live = token_positions[None, :] < row_total
    flag_list = []
    for tap_index in range(KER):
        target = token_positions[None, :] + (tap_index - KER // 2) * dilation_step
        flag_list.append(is_live & (target >= doc_start) & (target < doc_stop))
    flag_list += [flag_list[-1]] * (8 - KER)
    return jnp.stack(flag_list, axis=2).astype(jnp.bfloat16)


def project_kernel(x_ref, w_ref, wide_ref, narrow_ref, act_one_ref, u_ref, act_two_ref):
    act_one = norm_gelu(
        x_ref[...].astype(jnp.float32), wide_ref[0:1, :], wide_ref[1:2, :]
    ).astype(jnp.bfloat16)
    act_one_ref[...] = act_one
    u = matmul(act_one, merged(w_ref)) + narrow_ref[0:1, :]
    u_ref[...] = u
    act_two_ref[...] = norm_gelu(u, narrow_ref[1:2, :], narrow_ref[2:3, :]).astype(jnp.bfloat16)


def tap_slices(low_ref, own_ref, high_ref, flag_ref, dilation_step):
    length = own_ref.shape[1]
    width = low_ref.shape[1]
    padded = jnp.concatenate([low_ref[0], own_ref[0], high_ref[0]], axis=0)
    for k in range(KER):
        start = width + (k - KER // 2) * dilation_step
        yield k, padded[start : start + length] * flag_ref[0][:, k : k + 1]


def convolve_kernel(
    dilation_step,
    low_ref,
    own_ref,
    high_ref,
    flag_ref,
    x_ref,
    k0_ref,
    k1_ref,
    k2_ref,
    k3_ref,
    k4_ref,
    left_ref,
    right_ref,
    wide_ref,
    narrow_ref,
    tap_ref,
    v_ref,
    act_three_ref,
    next_ref,
):
    taps = (k0_ref, k1_ref, k2_ref, k3_ref, k4_ref)
    hidden = own_ref.shape[2]
    total = narrow_ref[3:4, :]
    for k, piece in tap_slices(low_ref, own_ref, high_ref, flag_ref, dilation_step):
        tap_ref[:, k * hidden : (k + 1) * hidden] = piece
        total = total + matmul(piece, merged(taps[k]))
    v_ref[...] = total
    act_three = norm_gelu(total, narrow_ref[4:5, :], narrow_ref[5:6, :]).astype(jnp.bfloat16)
    act_three_ref[...] = act_three
    for i, half_ref in enumerate((left_ref, right_ref)):
        columns = slice(i * hidden, (i + 1) * hidden)
        branch = matmul(act_three, merged(half_ref)) + wide_ref[2:3, columns]
        next_ref[:, columns] = (x_ref[:, columns].astype(jnp.float32) + branch).astype(
            next_ref.dtype
        )


def out_back_kernel(
    g_ref, v_ref, left_ref, right_ref, narrow_ref, short_ref, gv_ref, narrow_sum_ref, wide_sum_ref
):
    hidden = v_ref.shape[1]

    @pl.when(pl.program_id(0) == 0)
    def _():
        narrow_sum_ref[...] = jnp.zeros_like(narrow_sum_ref)
        wide_sum_ref[...] = jnp.zeros_like(wide_sum_ref)

    short = g_ref[...].astype(jnp.bfloat16)
    short_ref[...] = short
    wide_sum_ref[0:1, :] += column_sum(short.astype(jnp.float32))
    incoming = matmul_back(short[:, :hidden], merged(left_ref))
    incoming = incoming + matmul_back(short[:, hidden:], merged(right_ref))
    gv, gain_sum, bias_sum = norm_gelu_back(
        incoming, v_ref[...], narrow_ref[4:5, :], narrow_ref[5:6, :]
    )
    gv = gv.astype(jnp.bfloat16)
    gv_ref[...] = gv
    narrow_sum_ref[0:1, :] += column_sum(gv.astype(jnp.float32))
    narrow_sum_ref[1:2, :] += gain_sum
    narrow_sum_ref[2:3, :] += bias_sum


def weight_grad_kernel(tap_ref, gv_ref, act_three_ref, short_ref, pack_ref):
    step = pl.program_id(0)

    def store(value):
        pack_ref[...] = value.astype(jnp.bfloat16).reshape(pack_ref.shape)

    @pl.when(step < KER)
    def _():
        store(matmul_rows(tap_ref[...], gv_ref[...]))

    @pl.when(step >= KER)
    def _():
        store(matmul_rows(act_three_ref[...], short_ref[...]))


def conv_back_kernel(
    dilation_step,
    low_ref,
    own_ref,
    high_ref,
    flag_ref,
    u_ref,
    x_ref,
    g_ref,
    k0_ref,
    k1_ref,
    k2_ref,
    k3_ref,
    k4_ref,
    w_ref,
    wide_ref,
    narrow_ref,
    gu_ref,
    next_ref,
    narrow_sum_ref,
    wide_sum_ref,
):
    @pl.when(pl.program_id(0) == 0)
    def _():
        narrow_sum_ref[...] = jnp.zeros_like(narrow_sum_ref)
        wide_sum_ref[...] = jnp.zeros_like(wide_sum_ref)

    taps = (k0_ref, k1_ref, k2_ref, k3_ref, k4_ref)
    total = None
    for k, piece in tap_slices(low_ref, own_ref, high_ref, flag_ref, dilation_step):
        term = matmul_back(piece, merged(taps[KER - 1 - k]))
        total = term if total is None else total + term
    gu, gain_sum, bias_sum = norm_gelu_back(
        total, u_ref[...], narrow_ref[1:2, :], narrow_ref[2:3, :]
    )
    gu = gu.astype(jnp.bfloat16)
    gu_ref[...] = gu
    narrow_sum_ref[0:1, :] += column_sum(gu.astype(jnp.float32))
    narrow_sum_ref[1:2, :] += gain_sum
    narrow_sum_ref[2:3, :] += bias_sum
    gx, gain_sum, bias_sum = norm_gelu_back(
        matmul_back(gu, merged(w_ref)),
        x_ref[...].astype(jnp.float32),
        wide_ref[0:1, :],
        wide_ref[1:2, :],
    )
    next_ref[...] = g_ref[...].astype(jnp.float32) + gx
    wide_sum_ref[0:1, :] += gain_sum
    wide_sum_ref[1:2, :] += bias_sum


def in_grad_kernel(pack_in_ref, act_one_ref, gu_ref, pack_ref):
    value = matmul_rows(act_one_ref[...], gu_ref[...])
    pack_ref[...] = value.astype(jnp.bfloat16).reshape(pack_ref.shape)


def spread(rows, place_ref, hold_ref, own_ref, other_ref):
    chip, core = place_ref[0] // 2, place_ref[0] % 2
    for i in range(own_ref.shape[0]):
        at = 2 * (chip ^ i)
        own_ref[i] = hold_ref[at + core, rows]
        other_ref[i] = hold_ref[at + 1 - core, rows]


def share_grad_kernel(
    place_ref, tap_ref, gv_ref, act_three_ref, short_ref, own_ref, other_ref, hold_ref
):
    step = pl.program_id(0)

    def store(value):
        hold_ref[...] = value.astype(jnp.bfloat16).reshape(hold_ref.shape)

    @pl.when(step < KER)
    def _():
        store(matmul_rows(tap_ref[...], gv_ref[...]))

    @pl.when(step >= KER)
    def _():
        store(matmul_rows(act_three_ref[...], short_ref[...]))

    spread(slice(None), place_ref, hold_ref, own_ref, other_ref)


def share_in_kernel(place_ref, act_one_ref, gu_ref, *refs):
    *sum_refs, own_ref, other_ref, hold_ref = refs
    parts = hold_ref.shape[0]
    hidden = gu_ref.shape[1]
    depth = act_one_ref.shape[1] // parts
    value = matmul_rows(act_one_ref[...], gu_ref[...]).astype(jnp.bfloat16)
    hold_ref[:, :depth, :] = value.reshape(parts, depth, hidden)
    for block in range(len(sum_refs) // 4):
        narrow_a, wide_a, narrow_b, wide_b = (ref[...] for ref in sum_refs[4 * block : 4 * block + 4])
        wide = jnp.concatenate([wide_b[0:2], wide_a[0:1]], axis=0)
        narrow = jnp.concatenate([narrow_b[0:3], narrow_a[0:3]], axis=0)
        narrow_depth = hidden // parts
        for part in range(parts):
            rows = [
                wide[:, part * depth : (part + 1) * depth],
                jnp.concatenate(
                    [
                        narrow[:, part * narrow_depth : (part + 1) * narrow_depth],
                        jnp.zeros((6, depth - narrow_depth), jnp.float32),
                    ],
                    axis=1,
                ),
                jnp.zeros((VECTOR_ROWS - 9, depth), jnp.float32),
            ]
            rows = jnp.concatenate(rows, axis=0)
            rows = jnp.concatenate(
                [rows, jnp.zeros((VECTOR_ROWS, hidden - depth), jnp.float32)], axis=1
            )
            start = depth + block * VECTOR_ROWS
            hold_ref[part, start : start + VECTOR_ROWS, :] = rows.astype(jnp.bfloat16)
    spread(slice(None), place_ref, hold_ref, own_ref, other_ref)


def plus(left, right):
    return left.astype(jnp.float32) + right.astype(jnp.float32)


def first_sum_kernel(cut, count, *refs):
    step = pl.program_id(0)
    keep_a, send_a, keep_b, send_b = refs[2 * count :]
    pieces = [
        plus(own[0], got[0]).astype(jnp.bfloat16) for own, got in zip(refs[:count], refs[count:])
    ]
    total = pieces[0] if count == 1 else jnp.concatenate(pieces, axis=0)
    upper, lower = total[:cut], total[cut:]

    @pl.when(step % 2 == 0)
    def _():
        keep_a[0] = upper

    @pl.when(step % 2 == 1)
    def _():
        send_a[0] = upper

    @pl.when(step < 2)
    def _():
        keep_b[0] = lower

    @pl.when(step >= 2)
    def _():
        send_b[0] = lower


def second_sum_kernel(keep_a, got_a, keep_b, got_b, kept_a, send_a, kept_b, send_b):
    for keep, got, kept, send in (
        (keep_a, got_a, kept_a, send_a),
        (keep_b, got_b, kept_b, send_b),
    ):
        kept[...] = plus(keep[0], got[0]).astype(jnp.bfloat16)
        send[...] = plus(keep[1], got[1]).astype(jnp.bfloat16)


def lane_packed(rows, depth, count):
    missing = count * depth - rows.shape[0]
    if missing:
        rows = jnp.concatenate([rows, jnp.zeros((missing, rows.shape[1]), rows.dtype)], axis=0)
    return jnp.concatenate([rows[i * depth : (i + 1) * depth] for i in range(count)], axis=1)


def lane_unpacked(packed, count):
    width = packed.shape[1] // count
    return jnp.concatenate([packed[:, i * width : (i + 1) * width] for i in range(count)], axis=0)


def packed_depth(rows, count):
    return -(-rows // (16 * count)) * 16


def seq_split_kernel(folded_rows, vector_rows, place_ref, *refs):
    *in_refs, out_ref = refs
    if len(in_refs) == 1:
        total = in_refs[0][...]
    else:
        halves = [plus(in_refs[i][...], in_refs[i + 1][...]) for i in range(0, len(in_refs), 2)]
        total = jnp.concatenate(halves, axis=0)
    total = total.astype(jnp.float32)
    count, width = out_ref.shape[0], total.shape[1] // out_ref.shape[0]
    rows = total.shape[0]
    at, end = folded_rows
    fold = (end - at) // 2
    for s in range(count):
        columns = total[:, s * width : (s + 1) * width]
        if end > at:
            unit = at + (s // 2) * fold
            left = (s % 2) * 2 * width
            pair = total[unit : unit + fold, left : left + 2 * width]
            pieces = [columns[:at], pair[:, :width], pair[:, width:], columns[end:]]
            columns = jnp.concatenate([p for p in pieces if p.shape[0]], axis=0)
        if vector_rows:
            columns = jnp.concatenate(
                [columns[: rows - vector_rows], total[rows - vector_rows :, :width]], axis=0
            )
        packed = lane_packed(columns, out_ref.shape[1], count)
        out_ref[(s - place_ref[1] + count) % count] = packed.astype(jnp.bfloat16)


def last_sum_kernel(layout, *refs):
    sums = {}
    at = 0
    for name, count in layout:
        own, one, two, three = (ref[...].astype(jnp.float32) for ref in refs[at : at + 4])
        at += 4
        sums[name] = lane_unpacked((own + two) + (one + three), 4)
    first_ref, taps_ref, last_ref = refs[at : at + 3]
    vector_refs = refs[at + 3 :]
    depth = taps_ref.shape[2]
    straight = KER * depth
    first_rows = first_ref.shape[1]
    for block, piece in ((0, sums["early"]), (1, sums["late"])):
        for k in range(KER):
            taps_ref[block, k] = piece[k * depth : (k + 1) * depth]
        last_ref[block] = jnp.concatenate(
            [piece[straight : straight + depth], piece[straight + depth : straight + 2 * depth]],
            axis=1,
        )
    rest = sums["early"][straight + 2 * depth :]
    first_ref[0] = rest[first_rows : 2 * first_rows]
    first_ref[1] = rest[:first_rows]
    for block in range(2):
        start = 2 * first_rows + block * VECTOR_ROWS
        for i, ref in enumerate(vector_refs):
            row = rest[start + i : start + i + 1]
            ref[block : block + 1, :] = row[:, : ref.shape[1]]


def shard_pack_kernel(w_in, w_conv, w_out, lead_ref, early_ref, late_ref):
    count = lead_ref.shape[1] // w_in.shape[2]
    lead = jnp.concatenate([w_in[0], w_in[1]], axis=0)
    lead_ref[...] = lane_packed(lead, lead_ref.shape[0], count)
    width = w_conv.shape[3]
    count = early_ref.shape[1] // width
    for block, ref in ((0, early_ref), (1, late_ref)):
        rows = [w_conv[block, k] for k in range(KER)]
        rows += [w_out[block][:, :width], w_out[block][:, width:]]
        ref[...] = lane_packed(jnp.concatenate(rows, axis=0), ref.shape[0], count)


def vector_pack_kernel(wide, narrow, vector_ref):
    hidden = vector_ref.shape[1]
    for block in range(2):
        rows = []
        for ref in (wide, narrow):
            part = ref[block].astype(jnp.float32)
            rows.append(
                jnp.concatenate(
                    [part, jnp.zeros((part.shape[0], hidden - part.shape[1]), jnp.float32)], axis=1
                )
            )
        rows.append(jnp.zeros((VECTOR_ROWS - 9, hidden), jnp.float32))
        start = block * VECTOR_ROWS
        vector_ref[start : start + VECTOR_ROWS, :] = jnp.concatenate(rows, axis=0).astype(
            jnp.bfloat16
        )


def seq_join_kernel(folded_rows, vector_rows, place_ref, *refs):
    *in_refs, out_ref, hold_ref = refs
    vector_in = in_refs.pop() if vector_rows else None
    count = len(in_refs)
    for step, ref in enumerate(in_refs):
        hold_ref[(place_ref[1] - step + count) % count] = ref[...]
    shares = [lane_unpacked(hold_ref[s], count) for s in range(count)]
    rows = out_ref.shape[0] - vector_rows
    at, end = folded_rows
    if at:
        out_ref[:at, :] = jnp.concatenate([share[:at] for share in shares], axis=1)
    if end > at:
        fold = (end - at) // 2
        for half in range(2):
            columns = []
            for share in shares[half * count // 2 : (half + 1) * count // 2]:
                columns += [share[at : at + fold], share[at + fold : end]]
            start = at + half * fold
            out_ref[start : start + fold, :] = jnp.concatenate(columns, axis=1)
    if vector_in is not None:
        out_ref[rows:, :] = vector_in[...]


def place_kernel(place_ref, *refs):
    *in_refs, out_ref = refs
    chip, core = place_ref[0] // 2, place_ref[0] % 2
    cut = in_refs[0].shape[1]
    for at, share_core in ((0, core), (4, 1 - core)):
        near_a, far_a, near_b, far_b = in_refs[at : at + 4]
        for i in range(2):
            out_ref[2 * (chip ^ i) + share_core, :cut] = near_a[i]
            out_ref[2 * (chip ^ (2 + i)) + share_core, :cut] = far_a[i]
            out_ref[2 * (chip ^ (2 * i)) + share_core, cut:] = near_b[i]
            out_ref[2 * (chip ^ (2 * i + 1)) + share_core, cut:] = far_b[i]


def tiled(rows, columns):
    return pl.BlockSpec((rows, columns), lambda i: (i, 0))


def fixed(*shape):
    return pl.BlockSpec(shape, lambda i: (0,) * len(shape))


def row_block(shape):
    return pl.BlockSpec((1,) + shape[1:], lambda i: (i, 0, 0))


def pack_block(parts, rows, columns, index):
    return pl.BlockSpec((parts, rows, columns), lambda i: (0, index, 0))


def cost(flops, width):
    return pl.CostEstimate(flops=flops, bytes_accessed=width, transcendentals=0)


def call(kernel, grid, in_specs, out_specs, out_shape, flops, moved, name, aliases=None, scratch=(), room=32):
    return pl.pallas_call(
        kernel,
        grid=(grid,),
        in_specs=in_specs,
        out_specs=out_specs,
        out_shape=out_shape,
        scratch_shapes=list(scratch),
        input_output_aliases=aliases or {},
        cost_estimate=cost(flops, moved),
        compiler_params=pltpu.CompilerParams(vmem_limit_bytes=room * 1024 * 1024),
        name=name,
    )


def shape_of(shape, dtype):
    return jax.ShapeDtypeStruct(shape, dtype)


class Weights:
    def __init__(self, first, taps, last, wide, narrow):
        self.first, self.taps, self.last = first, taps, last
        self.wide, self.narrow = wide, narrow
        self.model, self.hidden = wide.shape[1], narrow.shape[1]

    def first_spec(self):
        array, index = self.first
        return pack_block(array.shape[0], self.model // array.shape[0], self.hidden, index)

    def specs(self, units):
        return [
            pack_block(array.shape[0], self.hidden // array.shape[0], self.hidden, index)
            for array, index in units
        ]


def arrays(units):
    return [array for array, _ in units]


def pack_weights(pack, wide, narrow):
    folds = wide.shape[1] // narrow.shape[1]
    units = [(pack, folds + i) for i in range(KER + folds)]
    return Weights((pack, 0), units[:KER], units[KER:], wide, narrow)


class Sizes:
    def __init__(self, pack, model, hidden):
        self.parts = pack.shape[0]
        self.model, self.hidden = model, hidden
        self.first_rows = model // self.parts
        self.middle_rows = hidden // self.parts
        self.folds = model // hidden
        self.conv_at = self.first_rows // self.middle_rows

    def first(self):
        return pack_block(self.parts, self.first_rows, self.hidden, 0)


def project(inputs, weights):
    tokens, model = inputs.shape
    hidden = weights.hidden
    tile = min(256, tokens)
    return call(
        project_kernel,
        tokens // tile,
        [tiled(tile, model), weights.first_spec(), fixed(3, model), fixed(6, hidden)],
        [tiled(tile, model), tiled(tile, hidden), tiled(tile, hidden)],
        [
            shape_of((tokens, model), jnp.bfloat16),
            shape_of((tokens, hidden), jnp.float32),
            shape_of((tokens, hidden), jnp.bfloat16),
        ],
        4 * tokens * model * hidden,
        12 * tokens * model,
        "project",
    )(inputs, weights.first[0], weights.wide, weights.narrow)


def convolve(act_two, halos, flags, inputs, weights, dilation_step, next_dtype):
    rows, length, hidden = act_two.shape
    tokens, model = inputs.shape
    low, high = halos
    return call(
        functools.partial(convolve_kernel, dilation_step),
        rows,
        [
            row_block(low.shape),
            row_block(act_two.shape),
            row_block(high.shape),
            row_block(flags.shape),
            tiled(length, model),
            *weights.specs(weights.taps + weights.last),
            fixed(3, model),
            fixed(6, hidden),
        ],
        [
            tiled(length, KER * hidden),
            tiled(length, hidden),
            tiled(length, hidden),
            tiled(length, model),
        ],
        [
            shape_of((tokens, KER * hidden), jnp.bfloat16),
            shape_of((tokens, hidden), jnp.float32),
            shape_of((tokens, hidden), jnp.bfloat16),
            shape_of((tokens, model), next_dtype),
        ],
        2 * tokens * hidden * (KER * hidden + model),
        16 * tokens * model,
        "convolve",
    )(
        low,
        act_two,
        high,
        flags,
        inputs,
        *arrays(weights.taps + weights.last),
        weights.wide,
        weights.narrow,
    )


def out_back(upstream, conv_out, weights):
    tokens, model = upstream.shape
    hidden = weights.hidden
    tile = min(256, tokens)
    return call(
        out_back_kernel,
        tokens // tile,
        [
            tiled(tile, model),
            tiled(tile, hidden),
            *weights.specs(weights.last),
            fixed(6, hidden),
        ],
        [tiled(tile, model), tiled(tile, hidden), fixed(8, hidden), fixed(8, model)],
        [
            shape_of((tokens, model), jnp.bfloat16),
            shape_of((tokens, hidden), jnp.bfloat16),
            shape_of((8, hidden), jnp.float32),
            shape_of((8, model), jnp.float32),
        ],
        4 * tokens * model * hidden,
        10 * tokens * model,
        "out_back",
    )(upstream, conv_out, *arrays(weights.last), weights.narrow)


def weight_grads(tap_rows, gv, act_three, short, pack, conv_at=None):
    tokens, hidden = gv.shape
    model = short.shape[1]
    sizes = Sizes(pack, model, hidden)
    conv_at = sizes.conv_at if conv_at is None else conv_at
    whole = pl.BlockSpec((tokens, hidden), lambda s: (0, 0))
    return call(
        weight_grad_kernel,
        KER + sizes.folds,
        [
            pl.BlockSpec((tokens, hidden), lambda s: (0, jnp.minimum(s, KER - 1))),
            whole,
            whole,
            pl.BlockSpec((tokens, hidden), lambda s: (0, jnp.maximum(s - KER, 0))),
        ],
        pl.BlockSpec(
            (sizes.parts, sizes.middle_rows, hidden), lambda s: (0, conv_at + s, 0)
        ),
        shape_of(pack.shape, jnp.bfloat16),
        2 * tokens * hidden * (KER * hidden + model),
        8 * tokens * model,
        "weight_grads",
    )(tap_rows, gv, act_three, short)


def conv_back(gv, flags, u, inputs, upstream, weights, dilation_step):
    low, high = seq_neighbours(gv, KER // 2 * dilation_step)
    return conv_back_with(low, gv, high, flags, u, inputs, upstream, weights, dilation_step)


def conv_back_with(low, gv, high, flags, u, inputs, upstream, weights, dilation_step):
    rows, length, hidden = gv.shape
    tokens, model = inputs.shape
    return call(
        functools.partial(conv_back_kernel, dilation_step),
        rows,
        [
            row_block(low.shape),
            row_block(gv.shape),
            row_block(high.shape),
            row_block(flags.shape),
            tiled(length, hidden),
            tiled(length, model),
            tiled(length, model),
            *weights.specs(weights.taps),
            weights.first_spec(),
            fixed(3, model),
            fixed(6, hidden),
        ],
        [tiled(length, hidden), tiled(length, model), fixed(8, hidden), fixed(8, model)],
        [
            shape_of((tokens, hidden), jnp.bfloat16),
            shape_of((tokens, model), jnp.float32),
            shape_of((8, hidden), jnp.float32),
            shape_of((8, model), jnp.float32),
        ],
        2 * tokens * hidden * (KER * hidden + model),
        16 * tokens * model,
        "conv_back",
        room=56 if dilation_step == SECOND_DILATION else 32,
    )(
        low,
        gv,
        high,
        flags,
        u,
        inputs,
        upstream,
        *arrays(weights.taps),
        weights.first[0],
        weights.wide,
        weights.narrow,
    )


def in_grads(grad_pack, act_one, gu):
    tokens, model = act_one.shape
    hidden = gu.shape[1]
    sizes = Sizes(grad_pack, model, hidden)
    return call(
        in_grad_kernel,
        1,
        [pl.BlockSpec(memory_space=pl.ANY), fixed(tokens, model), fixed(tokens, hidden)],
        sizes.first(),
        shape_of(grad_pack.shape, jnp.bfloat16),
        2 * tokens * hidden * model,
        4 * tokens * model,
        "in_grads",
        {0: 0},
    )(grad_pack, act_one, gu)


def scalars():
    return pl.BlockSpec(memory_space=pltpu.SMEM)


def place():
    return jnp.stack([lax.axis_index("dp"), lax.axis_index("seq")]).astype(jnp.int32)


def share_grads(where, tap_rows, gv, act_three, short):
    tokens, hidden = gv.shape
    model = short.shape[1]
    parts = lax.axis_size("dp")
    folds = model // hidden
    depth = hidden // parts
    whole = pl.BlockSpec((tokens, hidden), lambda s: (0, 0))
    share = pl.BlockSpec((parts // 2, depth, hidden), lambda s: (0, s, 0))
    shape = shape_of((parts // 2, (KER + folds) * depth, hidden), jnp.bfloat16)
    return call(
        share_grad_kernel,
        KER + folds,
        [
            scalars(),
            pl.BlockSpec((tokens, hidden), lambda s: (0, jnp.minimum(s, KER - 1))),
            whole,
            whole,
            pl.BlockSpec((tokens, hidden), lambda s: (0, jnp.maximum(s - KER, 0))),
        ],
        [share, share],
        [shape, shape],
        2 * tokens * hidden * (KER * hidden + model),
        8 * tokens * model,
        "share_grads",
        scratch=[pltpu.VMEM((parts, depth, hidden), jnp.bfloat16)],
    )(where, tap_rows, gv, act_three, short)


def share_in_grads(where, act_one, gu, sums):
    tokens, model = act_one.shape
    hidden = gu.shape[1]
    parts = lax.axis_size("dp")
    rows = model // parts + len(sums) // 4 * VECTOR_ROWS
    shape = shape_of((parts // 2, rows, hidden), jnp.bfloat16)
    return call(
        share_in_kernel,
        1,
        [scalars()] + [fixed(*array.shape) for array in (act_one, gu, *sums)],
        [fixed(*shape.shape)] * 2,
        [shape, shape],
        2 * tokens * hidden * model,
        4 * tokens * model,
        "share_in_grads",
        scratch=[pltpu.VMEM((parts, rows, hidden), jnp.bfloat16)],
    )(where, act_one, gu, *sums)


def chip_slot(shape, index):
    return pl.BlockSpec((1,) + shape[1:], lambda i: (index(i), 0, 0))


def first_sum(owns, gots):
    hidden = owns[0].shape[2]
    rows = sum(own.shape[1] for own in owns)
    cut = rows // 32 * 16
    a, b = (2, cut, hidden), (2, rows - cut, hidden)
    outs = [
        (a, lambda i: i // 2),
        (a, lambda i: i // 2),
        (b, lambda i: jnp.minimum(i, 1)),
        (b, lambda i: jnp.maximum(i - 2, 0)),
    ]
    return call(
        functools.partial(first_sum_kernel, cut, len(owns)),
        4,
        [chip_slot(array.shape, lambda i: i) for array in (*owns, *gots)],
        [chip_slot(shape, index) for shape, index in outs],
        [shape_of(shape, jnp.bfloat16) for shape, _ in outs],
        4 * rows * hidden,
        24 * rows * hidden,
        "first_sum",
    )(*owns, *gots)


def second_sum(keep_a, got_a, keep_b, got_b):
    ins = (keep_a, got_a, keep_b, got_b)
    outs = [shape_of(array.shape[1:], jnp.bfloat16) for array in ins]
    return call(
        second_sum_kernel,
        1,
        [fixed(*array.shape) for array in ins],
        [fixed(*out.shape) for out in outs],
        outs,
        2 * keep_a.size,
        12 * keep_a.size,
        "second_sum",
    )(*ins)


def seq_split(where, folded_rows, vector_rows, *ins):
    count = lax.axis_size("seq")
    rows = sum(array.shape[0] for array in ins[:: 2 if len(ins) > 1 else 1])
    hidden = ins[0].shape[1]
    shape = (count, packed_depth(rows, count), hidden)
    return call(
        functools.partial(seq_split_kernel, folded_rows, vector_rows),
        1,
        [scalars()] + [fixed(*array.shape) for array in ins],
        fixed(*shape),
        shape_of(shape, jnp.bfloat16),
        rows * hidden,
        6 * rows * hidden,
        "seq_split",
    )(where, *ins)


def seq_exchange(split):
    return [split[0]] + [shifted(split[step], step) for step in range(1, split.shape[0])]


def last_sum(pieces, out_shapes):
    flat = [array for _, piece in pieces for array in piece]
    outs = [shape_of(shape, jnp.float32) for shape in out_shapes]
    return call(
        functools.partial(last_sum_kernel, [(name, len(piece)) for name, piece in pieces]),
        1,
        [fixed(*array.shape) for array in flat],
        [fixed(*shape) for shape in out_shapes],
        outs,
        4 * flat[0].size,
        8 * flat[0].size,
        "last_sum",
    )(*flat)


def dp_swapped(block, bit):
    count = lax.axis_size("dp")
    return lax.ppermute(block, "dp", [(i, i ^ (1 << bit)) for i in range(count)])


class Chain:
    def __init__(self, token):
        self.token = token

    def hold(self, *values):
        return lax.optimization_barrier((*values, self.token))[:-1]

    def step(self, function, *values):
        out = function(*self.hold(*values))
        self.token = out[0] if isinstance(out, (list, tuple)) else out
        return out


def shifted(block, step):
    count = lax.axis_size("seq")
    return lax.ppermute(block, "seq", [(i, (i + step) % count) for i in range(count)])


def weight_pack(block_number, device_shards):
    w_in, w_conv, w_out = (device_shards[i][block_number] for i in (2, 6, 10))
    width = w_in.shape[1]
    folds = w_out.shape[1] // width
    pieces = [w_in, w_conv.reshape(-1, width)]
    pieces += [w_out[:, i * width : (i + 1) * width] for i in range(folds)]
    return jnp.concatenate(pieces, axis=0)


def vector_pack(block_number, device_shards, width):
    order = (0, 1, 11, 3, 4, 5, 7, 8, 9)
    rows = [device_shards[i][block_number] for i in order]
    rows = [jnp.pad(row, (0, width - row.shape[0])) for row in rows]
    return jnp.pad(jnp.stack(rows), ((0, VECTOR_ROWS - len(rows)), (0, 0)))


def seq_gathered(packed):
    count = lax.axis_size("seq")
    me = lax.axis_index("seq")
    held = [packed] + [shifted(packed, step) for step in range(1, count)]
    ring = jnp.stack(held[::-1] + held[::-1])
    return lax.dynamic_slice_in_dim(ring, (count - 1 - me) % count, count, axis=0)


def folded_columns(out_parts):
    count, folds, depth, width = out_parts.shape
    per_fold = count // folds
    return (
        out_parts.reshape(folds, per_fold, folds, depth, width)
        .transpose(0, 3, 1, 2, 4)
        .reshape(folds * depth, per_fold * folds * width)
    )


def unfolded_columns(out_rows, folds, count):
    per_fold = count // folds
    depth = out_rows.shape[0] // folds
    width = out_rows.shape[1] // count
    return (
        out_rows.reshape(folds, depth, per_fold, folds, width)
        .transpose(0, 2, 3, 1, 4)
        .reshape(count, folds * depth, width)
    )


def pack_is_aligned(middle_rows):
    return middle_rows % 16 == 0


def gathered_params(block_number, device_shards, after=None):
    w_in, w_conv, w_out = (device_shards[i][block_number] for i in (2, 6, 10))
    first_rows = w_in.shape[0]
    taps, middle_rows, width = w_conv.shape
    folds = w_out.shape[1] // width
    count = lax.axis_size("seq")
    hidden = width * count
    by_seq = seq_gathered(weight_pack(block_number, device_shards))
    straight = first_rows + taps * middle_rows
    total = straight + folds * middle_rows
    upper = by_seq[:, :straight].transpose(1, 0, 2).reshape(straight, hidden)
    lower = folded_columns(by_seq[:, straight:].reshape(count, folds, middle_rows, width))
    vectors = vector_pack(block_number, device_shards, hidden)
    packed = jnp.concatenate([upper, lower, vectors])
    if after is not None:
        packed, after = lax.optimization_barrier((packed, after))
    whole = lax.all_gather(packed, "dp")
    tail = whole[:, total:].astype(jnp.float32)
    wide = tail[:, :3, :first_rows].transpose(1, 0, 2).reshape(3, -1)
    narrow = tail[:, 3:9, :middle_rows].transpose(1, 0, 2).reshape(6, -1)
    if not pack_is_aligned(middle_rows):
        bounds = [0, first_rows]
        bounds += [first_rows + (k + 1) * middle_rows for k in range(taps + folds)]
        whole = jnp.concatenate(
            [whole[:, a:b].reshape(1, -1, hidden) for a, b in zip(bounds, bounds[1:])], axis=1
        )
    return pack_weights(whole, wide, narrow)


def reduce_dp(grad_pack, wide_grads, narrow_grads):
    parts = lax.axis_size("dp")
    hidden = narrow_grads.shape[1]
    model = wide_grads.shape[1]
    first_rows = model // parts
    middle_rows = hidden // parts
    folds = model // hidden
    total = first_rows + (KER + folds) * middle_rows
    if not pack_is_aligned(middle_rows):
        bounds = [0, model] + [model + (k + 1) * hidden for k in range(KER + folds)]
        grad_pack = jnp.concatenate(
            [grad_pack[0, a:b].reshape(parts, -1, hidden) for a, b in zip(bounds, bounds[1:])]
            + [jnp.zeros((parts, VECTOR_ROWS, hidden), jnp.bfloat16)],
            axis=1,
        )
    vectors = jnp.concatenate(
        [
            jnp.pad(
                block.reshape(-1, parts, rows).transpose(1, 0, 2),
                ((0, 0), (0, 0), (0, hidden - rows)),
            )
            for block, rows in ((wide_grads, first_rows), (narrow_grads, middle_rows))
        ]
        + [jnp.zeros((parts, VECTOR_ROWS - 9, hidden), jnp.float32)],
        axis=1,
    ).astype(jnp.bfloat16)
    grad_pack = lax.dynamic_update_slice(grad_pack, vectors, (0, total, 0))
    return lax.psum_scatter(grad_pack, "dp", scatter_dimension=0, tiled=False)


def reduce_seq(mine, model, hidden):
    parts = lax.axis_size("dp")
    count = lax.axis_size("seq")
    me = lax.axis_index("seq")
    first_rows = model // parts
    middle_rows = hidden // parts
    width = hidden // count
    folds = model // hidden
    straight = first_rows + KER * middle_rows
    total = straight + folds * middle_rows
    upper = mine[:straight].reshape(straight, count, width).transpose(1, 0, 2)
    lower = unfolded_columns(mine[straight:total], folds, count)
    fold = -(-first_rows // width)
    tail = mine[total:, : fold * width].reshape(1, VECTOR_ROWS * fold, width)
    tail = jnp.broadcast_to(tail, (count,) + tail.shape[1:])
    ring = jnp.concatenate([upper, lower, tail], axis=1)
    ring = jnp.concatenate([ring, ring])
    ring = lax.dynamic_slice_in_dim(ring, me, count, axis=0)
    held = [ring[0]] + [shifted(ring[step], step) for step in range(1, count)]
    held = [block.astype(jnp.float32) for block in held]
    while len(held) > 1:
        half = len(held) // 2
        held = [held[i] + held[i + half] for i in range(half)]
    summed = held[0]
    last = summed[straight:total].reshape(folds, middle_rows, width).transpose(1, 0, 2)
    tail = summed[total:].reshape(VECTOR_ROWS, fold * width)
    return (
        summed[:first_rows],
        summed[first_rows:straight].reshape(KER, middle_rows, width),
        last.reshape(middle_rows, folds * width),
        tail[:3, :first_rows],
        tail[3:9, :middle_rows],
    )


def block_forward(inputs, projected, halos, weights, flags, dilation_step, next_dtype):
    rows, length, _ = flags.shape
    act_one, u, act_two = projected
    tap_rows, conv_out, act_three, output = convolve(
        act_two.reshape(rows, length, -1), halos, flags, inputs, weights, dilation_step, next_dtype
    )
    return output, (act_one, u, tap_rows, conv_out, act_three)


def block_backward(inputs, upstream, weights, kept, flags, dilation_step, before=None):
    act_one, u, tap_rows, conv_out, act_three = kept
    rows, length, _ = flags.shape
    short, gv, narrow_a, wide_a = out_back(upstream, conv_out, weights)
    pack = weights.first[0]
    grad_shape = shape_of(
        (pack.shape[0], sum(pack_rows(pack, inputs.shape[1], gv.shape[1])), gv.shape[1]),
        jnp.bfloat16,
    )
    grad_pack = weight_grads(tap_rows, gv, act_three, short, grad_shape)
    gu, result, narrow_b, wide_b = conv_back(
        gv.reshape(rows, length, -1), flags, u, inputs, upstream, weights, dilation_step
    )
    if before is not None:
        gu, before = lax.optimization_barrier((gu, before))
    grad_pack = in_grads(grad_pack, act_one, gu)
    wide = jnp.concatenate([wide_b[0:2], wide_a[0:1]])
    narrow = jnp.concatenate([narrow_b[0:3], narrow_a[0:3]])
    return result, reduce_dp(grad_pack, wide, narrow), before


def shard_pack(w_in, w_conv, w_out):
    count = lax.axis_size("seq")
    depth, width = w_conv.shape[2:]
    ins = (w_in, w_conv, w_out)
    rest = packed_depth((KER + w_out.shape[2] // width) * depth, count)
    lead = packed_depth(2 * w_in.shape[1], count)
    outs = [shape_of((n, width * count), jnp.bfloat16) for n in (lead, rest, rest)]
    return call(
        shard_pack_kernel,
        1,
        [fixed(*array.shape) for array in ins],
        [fixed(*out.shape) for out in outs],
        outs,
        rest * width,
        8 * rest * width,
        "shard_pack",
        room=60,
    )(*ins)


def pack_vectors(wide, narrow, hidden):
    ins = (jnp.stack(wide, axis=1), jnp.stack(narrow, axis=1))
    out = (2 * VECTOR_ROWS, hidden)
    return call(
        vector_pack_kernel,
        1,
        [fixed(*array.shape) for array in ins],
        fixed(*out),
        shape_of(out, jnp.bfloat16),
        hidden,
        hidden,
        "pack_vectors",
    )(*ins)


def seq_shares(packed):
    return [packed] + [shifted(packed, step) for step in range(1, lax.axis_size("seq"))]


def seq_join(where, folded_rows, held, vectors=None):
    count = len(held)
    packed = held[0]
    extra = [] if vectors is None else [vectors]
    vector_rows = 0 if vectors is None else vectors.shape[0]
    rows = folded_rows[1] + vector_rows
    hidden = packed.shape[1]
    return call(
        functools.partial(seq_join_kernel, folded_rows, vector_rows),
        1,
        [scalars()] + [fixed(*array.shape) for array in held + extra],
        fixed(rows, hidden),
        shape_of((rows, hidden), jnp.bfloat16),
        rows * hidden,
        4 * rows * hidden,
        "seq_join",
        scratch=[pltpu.VMEM((count,) + packed.shape, jnp.bfloat16)],
    )(where, *held, *extra)


class Exchange:
    def __init__(self, block, beside):
        self.block = block
        self.cut = block.shape[0] // 32 * 16
        a, b = block[: self.cut], block[self.cut :]
        got_a, got_b, *self.beside = lax.optimization_barrier(
            (dp_swapped(a, 1), dp_swapped(b, 2), *beside)
        )
        self.near = (jnp.stack([a, got_a]), jnp.stack([b, got_b]))

    def finish(self, where, beside):
        rows, hidden = self.block.shape
        near_a, near_b = self.near
        far_a, far_b, *beside = lax.optimization_barrier(
            (dp_swapped(near_a, 2), dp_swapped(near_b, 1), *beside)
        )
        near = (near_a, far_a, near_b, far_b)
        ins = near + tuple(dp_swapped(share, 0) for share in near)
        parts = lax.axis_size("dp")
        return call(
            place_kernel,
            1,
            [scalars()] + [fixed(*array.shape) for array in ins],
            fixed(parts, rows, hidden),
            shape_of((parts, rows, hidden), jnp.bfloat16),
            parts * rows * hidden,
            4 * parts * rows * hidden,
            "place",
        )(where, *ins), beside


def after(value, *earlier):
    return lax.optimization_barrier((value, *earlier))[0]


def exchanged_weights(where, shards):
    w_in, w_conv, w_out = shards[2], shards[6], shards[10]
    first_rows = w_in.shape[1]
    depth, width = w_conv.shape[2:]
    folds = w_out.shape[2] // width
    folded = (KER * depth, (KER + folds) * depth)
    plain = (2 * first_rows, 2 * first_rows)
    lead, early, late = shard_pack(w_in, w_conv, w_out)
    wide = [shards[i] for i in (0, 1, 11)]
    narrow = [shards[i] for i in (3, 4, 5, 7, 8, 9)]
    vectors = pack_vectors(wide, narrow, width * lax.axis_size("seq"))
    lead = seq_join(where, plain, seq_shares(lead), vectors)
    exchange = Exchange(lead, seq_shares(after(early, lead)))
    early = seq_join(where, folded, exchange.beside)
    early_whole = lax.all_gather(early, "dp")
    lead, late = exchange.finish(where, seq_shares(after(late, early)))
    tail = lead[:, 2 * first_rows :].astype(jnp.float32)

    def weights(block, whole):
        start = block * VECTOR_ROWS
        wide = tail[:, start : start + 3, :first_rows].transpose(1, 0, 2).reshape(3, -1)
        narrow = tail[:, start + 3 : start + 9, :depth].transpose(1, 0, 2).reshape(6, -1)
        units = [(whole, i) for i in range(KER + folds)]
        return Weights((lead, block), units[:KER], units[KER:], wide, narrow)

    def late_weights(projected):
        rows = seq_join(where, folded, list(after(tuple(late), lead)))
        return weights(1, lax.all_gather(after(rows, early_whole, projected), "dp"))

    return weights(0, early_whole), late_weights


def exchanged_backward(inputs, weights, kept, flags, dilations, cotangent, out_shapes):
    where = place()
    parts = lax.axis_size("dp")
    hidden = weights[1].hidden
    model = inputs[0].shape[1]
    depth = hidden // parts
    folded = (KER * depth, (KER + model // hidden) * depth)
    rows, length, _ = flags[0].shape

    act_one, u, tap_rows, conv_out, act_three = kept[1]
    short, gv, *out_sums_late = out_back(cotangent, conv_out, weights[1])
    blocks = gv.reshape(rows, length, -1)
    halos = seq_neighbours(blocks, KER // 2 * dilations[1])
    pack_shape = shape_of((parts, folded[1], hidden), jnp.bfloat16)
    pack = weight_grads(tap_rows, gv, act_three, short, pack_shape, 0)
    pack, low, high = lax.optimization_barrier((pack, *halos))
    late_sum = lax.psum_scatter(pack, "dp", scatter_dimension=0, tiled=False)
    gu, middle_grad, *in_sums_late = conv_back_with(
        low, blocks, high, flags[1], u, inputs[1], cotangent, weights[1], dilations[1]
    )
    chain = Chain(gu)
    own_first, other_first = chain.step(
        lambda *values: share_in_grads(where, *values, ()), act_one, gu
    )

    act_one, u, tap_rows, conv_out, act_three = kept[0]
    short, gv, *out_sums = chain.step(
        lambda value: out_back(value, conv_out, weights[0]), middle_grad
    )
    blocks = gv.reshape(rows, length, -1)
    halos = seq_neighbours(blocks, KER // 2 * dilations[0])
    own_taps, other_taps = share_grads(where, tap_rows, gv, act_three, short)
    low, high, own_taps, other_taps, other_first = lax.optimization_barrier(
        (*halos, own_taps, other_taps, other_first)
    )
    got_taps, got_first = dp_swapped(other_taps, 0), dp_swapped(other_first, 0)
    gu, input_grad, *in_sums = chain.step(
        lambda low, high: conv_back_with(
            low, blocks, high, flags[0], u, inputs[0], middle_grad, weights[0], dilations[0]
        ),
        low,
        high,
    )

    def first_round(sums):
        keep_a, send_a, keep_b, send_b = sums
        return keep_a, dp_swapped(send_a, 1), keep_b, dp_swapped(send_b, 2)

    def second_round(sums):
        kept_a, send_a, kept_b, send_b = sums
        return kept_a, dp_swapped(send_a, 2), kept_b, dp_swapped(send_b, 1)

    all_sums = (*out_sums, *in_sums, *out_sums_late, *in_sums_late)
    own, other = chain.step(
        lambda a, b: share_in_grads(where, a, b, all_sums), act_one, gu
    )
    owns = (own_taps, own_first, own)
    gots = (got_taps, got_first, dp_swapped(other, 0))
    main = first_round(
        chain.step(lambda *values: first_sum(values[:3], values[3:]), *owns, *gots)
    )
    late = seq_exchange(chain.step(lambda value: seq_split(where, folded, 0, value), late_sum))
    main, late = lax.optimization_barrier((main, late))
    main = second_round(second_sum(*main))
    main = seq_exchange(seq_split(where, folded, 2 * VECTOR_ROWS, *main))
    return input_grad, last_sum((("early", main), ("late", late)), out_shapes)


def pack_rows(pack, model, hidden):
    parts = pack.shape[0]
    extra = VECTOR_ROWS if pack_is_aligned(hidden // lax.axis_size("dp")) else 0
    return model // parts, (KER * hidden + model) // parts, extra


def local(
    tokens,
    protein_lengths,
    norm1_gain,
    norm1_bias,
    w_in,
    in_bias,
    norm2_gain,
    norm2_bias,
    w_conv,
    conv_bias,
    norm3_gain,
    norm3_bias,
    w_out,
    out_bias,
    cotangent,
):
    device_shards = (
        norm1_gain,
        norm1_bias,
        w_in,
        in_bias,
        norm2_gain,
        norm2_bias,
        w_conv,
        conv_bias,
        norm3_gain,
        norm3_bias,
        w_out,
        out_bias,
    )
    rows, seq_len, model = tokens.shape
    token_positions = lax.axis_index("seq") * seq_len + jnp.arange(seq_len, dtype=jnp.int32)
    early_flags = kernel_tap_flags(protein_lengths, token_positions, FIRST_DILATION)
    later_flags = kernel_tap_flags(protein_lengths, token_positions, SECOND_DILATION)
    parts = lax.axis_size("dp")
    fast = parts == 8 and pack_is_aligned(in_bias.shape[1])
    if fast:
        early_weights, late_weights = exchanged_weights(place(), device_shards)
    else:
        early_weights = gathered_params(0, device_shards)
        late_weights = gathered_params(1, device_shards, early_weights.first[0])
    flat_tokens = tokens.reshape(rows * seq_len, model)
    projected = project(flat_tokens, early_weights)
    halos = seq_neighbours(projected[2].reshape(rows, seq_len, -1), KER // 2 * FIRST_DILATION)
    if fast:
        late_weights = late_weights(halos)
    middle, early_kept = block_forward(
        flat_tokens, projected, halos, early_weights, early_flags, FIRST_DILATION, jnp.float32
    )
    projected = project(middle, late_weights)
    halos = seq_neighbours(projected[2].reshape(rows, seq_len, -1), KER // 2 * SECOND_DILATION)
    output, late_kept = block_forward(
        middle, projected, halos, late_weights, later_flags, SECOND_DILATION, jnp.bfloat16
    )
    hidden = early_weights.hidden
    if fast:
        shapes = [w.shape for w in (w_in, w_conv, w_out, norm1_gain, norm1_bias, out_bias)]
        shapes += [w.shape for w in (in_bias, norm2_gain, norm2_bias)]
        shapes += [w.shape for w in (conv_bias, norm3_gain, norm3_bias)]
        input_grad, grads = exchanged_backward(
            (flat_tokens, middle),
            (early_weights, late_weights),
            (early_kept, late_kept),
            (early_flags, later_flags),
            (FIRST_DILATION, SECOND_DILATION),
            cotangent.reshape(rows * seq_len, model),
            shapes,
        )
        order = (3, 4, 0, 6, 7, 8, 1, 9, 10, 11, 2, 5)
        return (
            output.reshape(tokens.shape),
            input_grad.reshape(tokens.shape),
            *(grads[i] for i in order),
        )
    middle_grad, mine_late, _ = block_backward(
        middle,
        cotangent.reshape(rows * seq_len, model),
        late_weights,
        late_kept,
        later_flags,
        SECOND_DILATION,
    )
    input_grad, mine_early, mine_late = block_backward(
        flat_tokens,
        middle_grad,
        early_weights,
        early_kept,
        early_flags,
        FIRST_DILATION,
        mine_late,
    )
    reduced_late = reduce_seq(mine_late, model, hidden)
    reduced_early = reduce_seq(mine_early, model, hidden)
    first_early, middle_early, last_early, wide_early, narrow_early = reduced_early
    first_late, middle_late, last_late, wide_late, narrow_late = reduced_late
    return (
        output.reshape(tokens.shape),
        input_grad.reshape(tokens.shape),
        jnp.stack([wide_early[0], wide_late[0]]),
        jnp.stack([wide_early[1], wide_late[1]]),
        jnp.stack([first_early, first_late]),
        jnp.stack([narrow_early[0], narrow_late[0]]),
        jnp.stack([narrow_early[1], narrow_late[1]]),
        jnp.stack([narrow_early[2], narrow_late[2]]),
        jnp.stack([middle_early, middle_late]),
        jnp.stack([narrow_early[3], narrow_late[3]]),
        jnp.stack([narrow_early[4], narrow_late[4]]),
        jnp.stack([narrow_early[5], narrow_late[5]]),
        jnp.stack([last_early, last_late]),
        jnp.stack([wide_early[2], wide_late[2]]),
    )


def solution(mesh):
    placed = (
        P("dp", "seq", None),
        P("dp", None),
        P(None, "dp"),
        P(None, "dp"),
        P(None, "dp", "seq"),
        P(None, "dp"),
        P(None, "dp"),
        P(None, "dp"),
        P(None, None, "dp", "seq"),
        P(None, "dp"),
        P(None, "dp"),
        P(None, "dp"),
        P(None, "dp", "seq"),
        P(None, "dp"),
        P("dp", "seq", None),
    )
    return jax.shard_map(
        local,
        mesh=mesh,
        in_specs=placed,
        out_specs=(
            P("dp", "seq", None),
            P("dp", "seq", None),
            P(None, "dp"),
            P(None, "dp"),
            P(None, "dp", "seq"),
            P(None, "dp"),
            P(None, "dp"),
            P(None, "dp"),
            P(None, None, "dp", "seq"),
            P(None, "dp"),
            P(None, "dp"),
            P(None, "dp"),
            P(None, "dp", "seq"),
            P(None, "dp"),
        ),
        check_vma=False,
    )
```

```python
import functools
import math

import jax
import jax.numpy as jnp
from jax import lax
from jax.experimental import pallas as pl
from jax.experimental.pallas import tpu as pltpu
from jax.sharding import PartitionSpec as P

KER = 5
FIRST_DILATION = 64
SECOND_DILATION = 128


epsilon = 1e-05
CUBIC = 0.044715
SLOPE = math.sqrt(2.0 / math.pi)
VECTOR_ROWS = 16


def seq_neighbours(block, width):
    count = lax.axis_size("seq")
    odd = lax.axis_index("seq") % 2 == 1
    near = [(i, i ^ 1) for i in range(count)]
    far = [(i, i + 1) for i in range(1, count - 1, 2)]
    far += [(target, source) for source, target in far]
    low_part, high_part = block[:, :width], block[:, block.shape[1] - width :]
    whole = width == block.shape[1]
    first = block if whole else jnp.where(odd, low_part, high_part)
    second = block if whole else jnp.where(odd, high_part, low_part)
    return lax.ppermute(first, "seq", near), lax.ppermute(second, "seq", far)


def normalized(values):
    centred = values - jnp.mean(values, -1, keepdims=True)
    scale = lax.rsqrt(jnp.mean(centred * centred, -1, keepdims=True) + epsilon)
    return centred * scale, scale


def gelu(h):
    half = 0.5 * h
    return half + half * jnp.tanh(h * (SLOPE + (SLOPE * CUBIC) * (h * h)))


def norm_gelu(values, gain_vector, bias_vector):
    return gelu(normalized(values)[0] * gain_vector + bias_vector)


def norm_gelu_back(incoming, values, gain_vector, bias_vector):
    n, scale = normalized(values)
    h = n * gain_vector + bias_vector
    square = h * h
    rise = 0.5 + 0.5 * jnp.tanh(h * (SLOPE + (SLOPE * CUBIC) * square))
    bend = h * (2.0 * SLOPE + (6.0 * SLOPE * CUBIC) * square)
    slope = rise + (rise - rise * rise) * bend
    dh = incoming * slope
    dn = dh * gain_vector
    back = dn - jnp.mean(dn, -1, keepdims=True) - n * jnp.mean(dn * n, -1, keepdims=True)
    return back * scale, column_sum(dh * n), column_sum(dh)


def column_sum(values):
    return jnp.sum(values, axis=0, keepdims=True)


def matmul(left, right):
    return jnp.dot(left, right, preferred_element_type=jnp.float32)


def matmul_back(left, right):
    return lax.dot_general(
        left, right, (((1,), (1,)), ((), ())), preferred_element_type=jnp.float32
    )


def matmul_rows(left, right):
    return lax.dot_general(
        left, right, (((0,), (0,)), ((), ())), preferred_element_type=jnp.float32
    )


def merged(ref):
    parts, rows, columns = ref.shape
    return ref[...].reshape(parts * rows, columns)


def kernel_tap_flags(lengths, token_positions, dilation_step):
    doc_ends = jnp.cumsum(lengths, axis=1)
    row_total = doc_ends[:, -1:]
    where_pos = token_positions[None, :, None]
    finished = doc_ends[:, None, :] <= where_pos
    doc_start = jnp.sum(jnp.where(finished, lengths[:, None, :], 0), axis=2)
    doc_stop = jnp.min(jnp.where(finished, row_total[:, :, None] + 1, doc_ends[:, None, :]), axis=2)
    is_live = token_positions[None, :] < row_total
    flag_list = []
    for tap_index in range(KER):
        target = token_positions[None, :] + (tap_index - KER // 2) * dilation_step
        flag_list.append(is_live & (target >= doc_start) & (target < doc_stop))
    flag_list += [flag_list[-1]] * (8 - KER)
    return jnp.stack(flag_list, axis=2).astype(jnp.bfloat16)


def project_kernel(x_ref, w_ref, wide_ref, narrow_ref, act_one_ref, u_ref, act_two_ref):
    act_one = norm_gelu(
        x_ref[...].astype(jnp.float32), wide_ref[0:1, :], wide_ref[1:2, :]
    ).astype(jnp.bfloat16)
    act_one_ref[...] = act_one
    u = matmul(act_one, merged(w_ref)) + narrow_ref[0:1, :]
    u_ref[...] = u
    act_two_ref[...] = norm_gelu(u, narrow_ref[1:2, :], narrow_ref[2:3, :]).astype(jnp.bfloat16)


def tap_slices(place_ref, first_ref, own_ref, second_ref, flag_ref, dilation_step):
    length = own_ref.shape[1]
    width = first_ref.shape[1]
    odd = place_ref[1] % 2 == 1
    low = jnp.where(odd, first_ref[0], second_ref[0])
    high = jnp.where(odd, second_ref[0], first_ref[0])
    padded = jnp.concatenate([low, own_ref[0], high], axis=0)
    for k in range(KER):
        start = width + (k - KER // 2) * dilation_step
        yield k, padded[start : start + length] * flag_ref[0][:, k : k + 1]


def convolve_kernel(
    dilation_step,
    place_ref,
    low_ref,
    own_ref,
    high_ref,
    flag_ref,
    x_ref,
    k0_ref,
    k1_ref,
    k2_ref,
    k3_ref,
    k4_ref,
    left_ref,
    right_ref,
    wide_ref,
    narrow_ref,
    tap_ref,
    v_ref,
    act_three_ref,
    next_ref,
):
    taps = (k0_ref, k1_ref, k2_ref, k3_ref, k4_ref)
    hidden = own_ref.shape[2]
    total = narrow_ref[3:4, :]
    for k, piece in tap_slices(place_ref, low_ref, own_ref, high_ref, flag_ref, dilation_step):
        tap_ref[:, k * hidden : (k + 1) * hidden] = piece
        total = total + matmul(piece, merged(taps[k]))
    v_ref[...] = total
    act_three = norm_gelu(total, narrow_ref[4:5, :], narrow_ref[5:6, :]).astype(jnp.bfloat16)
    act_three_ref[...] = act_three
    for i, half_ref in enumerate((left_ref, right_ref)):
        columns = slice(i * hidden, (i + 1) * hidden)
        branch = matmul(act_three, merged(half_ref)) + wide_ref[2:3, columns]
        next_ref[:, columns] = (x_ref[:, columns].astype(jnp.float32) + branch).astype(
            next_ref.dtype
        )


def out_back_kernel(
    g_ref, v_ref, left_ref, right_ref, narrow_ref, short_ref, gv_ref, narrow_sum_ref, wide_sum_ref
):
    hidden = v_ref.shape[1]

    @pl.when(pl.program_id(0) == 0)
    def _():
        narrow_sum_ref[...] = jnp.zeros_like(narrow_sum_ref)
        wide_sum_ref[...] = jnp.zeros_like(wide_sum_ref)

    short = g_ref[...].astype(jnp.bfloat16)
    short_ref[...] = short
    wide_sum_ref[0:1, :] += column_sum(short.astype(jnp.float32))
    incoming = matmul_back(short[:, :hidden], merged(left_ref))
    incoming = incoming + matmul_back(short[:, hidden:], merged(right_ref))
    gv, gain_sum, bias_sum = norm_gelu_back(
        incoming, v_ref[...], narrow_ref[4:5, :], narrow_ref[5:6, :]
    )
    gv = gv.astype(jnp.bfloat16)
    gv_ref[...] = gv
    narrow_sum_ref[0:1, :] += column_sum(gv.astype(jnp.float32))
    narrow_sum_ref[1:2, :] += gain_sum
    narrow_sum_ref[2:3, :] += bias_sum


def weight_grad_kernel(tap_ref, gv_ref, act_three_ref, short_ref, pack_ref):
    step = pl.program_id(0)

    def store(value):
        pack_ref[...] = value.astype(jnp.bfloat16).reshape(pack_ref.shape)

    @pl.when(step < KER)
    def _():
        store(matmul_rows(tap_ref[...], gv_ref[...]))

    @pl.when(step >= KER)
    def _():
        store(matmul_rows(act_three_ref[...], short_ref[...]))


def conv_back_kernel(
    dilation_step,
    place_ref,
    low_ref,
    own_ref,
    high_ref,
    flag_ref,
    u_ref,
    x_ref,
    g_ref,
    k0_ref,
    k1_ref,
    k2_ref,
    k3_ref,
    k4_ref,
    w_ref,
    wide_ref,
    narrow_ref,
    gu_ref,
    next_ref,
    narrow_sum_ref,
    wide_sum_ref,
):
    @pl.when(pl.program_id(0) == 0)
    def _():
        narrow_sum_ref[...] = jnp.zeros_like(narrow_sum_ref)
        wide_sum_ref[...] = jnp.zeros_like(wide_sum_ref)

    taps = (k0_ref, k1_ref, k2_ref, k3_ref, k4_ref)
    total = None
    for k, piece in tap_slices(place_ref, low_ref, own_ref, high_ref, flag_ref, dilation_step):
        term = matmul_back(piece, merged(taps[KER - 1 - k]))
        total = term if total is None else total + term
    gu, gain_sum, bias_sum = norm_gelu_back(
        total, u_ref[...], narrow_ref[1:2, :], narrow_ref[2:3, :]
    )
    gu = gu.astype(jnp.bfloat16)
    gu_ref[...] = gu
    narrow_sum_ref[0:1, :] += column_sum(gu.astype(jnp.float32))
    narrow_sum_ref[1:2, :] += gain_sum
    narrow_sum_ref[2:3, :] += bias_sum
    gx, gain_sum, bias_sum = norm_gelu_back(
        matmul_back(gu, merged(w_ref)),
        x_ref[...].astype(jnp.float32),
        wide_ref[0:1, :],
        wide_ref[1:2, :],
    )
    next_ref[...] = g_ref[...].astype(jnp.float32) + gx
    wide_sum_ref[0:1, :] += gain_sum
    wide_sum_ref[1:2, :] += bias_sum


def in_grad_kernel(pack_in_ref, act_one_ref, gu_ref, pack_ref):
    value = matmul_rows(act_one_ref[...], gu_ref[...])
    pack_ref[...] = value.astype(jnp.bfloat16).reshape(pack_ref.shape)


def spread(rows, place_ref, hold_ref, own_ref, other_ref):
    chip, core = place_ref[0] // 2, place_ref[0] % 2
    for i in range(own_ref.shape[0]):
        at = 2 * (chip ^ i)
        own_ref[i] = hold_ref[at + core, rows]
        other_ref[i] = hold_ref[at + 1 - core, rows]


def share_grad_kernel(
    place_ref, tap_ref, gv_ref, act_three_ref, short_ref, own_ref, other_ref, hold_ref
):
    step = pl.program_id(0)

    def store(value):
        hold_ref[...] = value.astype(jnp.bfloat16).reshape(hold_ref.shape)

    @pl.when(step < KER)
    def _():
        store(matmul_rows(tap_ref[...], gv_ref[...]))

    @pl.when(step >= KER)
    def _():
        store(matmul_rows(act_three_ref[...], short_ref[...]))

    spread(slice(None), place_ref, hold_ref, own_ref, other_ref)


def share_in_kernel(place_ref, act_one_ref, gu_ref, *refs):
    *sum_refs, own_ref, other_ref, hold_ref = refs
    parts = hold_ref.shape[0]
    hidden = gu_ref.shape[1]
    depth = act_one_ref.shape[1] // parts
    value = matmul_rows(act_one_ref[...], gu_ref[...]).astype(jnp.bfloat16)
    hold_ref[:, :depth, :] = value.reshape(parts, depth, hidden)
    for block in range(len(sum_refs) // 4):
        narrow_a, wide_a, narrow_b, wide_b = (ref[...] for ref in sum_refs[4 * block : 4 * block + 4])
        wide = jnp.concatenate([wide_b[0:2], wide_a[0:1]], axis=0)
        narrow = jnp.concatenate([narrow_b[0:3], narrow_a[0:3]], axis=0)
        narrow_depth = hidden // parts
        for part in range(parts):
            rows = [
                wide[:, part * depth : (part + 1) * depth],
                jnp.concatenate(
                    [
                        narrow[:, part * narrow_depth : (part + 1) * narrow_depth],
                        jnp.zeros((6, depth - narrow_depth), jnp.float32),
                    ],
                    axis=1,
                ),
                jnp.zeros((VECTOR_ROWS - 9, depth), jnp.float32),
            ]
            rows = jnp.concatenate(rows, axis=0)
            rows = jnp.concatenate(
                [rows, jnp.zeros((VECTOR_ROWS, hidden - depth), jnp.float32)], axis=1
            )
            start = depth + block * VECTOR_ROWS
            hold_ref[part, start : start + VECTOR_ROWS, :] = rows.astype(jnp.bfloat16)
    spread(slice(None), place_ref, hold_ref, own_ref, other_ref)


def plus(left, right):
    return left.astype(jnp.float32) + right.astype(jnp.float32)


def first_sum_kernel(cut, count, *refs):
    step = pl.program_id(0)
    keep_a, send_a, keep_b, send_b = refs[2 * count :]
    pieces = [
        plus(own[0], got[0]).astype(jnp.bfloat16) for own, got in zip(refs[:count], refs[count:])
    ]
    total = pieces[0] if count == 1 else jnp.concatenate(pieces, axis=0)
    upper, lower = total[:cut], total[cut:]

    @pl.when(step % 2 == 0)
    def _():
        keep_a[0] = upper

    @pl.when(step % 2 == 1)
    def _():
        send_a[0] = upper

    @pl.when(step < 2)
    def _():
        keep_b[0] = lower

    @pl.when(step >= 2)
    def _():
        send_b[0] = lower


def second_sum_kernel(keep_a, got_a, keep_b, got_b, kept_a, send_a, kept_b, send_b):
    for keep, got, kept, send in (
        (keep_a, got_a, kept_a, send_a),
        (keep_b, got_b, kept_b, send_b),
    ):
        kept[...] = plus(keep[0], got[0]).astype(jnp.bfloat16)
        send[...] = plus(keep[1], got[1]).astype(jnp.bfloat16)


def lane_packed(rows, depth, count):
    missing = count * depth - rows.shape[0]
    if missing:
        rows = jnp.concatenate([rows, jnp.zeros((missing, rows.shape[1]), rows.dtype)], axis=0)
    return jnp.concatenate([rows[i * depth : (i + 1) * depth] for i in range(count)], axis=1)


def lane_unpacked(packed, count):
    width = packed.shape[1] // count
    return jnp.concatenate([packed[:, i * width : (i + 1) * width] for i in range(count)], axis=0)


def packed_depth(rows, count):
    return -(-rows // (16 * count)) * 16


def seq_split_kernel(folded_rows, vector_rows, place_ref, *refs):
    *in_refs, out_ref = refs
    if len(in_refs) == 1:
        total = in_refs[0][...]
    else:
        halves = [plus(in_refs[i][...], in_refs[i + 1][...]) for i in range(0, len(in_refs), 2)]
        total = jnp.concatenate(halves, axis=0)
    total = total.astype(jnp.float32)
    count, width = out_ref.shape[0], total.shape[1] // out_ref.shape[0]
    rows = total.shape[0]
    at, end = folded_rows
    fold = (end - at) // 2
    for s in range(count):
        columns = total[:, s * width : (s + 1) * width]
        if end > at:
            unit = at + (s // 2) * fold
            left = (s % 2) * 2 * width
            pair = total[unit : unit + fold, left : left + 2 * width]
            pieces = [columns[:at], pair[:, :width], pair[:, width:], columns[end:]]
            columns = jnp.concatenate([p for p in pieces if p.shape[0]], axis=0)
        if vector_rows:
            columns = jnp.concatenate(
                [columns[: rows - vector_rows], total[rows - vector_rows :, :width]], axis=0
            )
        packed = lane_packed(columns, out_ref.shape[1], count)
        out_ref[(s - place_ref[1] + count) % count] = packed.astype(jnp.bfloat16)


def last_sum_kernel(layout, *refs):
    sums = {}
    at = 0
    for name, count in layout:
        own, one, two, three = (ref[...].astype(jnp.float32) for ref in refs[at : at + 4])
        at += 4
        sums[name] = lane_unpacked((own + two) + (one + three), 4)
    first_ref, taps_ref, last_ref = refs[at : at + 3]
    vector_refs = refs[at + 3 :]
    depth = taps_ref.shape[2]
    straight = KER * depth
    first_rows = first_ref.shape[1]
    for block, piece in ((0, sums["early"]), (1, sums["late"])):
        for k in range(KER):
            taps_ref[block, k] = piece[k * depth : (k + 1) * depth]
        last_ref[block] = jnp.concatenate(
            [piece[straight : straight + depth], piece[straight + depth : straight + 2 * depth]],
            axis=1,
        )
    rest = sums["early"][straight + 2 * depth :]
    first_ref[0] = rest[first_rows : 2 * first_rows]
    first_ref[1] = rest[:first_rows]
    for block in range(2):
        start = 2 * first_rows + block * VECTOR_ROWS
        for i, ref in enumerate(vector_refs):
            row = rest[start + i : start + i + 1]
            ref[block : block + 1, :] = row[:, : ref.shape[1]]


def shard_pack_kernel(w_in, w_conv, w_out, lead_ref, early_ref, late_ref):
    count = lead_ref.shape[1] // w_in.shape[2]
    lead = jnp.concatenate([w_in[0], w_in[1]], axis=0)
    lead_ref[...] = lane_packed(lead, lead_ref.shape[0], count)
    width = w_conv.shape[3]
    count = early_ref.shape[1] // width
    for block, ref in ((0, early_ref), (1, late_ref)):
        rows = [w_conv[block, k] for k in range(KER)]
        rows += [w_out[block][:, :width], w_out[block][:, width:]]
        ref[...] = lane_packed(jnp.concatenate(rows, axis=0), ref.shape[0], count)


def vector_pack_kernel(wide, narrow, vector_ref):
    hidden = vector_ref.shape[1]
    for block in range(2):
        rows = []
        for ref in (wide, narrow):
            part = ref[block].astype(jnp.float32)
            rows.append(
                jnp.concatenate(
                    [part, jnp.zeros((part.shape[0], hidden - part.shape[1]), jnp.float32)], axis=1
                )
            )
        rows.append(jnp.zeros((VECTOR_ROWS - 9, hidden), jnp.float32))
        start = block * VECTOR_ROWS
        vector_ref[start : start + VECTOR_ROWS, :] = jnp.concatenate(rows, axis=0).astype(
            jnp.bfloat16
        )


def seq_join_kernel(folded_rows, vector_rows, place_ref, *refs):
    *in_refs, out_ref, hold_ref = refs
    vector_in = in_refs.pop() if vector_rows else None
    count = len(in_refs)
    for step, ref in enumerate(in_refs):
        hold_ref[(place_ref[1] - step + count) % count] = ref[...]
    shares = [lane_unpacked(hold_ref[s], count) for s in range(count)]
    rows = out_ref.shape[0] - vector_rows
    at, end = folded_rows
    if at:
        out_ref[:at, :] = jnp.concatenate([share[:at] for share in shares], axis=1)
    if end > at:
        fold = (end - at) // 2
        for half in range(2):
            columns = []
            for share in shares[half * count // 2 : (half + 1) * count // 2]:
                columns += [share[at : at + fold], share[at + fold : end]]
            start = at + half * fold
            out_ref[start : start + fold, :] = jnp.concatenate(columns, axis=1)
    if vector_in is not None:
        out_ref[rows:, :] = vector_in[...]


def place_kernel(place_ref, *refs):
    *in_refs, out_ref = refs
    chip, core = place_ref[0] // 2, place_ref[0] % 2
    cut = in_refs[0].shape[1]
    for at, share_core in ((0, core), (4, 1 - core)):
        near_a, far_a, near_b, far_b = in_refs[at : at + 4]
        for i in range(2):
            out_ref[2 * (chip ^ i) + share_core, :cut] = near_a[i]
            out_ref[2 * (chip ^ (2 + i)) + share_core, :cut] = far_a[i]
            out_ref[2 * (chip ^ (2 * i)) + share_core, cut:] = near_b[i]
            out_ref[2 * (chip ^ (2 * i + 1)) + share_core, cut:] = far_b[i]


def tiled(rows, columns):
    return pl.BlockSpec((rows, columns), lambda i: (i, 0))


def fixed(*shape):
    return pl.BlockSpec(shape, lambda i: (0,) * len(shape))


def row_block(shape):
    return pl.BlockSpec((1,) + shape[1:], lambda i: (i, 0, 0))


def pack_block(parts, rows, columns, index):
    return pl.BlockSpec((parts, rows, columns), lambda i: (0, index, 0))


def cost(flops, width):
    return pl.CostEstimate(flops=flops, bytes_accessed=width, transcendentals=0)


def call(kernel, grid, in_specs, out_specs, out_shape, flops, moved, name, aliases=None, scratch=(), room=32):
    return pl.pallas_call(
        kernel,
        grid=(grid,),
        in_specs=in_specs,
        out_specs=out_specs,
        out_shape=out_shape,
        scratch_shapes=list(scratch),
        input_output_aliases=aliases or {},
        cost_estimate=cost(flops, moved),
        compiler_params=pltpu.CompilerParams(vmem_limit_bytes=room * 1024 * 1024),
        name=name,
    )


def shape_of(shape, dtype):
    return jax.ShapeDtypeStruct(shape, dtype)


class Weights:
    def __init__(self, first, taps, last, wide, narrow):
        self.first, self.taps, self.last = first, taps, last
        self.wide, self.narrow = wide, narrow
        self.model, self.hidden = wide.shape[1], narrow.shape[1]

    def first_spec(self):
        array, index = self.first
        return pack_block(array.shape[0], self.model // array.shape[0], self.hidden, index)

    def specs(self, units):
        return [
            pack_block(array.shape[0], self.hidden // array.shape[0], self.hidden, index)
            for array, index in units
        ]


def arrays(units):
    return [array for array, _ in units]


def pack_weights(pack, wide, narrow):
    folds = wide.shape[1] // narrow.shape[1]
    units = [(pack, folds + i) for i in range(KER + folds)]
    return Weights((pack, 0), units[:KER], units[KER:], wide, narrow)


class Sizes:
    def __init__(self, pack, model, hidden):
        self.parts = pack.shape[0]
        self.model, self.hidden = model, hidden
        self.first_rows = model // self.parts
        self.middle_rows = hidden // self.parts
        self.folds = model // hidden
        self.conv_at = self.first_rows // self.middle_rows

    def first(self):
        return pack_block(self.parts, self.first_rows, self.hidden, 0)


def project(inputs, weights):
    tokens, model = inputs.shape
    hidden = weights.hidden
    tile = min(128, tokens)
    return call(
        project_kernel,
        tokens // tile,
        [tiled(tile, model), weights.first_spec(), fixed(3, model), fixed(6, hidden)],
        [tiled(tile, model), tiled(tile, hidden), tiled(tile, hidden)],
        [
            shape_of((tokens, model), jnp.bfloat16),
            shape_of((tokens, hidden), jnp.float32),
            shape_of((tokens, hidden), jnp.bfloat16),
        ],
        4 * tokens * model * hidden,
        12 * tokens * model,
        "project",
    )(inputs, weights.first[0], weights.wide, weights.narrow)


def convolve(act_two, halos, flags, inputs, weights, dilation_step, next_dtype):
    rows, length, hidden = act_two.shape
    tokens, model = inputs.shape
    low, high = halos
    return call(
        functools.partial(convolve_kernel, dilation_step),
        rows,
        [
            scalars(),
            row_block(low.shape),
            row_block(act_two.shape),
            row_block(high.shape),
            row_block(flags.shape),
            tiled(length, model),
            *weights.specs(weights.taps + weights.last),
            fixed(3, model),
            fixed(6, hidden),
        ],
        [
            tiled(length, KER * hidden),
            tiled(length, hidden),
            tiled(length, hidden),
            tiled(length, model),
        ],
        [
            shape_of((tokens, KER * hidden), jnp.bfloat16),
            shape_of((tokens, hidden), jnp.float32),
            shape_of((tokens, hidden), jnp.bfloat16),
            shape_of((tokens, model), next_dtype),
        ],
        2 * tokens * hidden * (KER * hidden + model),
        16 * tokens * model,
        "convolve",
    )(
        place(),
        low,
        act_two,
        high,
        flags,
        inputs,
        *arrays(weights.taps + weights.last),
        weights.wide,
        weights.narrow,
    )


def out_back(upstream, conv_out, weights):
    tokens, model = upstream.shape
    hidden = weights.hidden
    tile = min(128, tokens)
    return call(
        out_back_kernel,
        tokens // tile,
        [
            tiled(tile, model),
            tiled(tile, hidden),
            *weights.specs(weights.last),
            fixed(6, hidden),
        ],
        [tiled(tile, model), tiled(tile, hidden), fixed(8, hidden), fixed(8, model)],
        [
            shape_of((tokens, model), jnp.bfloat16),
            shape_of((tokens, hidden), jnp.bfloat16),
            shape_of((8, hidden), jnp.float32),
            shape_of((8, model), jnp.float32),
        ],
        4 * tokens * model * hidden,
        10 * tokens * model,
        "out_back",
    )(upstream, conv_out, *arrays(weights.last), weights.narrow)


def weight_grads(tap_rows, gv, act_three, short, pack, conv_at=None):
    tokens, hidden = gv.shape
    model = short.shape[1]
    sizes = Sizes(pack, model, hidden)
    conv_at = sizes.conv_at if conv_at is None else conv_at
    whole = pl.BlockSpec((tokens, hidden), lambda s: (0, 0))
    return call(
        weight_grad_kernel,
        KER + sizes.folds,
        [
            pl.BlockSpec((tokens, hidden), lambda s: (0, jnp.minimum(s, KER - 1))),
            whole,
            whole,
            pl.BlockSpec((tokens, hidden), lambda s: (0, jnp.maximum(s - KER, 0))),
        ],
        pl.BlockSpec(
            (sizes.parts, sizes.middle_rows, hidden), lambda s: (0, conv_at + s, 0)
        ),
        shape_of(pack.shape, jnp.bfloat16),
        2 * tokens * hidden * (KER * hidden + model),
        8 * tokens * model,
        "weight_grads",
    )(tap_rows, gv, act_three, short)


def conv_back(gv, flags, u, inputs, upstream, weights, dilation_step):
    low, high = seq_neighbours(gv, KER // 2 * dilation_step)
    return conv_back_with(low, gv, high, flags, u, inputs, upstream, weights, dilation_step)


def conv_back_with(low, gv, high, flags, u, inputs, upstream, weights, dilation_step):
    rows, length, hidden = gv.shape
    tokens, model = inputs.shape
    return call(
        functools.partial(conv_back_kernel, dilation_step),
        rows,
        [
            scalars(),
            row_block(low.shape),
            row_block(gv.shape),
            row_block(high.shape),
            row_block(flags.shape),
            tiled(length, hidden),
            tiled(length, model),
            tiled(length, model),
            *weights.specs(weights.taps),
            weights.first_spec(),
            fixed(3, model),
            fixed(6, hidden),
        ],
        [tiled(length, hidden), tiled(length, model), fixed(8, hidden), fixed(8, model)],
        [
            shape_of((tokens, hidden), jnp.bfloat16),
            shape_of((tokens, model), jnp.float32),
            shape_of((8, hidden), jnp.float32),
            shape_of((8, model), jnp.float32),
        ],
        2 * tokens * hidden * (KER * hidden + model),
        16 * tokens * model,
        "conv_back",
        room=56 if dilation_step == SECOND_DILATION else 32,
    )(
        place(),
        low,
        gv,
        high,
        flags,
        u,
        inputs,
        upstream,
        *arrays(weights.taps),
        weights.first[0],
        weights.wide,
        weights.narrow,
    )


def in_grads(grad_pack, act_one, gu):
    tokens, model = act_one.shape
    hidden = gu.shape[1]
    sizes = Sizes(grad_pack, model, hidden)
    return call(
        in_grad_kernel,
        1,
        [pl.BlockSpec(memory_space=pl.ANY), fixed(tokens, model), fixed(tokens, hidden)],
        sizes.first(),
        shape_of(grad_pack.shape, jnp.bfloat16),
        2 * tokens * hidden * model,
        4 * tokens * model,
        "in_grads",
        {0: 0},
    )(grad_pack, act_one, gu)


def scalars():
    return pl.BlockSpec(memory_space=pltpu.SMEM)


def place():
    return jnp.stack([lax.axis_index("dp"), lax.axis_index("seq")]).astype(jnp.int32)


def share_grads(where, tap_rows, gv, act_three, short):
    tokens, hidden = gv.shape
    model = short.shape[1]
    parts = lax.axis_size("dp")
    folds = model // hidden
    depth = hidden // parts
    whole = pl.BlockSpec((tokens, hidden), lambda s: (0, 0))
    share = pl.BlockSpec((parts // 2, depth, hidden), lambda s: (0, s, 0))
    shape = shape_of((parts // 2, (KER + folds) * depth, hidden), jnp.bfloat16)
    return call(
        share_grad_kernel,
        KER + folds,
        [
            scalars(),
            pl.BlockSpec((tokens, hidden), lambda s: (0, jnp.minimum(s, KER - 1))),
            whole,
            whole,
            pl.BlockSpec((tokens, hidden), lambda s: (0, jnp.maximum(s - KER, 0))),
        ],
        [share, share],
        [shape, shape],
        2 * tokens * hidden * (KER * hidden + model),
        8 * tokens * model,
        "share_grads",
        scratch=[pltpu.VMEM((parts, depth, hidden), jnp.bfloat16)],
    )(where, tap_rows, gv, act_three, short)


def share_in_grads(where, act_one, gu, sums):
    tokens, model = act_one.shape
    hidden = gu.shape[1]
    parts = lax.axis_size("dp")
    rows = model // parts + len(sums) // 4 * VECTOR_ROWS
    shape = shape_of((parts // 2, rows, hidden), jnp.bfloat16)
    return call(
        share_in_kernel,
        1,
        [scalars()] + [fixed(*array.shape) for array in (act_one, gu, *sums)],
        [fixed(*shape.shape)] * 2,
        [shape, shape],
        2 * tokens * hidden * model,
        4 * tokens * model,
        "share_in_grads",
        scratch=[pltpu.VMEM((parts, rows, hidden), jnp.bfloat16)],
    )(where, act_one, gu, *sums)


def chip_slot(shape, index):
    return pl.BlockSpec((1,) + shape[1:], lambda i: (index(i), 0, 0))


def first_sum(owns, gots):
    hidden = owns[0].shape[2]
    rows = sum(own.shape[1] for own in owns)
    cut = rows // 32 * 16
    a, b = (2, cut, hidden), (2, rows - cut, hidden)
    outs = [
        (a, lambda i: i // 2),
        (a, lambda i: i // 2),
        (b, lambda i: jnp.minimum(i, 1)),
        (b, lambda i: jnp.maximum(i - 2, 0)),
    ]
    return call(
        functools.partial(first_sum_kernel, cut, len(owns)),
        4,
        [chip_slot(array.shape, lambda i: i) for array in (*owns, *gots)],
        [chip_slot(shape, index) for shape, index in outs],
        [shape_of(shape, jnp.bfloat16) for shape, _ in outs],
        4 * rows * hidden,
        24 * rows * hidden,
        "first_sum",
    )(*owns, *gots)


def second_sum(keep_a, got_a, keep_b, got_b):
    ins = (keep_a, got_a, keep_b, got_b)
    outs = [shape_of(array.shape[1:], jnp.bfloat16) for array in ins]
    return call(
        second_sum_kernel,
        1,
        [fixed(*array.shape) for array in ins],
        [fixed(*out.shape) for out in outs],
        outs,
        2 * keep_a.size,
        12 * keep_a.size,
        "second_sum",
    )(*ins)


def seq_split(where, folded_rows, vector_rows, *ins):
    count = lax.axis_size("seq")
    rows = sum(array.shape[0] for array in ins[:: 2 if len(ins) > 1 else 1])
    hidden = ins[0].shape[1]
    shape = (count, packed_depth(rows, count), hidden)
    return call(
        functools.partial(seq_split_kernel, folded_rows, vector_rows),
        1,
        [scalars()] + [fixed(*array.shape) for array in ins],
        fixed(*shape),
        shape_of(shape, jnp.bfloat16),
        rows * hidden,
        6 * rows * hidden,
        "seq_split",
    )(where, *ins)


def seq_exchange(split):
    return [split[0]] + [shifted(split[step], step) for step in range(1, split.shape[0])]


def last_sum(pieces, out_shapes):
    flat = [array for _, piece in pieces for array in piece]
    outs = [shape_of(shape, jnp.float32) for shape in out_shapes]
    return call(
        functools.partial(last_sum_kernel, [(name, len(piece)) for name, piece in pieces]),
        1,
        [fixed(*array.shape) for array in flat],
        [fixed(*shape) for shape in out_shapes],
        outs,
        4 * flat[0].size,
        8 * flat[0].size,
        "last_sum",
    )(*flat)


def dp_swapped(block, bit):
    count = lax.axis_size("dp")
    return lax.ppermute(block, "dp", [(i, i ^ (1 << bit)) for i in range(count)])


class Chain:
    def __init__(self, token):
        self.token = token

    def hold(self, *values):
        return lax.optimization_barrier((*values, self.token))[:-1]

    def step(self, function, *values):
        out = function(*self.hold(*values))
        self.token = out[0] if isinstance(out, (list, tuple)) else out
        return out


def shifted(block, step):
    count = lax.axis_size("seq")
    return lax.ppermute(block, "seq", [(i, (i + step) % count) for i in range(count)])


def weight_pack(block_number, device_shards):
    w_in, w_conv, w_out = (device_shards[i][block_number] for i in (2, 6, 10))
    width = w_in.shape[1]
    folds = w_out.shape[1] // width
    pieces = [w_in, w_conv.reshape(-1, width)]
    pieces += [w_out[:, i * width : (i + 1) * width] for i in range(folds)]
    return jnp.concatenate(pieces, axis=0)


def vector_pack(block_number, device_shards, width):
    order = (0, 1, 11, 3, 4, 5, 7, 8, 9)
    rows = [device_shards[i][block_number] for i in order]
    rows = [jnp.pad(row, (0, width - row.shape[0])) for row in rows]
    return jnp.pad(jnp.stack(rows), ((0, VECTOR_ROWS - len(rows)), (0, 0)))


def seq_gathered(packed):
    count = lax.axis_size("seq")
    me = lax.axis_index("seq")
    held = [packed] + [shifted(packed, step) for step in range(1, count)]
    ring = jnp.stack(held[::-1] + held[::-1])
    return lax.dynamic_slice_in_dim(ring, (count - 1 - me) % count, count, axis=0)


def folded_columns(out_parts):
    count, folds, depth, width = out_parts.shape
    per_fold = count // folds
    return (
        out_parts.reshape(folds, per_fold, folds, depth, width)
        .transpose(0, 3, 1, 2, 4)
        .reshape(folds * depth, per_fold * folds * width)
    )


def unfolded_columns(out_rows, folds, count):
    per_fold = count // folds
    depth = out_rows.shape[0] // folds
    width = out_rows.shape[1] // count
    return (
        out_rows.reshape(folds, depth, per_fold, folds, width)
        .transpose(0, 2, 3, 1, 4)
        .reshape(count, folds * depth, width)
    )


def pack_is_aligned(middle_rows):
    return middle_rows % 16 == 0


def gathered_params(block_number, device_shards, after=None):
    w_in, w_conv, w_out = (device_shards[i][block_number] for i in (2, 6, 10))
    first_rows = w_in.shape[0]
    taps, middle_rows, width = w_conv.shape
    folds = w_out.shape[1] // width
    count = lax.axis_size("seq")
    hidden = width * count
    by_seq = seq_gathered(weight_pack(block_number, device_shards))
    straight = first_rows + taps * middle_rows
    total = straight + folds * middle_rows
    upper = by_seq[:, :straight].transpose(1, 0, 2).reshape(straight, hidden)
    lower = folded_columns(by_seq[:, straight:].reshape(count, folds, middle_rows, width))
    vectors = vector_pack(block_number, device_shards, hidden)
    packed = jnp.concatenate([upper, lower, vectors])
    if after is not None:
        packed, after = lax.optimization_barrier((packed, after))
    whole = lax.all_gather(packed, "dp")
    tail = whole[:, total:].astype(jnp.float32)
    wide = tail[:, :3, :first_rows].transpose(1, 0, 2).reshape(3, -1)
    narrow = tail[:, 3:9, :middle_rows].transpose(1, 0, 2).reshape(6, -1)
    if not pack_is_aligned(middle_rows):
        bounds = [0, first_rows]
        bounds += [first_rows + (k + 1) * middle_rows for k in range(taps + folds)]
        whole = jnp.concatenate(
            [whole[:, a:b].reshape(1, -1, hidden) for a, b in zip(bounds, bounds[1:])], axis=1
        )
    return pack_weights(whole, wide, narrow)


def reduce_dp(grad_pack, wide_grads, narrow_grads):
    parts = lax.axis_size("dp")
    hidden = narrow_grads.shape[1]
    model = wide_grads.shape[1]
    first_rows = model // parts
    middle_rows = hidden // parts
    folds = model // hidden
    total = first_rows + (KER + folds) * middle_rows
    if not pack_is_aligned(middle_rows):
        bounds = [0, model] + [model + (k + 1) * hidden for k in range(KER + folds)]
        grad_pack = jnp.concatenate(
            [grad_pack[0, a:b].reshape(parts, -1, hidden) for a, b in zip(bounds, bounds[1:])]
            + [jnp.zeros((parts, VECTOR_ROWS, hidden), jnp.bfloat16)],
            axis=1,
        )
    vectors = jnp.concatenate(
        [
            jnp.pad(
                block.reshape(-1, parts, rows).transpose(1, 0, 2),
                ((0, 0), (0, 0), (0, hidden - rows)),
            )
            for block, rows in ((wide_grads, first_rows), (narrow_grads, middle_rows))
        ]
        + [jnp.zeros((parts, VECTOR_ROWS - 9, hidden), jnp.float32)],
        axis=1,
    ).astype(jnp.bfloat16)
    grad_pack = lax.dynamic_update_slice(grad_pack, vectors, (0, total, 0))
    return lax.psum_scatter(grad_pack, "dp", scatter_dimension=0, tiled=False)


def reduce_seq(mine, model, hidden):
    parts = lax.axis_size("dp")
    count = lax.axis_size("seq")
    me = lax.axis_index("seq")
    first_rows = model // parts
    middle_rows = hidden // parts
    width = hidden // count
    folds = model // hidden
    straight = first_rows + KER * middle_rows
    total = straight + folds * middle_rows
    upper = mine[:straight].reshape(straight, count, width).transpose(1, 0, 2)
    lower = unfolded_columns(mine[straight:total], folds, count)
    fold = -(-first_rows // width)
    tail = mine[total:, : fold * width].reshape(1, VECTOR_ROWS * fold, width)
    tail = jnp.broadcast_to(tail, (count,) + tail.shape[1:])
    ring = jnp.concatenate([upper, lower, tail], axis=1)
    ring = jnp.concatenate([ring, ring])
    ring = lax.dynamic_slice_in_dim(ring, me, count, axis=0)
    held = [ring[0]] + [shifted(ring[step], step) for step in range(1, count)]
    held = [block.astype(jnp.float32) for block in held]
    while len(held) > 1:
        half = len(held) // 2
        held = [held[i] + held[i + half] for i in range(half)]
    summed = held[0]
    last = summed[straight:total].reshape(folds, middle_rows, width).transpose(1, 0, 2)
    tail = summed[total:].reshape(VECTOR_ROWS, fold * width)
    return (
        summed[:first_rows],
        summed[first_rows:straight].reshape(KER, middle_rows, width),
        last.reshape(middle_rows, folds * width),
        tail[:3, :first_rows],
        tail[3:9, :middle_rows],
    )


def block_forward(inputs, projected, halos, weights, flags, dilation_step, next_dtype):
    rows, length, _ = flags.shape
    act_one, u, act_two = projected
    tap_rows, conv_out, act_three, output = convolve(
        act_two.reshape(rows, length, -1), halos, flags, inputs, weights, dilation_step, next_dtype
    )
    return output, (act_one, u, tap_rows, conv_out, act_three)


def block_backward(inputs, upstream, weights, kept, flags, dilation_step, before=None):
    act_one, u, tap_rows, conv_out, act_three = kept
    rows, length, _ = flags.shape
    short, gv, narrow_a, wide_a = out_back(upstream, conv_out, weights)
    pack = weights.first[0]
    grad_shape = shape_of(
        (pack.shape[0], sum(pack_rows(pack, inputs.shape[1], gv.shape[1])), gv.shape[1]),
        jnp.bfloat16,
    )
    grad_pack = weight_grads(tap_rows, gv, act_three, short, grad_shape)
    gu, result, narrow_b, wide_b = conv_back(
        gv.reshape(rows, length, -1), flags, u, inputs, upstream, weights, dilation_step
    )
    if before is not None:
        gu, before = lax.optimization_barrier((gu, before))
    grad_pack = in_grads(grad_pack, act_one, gu)
    wide = jnp.concatenate([wide_b[0:2], wide_a[0:1]])
    narrow = jnp.concatenate([narrow_b[0:3], narrow_a[0:3]])
    return result, reduce_dp(grad_pack, wide, narrow), before


def shard_pack(w_in, w_conv, w_out):
    count = lax.axis_size("seq")
    depth, width = w_conv.shape[2:]
    ins = (w_in, w_conv, w_out)
    rest = packed_depth((KER + w_out.shape[2] // width) * depth, count)
    lead = packed_depth(2 * w_in.shape[1], count)
    outs = [shape_of((n, width * count), jnp.bfloat16) for n in (lead, rest, rest)]
    return call(
        shard_pack_kernel,
        1,
        [fixed(*array.shape) for array in ins],
        [fixed(*out.shape) for out in outs],
        outs,
        rest * width,
        8 * rest * width,
        "shard_pack",
        room=60,
    )(*ins)


def pack_vectors(wide, narrow, hidden):
    ins = (jnp.stack(wide, axis=1), jnp.stack(narrow, axis=1))
    out = (2 * VECTOR_ROWS, hidden)
    return call(
        vector_pack_kernel,
        1,
        [fixed(*array.shape) for array in ins],
        fixed(*out),
        shape_of(out, jnp.bfloat16),
        hidden,
        hidden,
        "pack_vectors",
    )(*ins)


def seq_shares(packed):
    return [packed] + [shifted(packed, step) for step in range(1, lax.axis_size("seq"))]


def seq_join(where, folded_rows, held, vectors=None):
    count = len(held)
    packed = held[0]
    extra = [] if vectors is None else [vectors]
    vector_rows = 0 if vectors is None else vectors.shape[0]
    rows = folded_rows[1] + vector_rows
    hidden = packed.shape[1]
    return call(
        functools.partial(seq_join_kernel, folded_rows, vector_rows),
        1,
        [scalars()] + [fixed(*array.shape) for array in held + extra],
        fixed(rows, hidden),
        shape_of((rows, hidden), jnp.bfloat16),
        rows * hidden,
        4 * rows * hidden,
        "seq_join",
        scratch=[pltpu.VMEM((count,) + packed.shape, jnp.bfloat16)],
    )(where, *held, *extra)


class Exchange:
    def __init__(self, block, beside):
        self.block = block
        self.cut = block.shape[0] // 32 * 16
        a, b = block[: self.cut], block[self.cut :]
        got_a, got_b, *self.beside = lax.optimization_barrier(
            (dp_swapped(a, 1), dp_swapped(b, 2), *beside)
        )
        self.near = (jnp.stack([a, got_a]), jnp.stack([b, got_b]))

    def finish(self, where, beside):
        rows, hidden = self.block.shape
        near_a, near_b = self.near
        far_a, far_b, *beside = lax.optimization_barrier(
            (dp_swapped(near_a, 2), dp_swapped(near_b, 1), *beside)
        )
        near = (near_a, far_a, near_b, far_b)
        ins = near + tuple(dp_swapped(share, 0) for share in near)
        parts = lax.axis_size("dp")
        return call(
            place_kernel,
            1,
            [scalars()] + [fixed(*array.shape) for array in ins],
            fixed(parts, rows, hidden),
            shape_of((parts, rows, hidden), jnp.bfloat16),
            parts * rows * hidden,
            4 * parts * rows * hidden,
            "place",
        )(where, *ins), beside


def after(value, *earlier):
    return lax.optimization_barrier((value, *earlier))[0]


def exchanged_weights(where, shards):
    w_in, w_conv, w_out = shards[2], shards[6], shards[10]
    first_rows = w_in.shape[1]
    depth, width = w_conv.shape[2:]
    folds = w_out.shape[2] // width
    folded = (KER * depth, (KER + folds) * depth)
    plain = (2 * first_rows, 2 * first_rows)
    lead, early, late = shard_pack(w_in, w_conv, w_out)
    wide = [shards[i] for i in (0, 1, 11)]
    narrow = [shards[i] for i in (3, 4, 5, 7, 8, 9)]
    vectors = pack_vectors(wide, narrow, width * lax.axis_size("seq"))
    lead = seq_join(where, plain, seq_shares(lead), vectors)
    exchange = Exchange(lead, seq_shares(after(early, lead)))
    early = seq_join(where, folded, exchange.beside)
    early_whole = lax.all_gather(early, "dp")
    lead, late = exchange.finish(where, seq_shares(after(late, early)))
    tail = lead[:, 2 * first_rows :].astype(jnp.float32)

    def weights(block, whole):
        start = block * VECTOR_ROWS
        wide = tail[:, start : start + 3, :first_rows].transpose(1, 0, 2).reshape(3, -1)
        narrow = tail[:, start + 3 : start + 9, :depth].transpose(1, 0, 2).reshape(6, -1)
        units = [(whole, i) for i in range(KER + folds)]
        return Weights((lead, block), units[:KER], units[KER:], wide, narrow)

    def late_weights(projected):
        rows = seq_join(where, folded, list(after(tuple(late), lead)))
        return weights(1, lax.all_gather(after(rows, early_whole, projected), "dp"))

    return weights(0, early_whole), late_weights


def exchanged_backward(inputs, weights, kept, flags, dilations, cotangent, out_shapes):
    where = place()
    parts = lax.axis_size("dp")
    hidden = weights[1].hidden
    model = inputs[0].shape[1]
    depth = hidden // parts
    folded = (KER * depth, (KER + model // hidden) * depth)
    rows, length, _ = flags[0].shape

    act_one, u, tap_rows, conv_out, act_three = kept[1]
    short, gv, *out_sums_late = out_back(cotangent, conv_out, weights[1])
    blocks = gv.reshape(rows, length, -1)
    halos = seq_neighbours(blocks, KER // 2 * dilations[1])
    pack_shape = shape_of((parts, folded[1], hidden), jnp.bfloat16)
    pack = weight_grads(tap_rows, gv, act_three, short, pack_shape, 0)
    pack, low, high = lax.optimization_barrier((pack, *halos))
    late_sum = lax.psum_scatter(pack, "dp", scatter_dimension=0, tiled=False)
    gu, middle_grad, *in_sums_late = conv_back_with(
        low, blocks, high, flags[1], u, inputs[1], cotangent, weights[1], dilations[1]
    )
    chain = Chain(gu)
    own_first, other_first = chain.step(
        lambda *values: share_in_grads(where, *values, ()), act_one, gu
    )

    act_one, u, tap_rows, conv_out, act_three = kept[0]
    short, gv, *out_sums = chain.step(
        lambda value: out_back(value, conv_out, weights[0]), middle_grad
    )
    blocks = gv.reshape(rows, length, -1)
    halos = seq_neighbours(blocks, KER // 2 * dilations[0])
    own_taps, other_taps = share_grads(where, tap_rows, gv, act_three, short)
    low, high, own_taps, other_taps, other_first = lax.optimization_barrier(
        (*halos, own_taps, other_taps, other_first)
    )
    got_taps, got_first = dp_swapped(other_taps, 0), dp_swapped(other_first, 0)
    gu, input_grad, *in_sums = chain.step(
        lambda low, high: conv_back_with(
            low, blocks, high, flags[0], u, inputs[0], middle_grad, weights[0], dilations[0]
        ),
        low,
        high,
    )

    def first_round(sums):
        keep_a, send_a, keep_b, send_b = sums
        return keep_a, dp_swapped(send_a, 1), keep_b, dp_swapped(send_b, 2)

    def second_round(sums):
        kept_a, send_a, kept_b, send_b = sums
        return kept_a, dp_swapped(send_a, 2), kept_b, dp_swapped(send_b, 1)

    all_sums = (*out_sums, *in_sums, *out_sums_late, *in_sums_late)
    own, other = chain.step(
        lambda a, b: share_in_grads(where, a, b, all_sums), act_one, gu
    )
    owns = (own_taps, own_first, own)
    gots = (got_taps, got_first, dp_swapped(other, 0))
    main = first_round(
        chain.step(lambda *values: first_sum(values[:3], values[3:]), *owns, *gots)
    )
    late = seq_exchange(chain.step(lambda value: seq_split(where, folded, 0, value), late_sum))
    main, late = lax.optimization_barrier((main, late))
    main = second_round(second_sum(*main))
    main = seq_exchange(seq_split(where, folded, 2 * VECTOR_ROWS, *main))
    return input_grad, last_sum((("early", main), ("late", late)), out_shapes)


def pack_rows(pack, model, hidden):
    parts = pack.shape[0]
    extra = VECTOR_ROWS if pack_is_aligned(hidden // lax.axis_size("dp")) else 0
    return model // parts, (KER * hidden + model) // parts, extra


def local(
    tokens,
    protein_lengths,
    norm1_gain,
    norm1_bias,
    w_in,
    in_bias,
    norm2_gain,
    norm2_bias,
    w_conv,
    conv_bias,
    norm3_gain,
    norm3_bias,
    w_out,
    out_bias,
    cotangent,
):
    device_shards = (
        norm1_gain,
        norm1_bias,
        w_in,
        in_bias,
        norm2_gain,
        norm2_bias,
        w_conv,
        conv_bias,
        norm3_gain,
        norm3_bias,
        w_out,
        out_bias,
    )
    rows, seq_len, model = tokens.shape
    token_positions = lax.axis_index("seq") * seq_len + jnp.arange(seq_len, dtype=jnp.int32)
    early_flags = kernel_tap_flags(protein_lengths, token_positions, FIRST_DILATION)
    later_flags = kernel_tap_flags(protein_lengths, token_positions, SECOND_DILATION)
    parts = lax.axis_size("dp")
    fast = parts == 8 and pack_is_aligned(in_bias.shape[1])
    if fast:
        early_weights, late_weights = exchanged_weights(place(), device_shards)
    else:
        early_weights = gathered_params(0, device_shards)
        late_weights = gathered_params(1, device_shards, early_weights.first[0])
    flat_tokens = tokens.reshape(rows * seq_len, model)
    projected = project(flat_tokens, early_weights)
    halos = seq_neighbours(projected[2].reshape(rows, seq_len, -1), KER // 2 * FIRST_DILATION)
    if fast:
        late_weights = late_weights(halos)
    middle, early_kept = block_forward(
        flat_tokens, projected, halos, early_weights, early_flags, FIRST_DILATION, jnp.float32
    )
    projected = project(middle, late_weights)
    halos = seq_neighbours(projected[2].reshape(rows, seq_len, -1), KER // 2 * SECOND_DILATION)
    output, late_kept = block_forward(
        middle, projected, halos, late_weights, later_flags, SECOND_DILATION, jnp.bfloat16
    )
    hidden = early_weights.hidden
    if fast:
        shapes = [w.shape for w in (w_in, w_conv, w_out, norm1_gain, norm1_bias, out_bias)]
        shapes += [w.shape for w in (in_bias, norm2_gain, norm2_bias)]
        shapes += [w.shape for w in (conv_bias, norm3_gain, norm3_bias)]
        input_grad, grads = exchanged_backward(
            (flat_tokens, middle),
            (early_weights, late_weights),
            (early_kept, late_kept),
            (early_flags, later_flags),
            (FIRST_DILATION, SECOND_DILATION),
            cotangent.reshape(rows * seq_len, model),
            shapes,
        )
        order = (3, 4, 0, 6, 7, 8, 1, 9, 10, 11, 2, 5)
        return (
            output.reshape(tokens.shape),
            input_grad.reshape(tokens.shape),
            *(grads[i] for i in order),
        )
    middle_grad, mine_late, _ = block_backward(
        middle,
        cotangent.reshape(rows * seq_len, model),
        late_weights,
        late_kept,
        later_flags,
        SECOND_DILATION,
    )
    input_grad, mine_early, mine_late = block_backward(
        flat_tokens,
        middle_grad,
        early_weights,
        early_kept,
        early_flags,
        FIRST_DILATION,
        mine_late,
    )
    reduced_late = reduce_seq(mine_late, model, hidden)
    reduced_early = reduce_seq(mine_early, model, hidden)
    first_early, middle_early, last_early, wide_early, narrow_early = reduced_early
    first_late, middle_late, last_late, wide_late, narrow_late = reduced_late
    return (
        output.reshape(tokens.shape),
        input_grad.reshape(tokens.shape),
        jnp.stack([wide_early[0], wide_late[0]]),
        jnp.stack([wide_early[1], wide_late[1]]),
        jnp.stack([first_early, first_late]),
        jnp.stack([narrow_early[0], narrow_late[0]]),
        jnp.stack([narrow_early[1], narrow_late[1]]),
        jnp.stack([narrow_early[2], narrow_late[2]]),
        jnp.stack([middle_early, middle_late]),
        jnp.stack([narrow_early[3], narrow_late[3]]),
        jnp.stack([narrow_early[4], narrow_late[4]]),
        jnp.stack([narrow_early[5], narrow_late[5]]),
        jnp.stack([last_early, last_late]),
        jnp.stack([wide_early[2], wide_late[2]]),
    )


def solution(mesh):
    placed = (
        P("dp", "seq", None),
        P("dp", None),
        P(None, "dp"),
        P(None, "dp"),
        P(None, "dp", "seq"),
        P(None, "dp"),
        P(None, "dp"),
        P(None, "dp"),
        P(None, None, "dp", "seq"),
        P(None, "dp"),
        P(None, "dp"),
        P(None, "dp"),
        P(None, "dp", "seq"),
        P(None, "dp"),
        P("dp", "seq", None),
    )
    return jax.shard_map(
        local,
        mesh=mesh,
        in_specs=placed,
        out_specs=(
            P("dp", "seq", None),
            P("dp", "seq", None),
            P(None, "dp"),
            P(None, "dp"),
            P(None, "dp", "seq"),
            P(None, "dp"),
            P(None, "dp"),
            P(None, "dp"),
            P(None, None, "dp", "seq"),
            P(None, "dp"),
            P(None, "dp"),
            P(None, "dp"),
            P(None, "dp", "seq"),
            P(None, "dp"),
        ),
        check_vma=False,
    )
```
